32 devices in a mesh: section: 2 (over core), dp: 16 (over z, y, x).
Axes of the slice: x: 2, y: 2, z: 4, core: 2. Of those that a mesh axis runs over, the one named last changes fastest.
Arguments:
- latent: bfloat16 [32768, 256], P('dp'), may hold values from -6 to 6
- codes: int32 [2, 5, 32768], P(None, None, 'dp'), may hold values from 0 to 31, as said below
- targets: int32 [2, 5, 32768], P(None, None, 'dp'), may hold values from 0 to 600
- valid: int32 [5, 32768], P(None, 'dp'), may hold values from 0 to 1
- code_table: float32 [2, 32, 256], P('section'), may hold values from -6 to 6
- code_table_mom: float32 [2, 32, 256], P('section'), may hold values from -1.25 to 1.25
- code_table_avg: float32 [2, 32, 256], P('section'), may hold values from -6 to 6
- in_weight: float32 [2, 256, 256], P('section'), may hold values from -0.375 to 0.375
- in_weight_mom: float32 [2, 256, 256], P('section'), may hold values from -1.25 to 1.25
- in_weight_avg: float32 [2, 256, 256], P('section'), may hold values from -0.375 to 0.375
- gains: float32 [2, 2, 256], P('section'), may hold values from 0.5 to 1.5
- gains_mom: float32 [2, 2, 256], P('section'), may hold values from -8 to 8
- gains_avg: float32 [2, 2, 256], P('section'), may hold values from 0.5 to 1.5
- up_weight: float32 [2, 256, 256], P('section'), may hold values from -0.375 to 0.375
- up_weight_mom: float32 [2, 256, 256], P('section'), may hold values from -1.25 to 1.25
- up_weight_avg: float32 [2, 256, 256], P('section'), may hold values from -0.375 to 0.375
- down_weight: float32 [2, 256, 256], P('section'), may hold values from -0.375 to 0.375
- down_weight_mom: float32 [2, 256, 256], P('section'), may hold values from -1.25 to 1.25
- down_weight_avg: float32 [2, 256, 256], P('section'), may hold values from -0.375 to 0.375
- head_weight: float32 [2, 256, 601], P('section'), may hold values from -0.75 to 0.75
- head_weight_mom: float32 [2, 256, 601], P('section'), may hold values from -1.25 to 1.25
- head_weight_avg: float32 [2, 256, 601], P('section'), may hold values from -0.75 to 0.75
Outputs:
- ends: float32 [2, 32768, 256], P('section', 'dp')
- table_momentum: float32 [2, 32, 256], P('section')
- table_average: float32 [2, 32, 256], P('section')
- table_master: float32 [2, 32, 256], P('section')
- table_copy: bfloat16 [2, 32, 256], P('section')
- input_momentum: float32 [2, 256, 256], P('section')
- input_average: float32 [2, 256, 256], P('section')
- input_master: float32 [2, 256, 256], P('section')
- input_copy: bfloat16 [2, 256, 256], P('section')
- gain_momentum: float32 [2, 2, 256], P('section')
- gain_average: float32 [2, 2, 256], P('section')
- gain_master: float32 [2, 2, 256], P('section')
- gain_copy: bfloat16 [2, 2, 256], P('section')
- upper_momentum: float32 [2, 256, 256], P('section')
- upper_average: float32 [2, 256, 256], P('section')
- upper_master: float32 [2, 256, 256], P('section')
- upper_copy: bfloat16 [2, 256, 256], P('section')
- lower_momentum: float32 [2, 256, 256], P('section')
- lower_average: float32 [2, 256, 256], P('section')
- lower_master: float32 [2, 256, 256], P('section')
- lower_copy: bfloat16 [2, 256, 256], P('section')
- heads_momentum: float32 [2, 256, 601], P('section')
- heads_average: float32 [2, 256, 601], P('section')
- heads_master: float32 [2, 256, 601], P('section')
- heads_copy: bfloat16 [2, 256, 601], P('section')
The draws below stay inside these ranges and needn't reach their ends.
Inputs may be any that keep to these rules, and one draw needn't show every extreme that they name: codes[0] holds actions below 4, codes[1] chance codes below 32.
All inputs are finite; a program needn't handle non-finite values.
Results may differ from the reference program's by a relative error of at most 0.012.
Values may be sent and summed in bfloat16 or wider, within the bound.
No kernel may reach another device: no remote copies, remote signals or barrier semaphores. Data moves between devices by JAX's collectives and lax.ppermute only.
A program may use at most 64 MiB of HBM per device.

```python
import math
import jax
import jax.numpy as jnp
from jax import lax

H = 256
BINS = 601
CODES = 32
ACTIONS = 4
K = 5
BATCH = 32768


def draw_codes(key, part):
    key = jax.random.fold_in(key, 11)
    first_key, second_key = jax.random.split(key)
    actions = jax.random.randint(first_key, (K, BATCH), 0, ACTIONS)
    chance = jax.random.randint(second_key, (K, BATCH), 0, CODES)
    actions = actions.at[0, 0].set(ACTIONS - 1)
    chance = chance.at[0, 0].set(CODES - 1)
    return jnp.stack([actions, chance]).astype(jnp.int32)


def draw_valid(key, part):
    key = jax.random.fold_in(key, 23)
    rolls = jax.random.randint(key, (K, BATCH), 0, 1000)
    positions = jnp.arange(BATCH, dtype=jnp.int32)
    limits = 250 + 500 * positions // BATCH
    return (rolls < limits[None, :]).astype(jnp.int32)


def draw_gains_mom(key, part):
    key = jax.random.fold_in(key, 37)
    sign_key, level_key = jax.random.split(key)
    flips = jax.random.bernoulli(sign_key, 0.5, (2, 2, H))
    sign_part = jnp.where(flips, 1.0, -1.0).astype(jnp.float32)
    levels = jax.random.uniform(level_key, (2, 2, H), jnp.float32, math.log(2.0), math.log(8.0))
    magnitude = jnp.exp(levels)
    return (sign_part * magnitude).astype(jnp.float32)


def place_ends(result, own_key, smallest, high):
    longest = result.shape.index(max(result.shape))
    spots = []
    for shift in (0, 1):
        where = [jax.random.randint(jax.random.fold_in(own_key, axis), (), 0, length) for axis, length in enumerate(result.shape)]
        where[longest] = (where[longest] + shift) % result.shape[longest]
        spots.append(tuple(where))
    return result.at[spots[0]].set(smallest).at[spots[1]].set(high)


def shard_levels(own_key, dims, shards, smallest, largest):
    level = 1.0
    for axis_at, shards_of in shards:
        draws = jax.random.uniform(jax.random.fold_in(jax.random.fold_in(own_key, 6), axis_at), (shards_of,), jnp.float32, smallest / len(shards), largest / len(shards))
        level = level * jnp.repeat(jnp.exp(draws), dims[axis_at] // shards_of).reshape((-1,) + (1,) * (len(dims) - 1 - axis_at))
    return level


def scatter_about(own_key, shape, scale, bound, shards=(), kind=jnp.bfloat16):
    entries = scale * jax.random.normal(own_key, shape, jnp.float32)
    if shards:
        entries = entries * shard_levels(own_key, shape, shards, -0.22, 0.18)
    return jnp.clip(entries, -bound, bound).astype(kind)


def setup_inputs(seed: int = 0) -> dict:
    streams_of = jax.random.split(jax.random.key(seed), 23)
    return {
        "latent": scatter_about(streams_of[0], (BATCH, H), 1.0, 6.0, ((0, 16),)),
        "codes": draw_codes(jax.random.fold_in(streams_of[22], 71), 0),
        "targets": place_ends(jax.random.randint(streams_of[2], (2, K, BATCH), 0, BINS), jax.random.fold_in(streams_of[2], 1), 0, BINS - 1).astype(jnp.int32),
        "valid": draw_valid(jax.random.fold_in(streams_of[22], 71), 0),
        "code_table": scatter_about(streams_of[4], (2, CODES, H), 1.0, 6.0, ((0, 2),), jnp.float32),
        "code_table_mom": scatter_about(streams_of[5], (2, CODES, H), 0.2, 1.25, ((0, 2),), jnp.float32),
        "code_table_avg": scatter_about(streams_of[6], (2, CODES, H), 1.0, 6.0, ((0, 2),), jnp.float32),
        "in_weight": scatter_about(streams_of[7], (2, H, H), H ** -0.5, 0.375, ((0, 2),), jnp.float32),
        "in_weight_mom": scatter_about(streams_of[8], (2, H, H), 0.2, 1.25, ((0, 2),), jnp.float32),
        "in_weight_avg": scatter_about(streams_of[9], (2, H, H), H ** -0.5, 0.375, ((0, 2),), jnp.float32),
        "gains": jnp.clip(1.0 + 0.1 * jax.random.normal(streams_of[10], (2, 2, H), jnp.float32), 0.5, 1.5),
        "gains_mom": draw_gains_mom(jax.random.fold_in(streams_of[22], 71), 0),
        "gains_avg": jnp.clip(1.0 + 0.1 * jax.random.normal(streams_of[12], (2, 2, H), jnp.float32), 0.5, 1.5),
        "up_weight": scatter_about(streams_of[13], (2, H, H), H ** -0.5, 0.375, ((0, 2),), jnp.float32),
        "up_weight_mom": scatter_about(streams_of[14], (2, H, H), 0.2, 1.25, ((0, 2),), jnp.float32),
        "up_weight_avg": scatter_about(streams_of[15], (2, H, H), H ** -0.5, 0.375, ((0, 2),), jnp.float32),
        "down_weight": scatter_about(streams_of[16], (2, H, H), H ** -0.5, 0.375, ((0, 2),), jnp.float32),
        "down_weight_mom": scatter_about(streams_of[17], (2, H, H), 0.2, 1.25, ((0, 2),), jnp.float32),
        "down_weight_avg": scatter_about(streams_of[18], (2, H, H), H ** -0.5, 0.375, ((0, 2),), jnp.float32),
        "head_weight": scatter_about(streams_of[19], (2, H, BINS), (H // 4) ** -0.5, 0.75, ((0, 2),), jnp.float32),
        "head_weight_mom": scatter_about(streams_of[20], (2, H, BINS), 0.2, 1.25, ((0, 2),), jnp.float32),
        "head_weight_avg": scatter_about(streams_of[21], (2, H, BINS), (H // 4) ** -0.5, 0.75, ((0, 2),), jnp.float32),
    }


EPS = 1e-05
MOMENTUM = 0.5
AVERAGE = 0.9
RATE = 0.2
GRAD_SCALE = 4.0

@jax.custom_vjp
def low(v):
    return lax.optimization_barrier(v.astype(jnp.bfloat16)).astype(jnp.float32)

@jax.custom_vjp
def low_back(v):
    return v

def low_keep(v):
    return (low(v), None)

def low_pass(kept, grad):
    return (grad,)

def back_keep(v):
    return (v, None)

def back_low(kept, grad):
    return (low(grad),)
low.defvjp(low_keep, low_pass)
low_back.defvjp(back_keep, back_low)

def matmul(left, right):
    return jnp.dot(left, right, precision=lax.Precision.HIGHEST, preferred_element_type=jnp.float32)

def layer_norm(value, gain):
    centered = value - lax.optimization_barrier(jnp.mean(value, axis=-1, keepdims=True))
    scale = lax.rsqrt(lax.optimization_barrier(jnp.mean(centered * centered, axis=-1, keepdims=True)) + EPS)
    return centered * scale * gain

def norm_gelu(value, gain):
    return jax.nn.gelu(layer_norm(value, gain))

def tower(inputs, code_ids, table, in_low, gain_pair, up_low, down_low, head_low, goal_ids, weight):
    inputs = low_back(inputs)
    picker = (code_ids[:, None] == jnp.arange(table.shape[0])[None, :]).astype(jnp.float32)
    pre_norm = low_back(matmul(inputs, in_low) + matmul(picker, table))
    hidden = norm_gelu(pre_norm, gain_pair[0])
    normed = low(layer_norm(hidden, gain_pair[1]))
    inner = low_back(matmul(normed, up_low))
    active = low(jax.nn.gelu(inner))
    state = hidden + low_back(matmul(active, down_low))
    sent = low(state)
    logits = low_back(matmul(sent, head_low))
    chosen = (goal_ids[:, None] == jnp.arange(logits.shape[1])[None, :]).astype(jnp.float32)
    picked = lax.optimization_barrier(jnp.sum(logits * chosen, axis=1))
    loss = jnp.sum(weight * (jax.nn.logsumexp(logits, axis=1) - picked))
    return (state, sent, loss)

def update(weight, moment, average, grad, count):
    step_grad = GRAD_SCALE * grad * lax.rsqrt(count)
    new_moment = MOMENTUM * moment + step_grad
    new_weight = weight - RATE * (step_grad + MOMENTUM * new_moment)
    new_average = AVERAGE * average + (1.0 - AVERAGE) * new_weight
    return (new_moment, new_average, new_weight, new_weight.astype(jnp.bfloat16))

def reference(latent, codes, targets, valid, code_table, code_table_mom, code_table_avg, in_weight, in_weight_mom, in_weight_avg, gains, gains_mom, gains_avg, up_weight, up_weight_mom, up_weight_avg, down_weight, down_weight_mom, down_weight_avg, head_weight, head_weight_mom, head_weight_avg):
    batch = latent.shape[0]
    width = latent.shape[1]
    unroll = codes.shape[1]
    block = min(4096, batch)
    blocks = batch // block
    start_blocks = latent.astype(jnp.float32).reshape(blocks, block, width)
    code_blocks = jnp.moveaxis(codes.reshape(2, unroll, blocks, block), 2, 0)
    goal_blocks = jnp.moveaxis(targets.reshape(2, unroll, blocks, block), 2, 0)
    valid_blocks = jnp.moveaxis(valid.reshape(unroll, blocks, block), 1, 0).astype(jnp.float32)
    params = (code_table, in_weight, gains, up_weight, down_weight, head_weight)

    def whole(param_set, starts):
        table, win, gain_set, wup, wdown, whead = param_set
        table_low = low(table)
        in_low = low(win)
        up_low = low(wup)
        down_low = low(wdown)
        head_low = low(whead)

        def one_block(pieces):
            begin, code_part, goal_part, valid_part = pieces
            inputs = begin
            total = jnp.zeros((), jnp.float32)
            state = begin
            for step in range(unroll):
                state, sent, first_loss = tower(inputs, code_part[0, step], table_low[0], in_low[0], gain_set[0], up_low[0], down_low[0], head_low[0], goal_part[0, step], valid_part[step])
                state, sent, second_loss = tower(sent, code_part[1, step], table_low[1], in_low[1], gain_set[1], up_low[1], down_low[1], head_low[1], goal_part[1, step], valid_part[step])
                total = total + first_loss + second_loss
                inputs = sent
            return (total, state)
        losses, finals = lax.map(jax.checkpoint(one_block), (starts, code_blocks, goal_blocks, valid_blocks))
        return (jnp.sum(losses), finals.reshape(batch, width))
    (loss, final), pull = jax.vjp(whole, params, start_blocks)
    param_grads, start_grad = pull((jnp.ones_like(loss), jnp.zeros_like(final)))
    ends = jnp.stack([start_grad.reshape(batch, width), final])
    count = jnp.sum(valid).astype(jnp.float32)
    table_m, table_a, table_w, table_c = update(code_table, code_table_mom, code_table_avg, param_grads[0], count)
    input_m, input_a, input_w, input_c = update(in_weight, in_weight_mom, in_weight_avg, param_grads[1], count)
    gain_m, gain_a, gain_w, gain_c = update(gains, gains_mom, gains_avg, param_grads[2], count)
    upper_m, upper_a, upper_w, upper_c = update(up_weight, up_weight_mom, up_weight_avg, param_grads[3], count)
    lower_m, lower_a, lower_w, lower_c = update(down_weight, down_weight_mom, down_weight_avg, param_grads[4], count)
    heads_m, heads_a, heads_w, heads_c = update(head_weight, head_weight_mom, head_weight_avg, param_grads[5], count)
    return (ends, table_m, table_a, table_w, table_c, input_m, input_a, input_w, input_c, gain_m, gain_a, gain_w, gain_c, upper_m, upper_a, upper_w, upper_c, lower_m, lower_a, lower_w, lower_c, heads_m, heads_a, heads_w, heads_c)
```

```python
import functools

import jax
import jax.numpy as jnp
from jax import lax
from jax.experimental import pallas as pl
from jax.experimental.pallas import tpu as pltpu
from jax.sharding import PartitionSpec as P

EPS = 1e-05
MOMENTUM = 0.5
AVERAGE = 0.9
RATE = 0.2
GRAD_SCALE = 4.0
GELU_LINE = 0.7978845608028654
GELU_CUBE = 0.7978845608028654 * 0.044715

BF16 = jnp.bfloat16
F32 = jnp.float32
LANES = 128
TILE = 16
BITS = 24
VMEM = 60 * 1024 * 1024


def dot(left, right):
    return jnp.dot(left, right, preferred_element_type=F32)


def dot_right_t(left, right):
    return lax.dot_general(left, right, (((1,), (1,)), ((), ())), preferred_element_type=F32)


def dot_left_t(left, right):
    return lax.dot_general(left, right, (((0,), (0,)), ((), ())), preferred_element_type=F32)


def gelu_and_slope(value):
    square = value * value
    half = 0.5 + 0.5 * jnp.tanh(value * (GELU_LINE + GELU_CUBE * square))
    result = value * half
    return result, half + result * (1.0 - half) * (2 * GELU_LINE + (6 * GELU_CUBE) * square)


def normalise(value):
    part = 1.0 / value.shape[-1]
    centered = value - jnp.sum(value, axis=-1, keepdims=True) * part
    scale = lax.rsqrt(jnp.sum(centered * centered, axis=-1, keepdims=True) * part + EPS)
    return centered * scale, scale


def normalise_back(out_grad, product, gain, unit, scale):
    part = 1.0 / unit.shape[-1]
    scaled = out_grad * gain
    first = jnp.sum(scaled, axis=-1, keepdims=True) * part
    second = jnp.sum(product * gain, axis=-1, keepdims=True) * part
    return (scaled - first - unit * second) * scale


class Layout:
    def __init__(self, codes, width, bins):
        self.codes, self.width, self.bins = codes, width, bins
        self.wide = -(-bins // LANES) * LANES
        spots, at = {}, 0
        for name in ("in", "up", "down"):
            spots[name] = (at, at + width)
            at += width
        self.full_heads = self.wide // width
        self.rest = self.wide - self.full_heads * width
        for part in range(self.full_heads):
            spots["head", part] = (at, at + width)
            at += width
        self.folds = 0 if self.rest == 0 else width // self.rest
        if self.rest:
            rows = width // self.folds
            spots["head_rest"] = (at, at + rows)
            at += rows
        codes_up = -(-codes // TILE) * TILE
        spots["table"] = (at, at + codes)
        at += codes_up
        spots["tail"] = (at, at + TILE)
        at += TILE
        self.spots = spots
        self.rows = -(-at // 64) * 64
        self.used = at

    def store_head(self, ref, head):
        width = self.width
        for part in range(self.full_heads):
            low, high = self.spots["head", part]
            ref[low:high, :] = head[:, part * width : (part + 1) * width].astype(ref.dtype)
        if self.rest:
            low, high = self.spots["head_rest"]
            tall = width // self.folds
            rest = head[:, self.full_heads * width :]
            for fold in range(self.folds):
                ref[low:high, fold * self.rest : (fold + 1) * self.rest] = rest[
                    fold * tall : (fold + 1) * tall, :
                ].astype(ref.dtype)

    def load_head(self, ref):
        parts = [ref[low:high, :] for low, high in (self.spots["head", p] for p in range(self.full_heads))]
        if self.rest:
            low, high = self.spots["head_rest"]
            parts.append(
                jnp.concatenate(
                    [ref[low:high, f * self.rest : (f + 1) * self.rest] for f in range(self.folds)],
                    axis=0,
                )
            )
        return jnp.concatenate(parts, axis=1)


def split_three(value):
    high = value.astype(BF16)
    left = value - high.astype(F32)
    middle = left.astype(BF16)
    low = (left - middle.astype(F32)).astype(BF16)
    return high, middle, low


def pack_kernel(lay, table, w_in, w_up, w_down, w_head, gains, out):
    for name, ref in (("in", w_in), ("up", w_up), ("down", w_down), ("table", table)):
        low, high = lay.spots[name]
        out[low:high, :] = ref[0].astype(BF16)
    head = w_head[0]
    head = jnp.concatenate([head, jnp.zeros((lay.width, lay.wide - lay.bins), F32)], axis=1)
    lay.store_head(out, head)
    low, high = lay.spots["tail"]
    pieces = [piece.astype(F32) for piece in split_three(gains[0])]
    pieces.append(jnp.zeros((high - low - 6, lay.width), F32))
    out[low:high, :] = jnp.concatenate(pieces, axis=0).astype(BF16)
    out[high:, :] = jnp.zeros((lay.rows - high, lay.width), BF16)


def towers_kernel(lay, steps, count_rows, which, latent, codes, targets, valid, whole_valid, mine, theirs,
                  keep, send, ends_mine, ends_send,
                  w_in, w_up, w_down, w_head, table, gains,
                  g_in, g_up, g_down, g_head, g_table, g_gain,
                  meta, sent_all, unit_one, slope_one, unit_two, slope_two, active_all,
                  scale_one, scale_two, back, final):
    rows, width = latent.shape
    code_count = lay.codes
    section = which[0]

    @pl.when(pl.program_id(0) == 0)
    def start():
        for ref in (g_in, g_up, g_down, g_head, g_table, g_gain):
            ref[...] = jnp.zeros_like(ref)
        for packed, slot in ((mine, section), (theirs, 1 - section)):
            for name, ref in (("in", w_in), ("up", w_up), ("down", w_down), ("table", table)):
                low, high = lay.spots[name]
                ref[slot] = packed[low:high, :]
            w_head[slot] = lay.load_head(packed)
            low, high = lay.spots["tail"]
            tail = packed[low:high, :].astype(F32)
            gains[slot] = tail[0:2] + tail[2:4] + tail[4:6]

    for step in range(steps):
        line = jnp.concatenate(
            [codes[0, step : step + 1, :], codes[1, step : step + 1, :], targets[0, step : step + 1, :],
             targets[1, step : step + 1, :], valid[step : step + 1, :], jnp.zeros((3, rows), jnp.int32)], axis=0)
        meta[step] = line.T
    sent_all[0] = latent[...]

    def pick_of(step, tower):
        code = meta[step, :, tower : tower + 1]
        return (code == lax.broadcasted_iota(jnp.int32, (rows, code_count), 1)).astype(F32).astype(BF16)

    def forward(step, tower):
        at = 2 * step + tower
        pre = dot(sent_all[at], w_in[tower]) + dot(pick_of(step, tower), table[tower])
        unit, scale = normalise(pre)
        unit_one[at] = unit
        scale_one[at] = scale
        hidden, slope = gelu_and_slope(unit * gains[tower, 0:1, :])
        slope_one[at] = slope
        unit, scale = normalise(hidden)
        unit_two[at] = unit
        scale_two[at] = scale
        normed = (unit * gains[tower, 1:2, :]).astype(BF16)
        active, slope = gelu_and_slope(dot(normed, w_up[tower]))
        slope_two[at] = slope
        active = active.astype(BF16)
        active_all[at] = active
        state = hidden + dot(active, w_down[tower])
        sent_all[at + 1] = state.astype(BF16)
        final[...] = state

    def forward_step(step, carry):
        forward(step, 0)
        forward(step, 1)
        return carry

    lax.fori_loop(0, steps, forward_step, 0)
    back[...] = jnp.zeros_like(back)

    def backward(step, tower):
        at = 2 * step + tower
        sent = sent_all[at + 1]
        logits = dot(sent, w_head[tower])
        column = lax.broadcasted_iota(jnp.int32, (rows, lay.wide), 1)
        goal = meta[step, :, 2 + tower : 3 + tower]
        weight = meta[step, :, 4:5].astype(F32)
        logits = jnp.where(column < lay.bins, logits, -1e30)
        raised = jnp.exp(logits - jnp.max(logits, axis=-1, keepdims=True))
        ratio = weight / jnp.sum(raised, axis=-1, keepdims=True)
        logit_grad = (raised * ratio - jnp.where(column == goal, weight, 0.0)).astype(BF16)
        g_head[tower] += dot_left_t(sent, logit_grad)
        state_grad = dot_right_t(logit_grad, w_head[tower]) + back[...].astype(F32)
        branch_grad = state_grad.astype(BF16)
        g_down[tower] += dot_left_t(active_all[at], branch_grad)
        inner_grad = (dot_right_t(branch_grad, w_down[tower]) * slope_two[at]).astype(BF16)
        unit = unit_two[at]
        gain = gains[tower, 1:2, :]
        g_up[tower] += dot_left_t((unit * gain).astype(BF16), inner_grad)
        out_grad = dot_right_t(inner_grad, w_up[tower])
        product = out_grad * unit
        block_gain_grad = jnp.sum(product, axis=0, keepdims=True)
        hidden_grad = state_grad + normalise_back(out_grad, product, gain, unit, scale_two[at])
        out_grad = hidden_grad * slope_one[at]
        unit = unit_one[at]
        product = out_grad * unit
        in_gain_grad = jnp.sum(product, axis=0, keepdims=True)
        g_gain[tower] += jnp.concatenate([in_gain_grad, block_gain_grad], axis=0)
        pre_grad = normalise_back(out_grad, product, gains[tower, 0:1, :], unit, scale_one[at]).astype(BF16)
        g_table[tower] += dot_left_t(pick_of(step, tower), pre_grad)
        g_in[tower] += dot_left_t(sent_all[at], pre_grad)
        back[...] = dot_right_t(pre_grad, w_in[tower]).astype(BF16)

    def backward_step(turn, carry):
        step = steps - 1 - turn
        backward(step, 1)
        backward(step, 0)
        return carry

    lax.fori_loop(0, steps, backward_step, 0)
    first = back[...].astype(F32)
    last = final[...]
    is_first = section == 0
    ends_mine[...] = jnp.where(is_first, first, last)
    ends_send[...] = jnp.where(is_first, last, first).astype(BF16)

    @pl.when(pl.program_id(0) == pl.num_programs(0) - 1)
    def finish():
        count = jnp.sum(whole_valid[...].astype(F32), axis=(0, 1), keepdims=True).astype(jnp.int32)
        lane = lax.broadcasted_iota(jnp.int32, (1, width), 1)
        bits = jnp.where(lane < BITS, (count >> jnp.minimum(lane, BITS)) & 1, 0).astype(F32)
        for packed, slot in ((keep, section), (send, 1 - section)):
            kind = packed.dtype
            for name, ref in (("in", g_in), ("up", g_up), ("down", g_down), ("table", g_table)):
                low, high = lay.spots[name]
                packed[low:high, :] = ref[slot].astype(kind)
            lay.store_head(packed, g_head[slot])
            low, high = lay.spots["tail"]
            own = bits if packed is keep else jnp.zeros_like(bits)
            tail = jnp.concatenate([g_gain[slot], own, jnp.zeros((high - low - 3, width), F32)], axis=0)
            packed[low:high, :] = tail.astype(kind)
            packed[high:, :] = jnp.zeros((lay.rows - high, width), kind)


def update_kernel(lay, total, *refs):
    ins, outs = refs[:18], refs[18:]
    low, high = lay.spots["tail"]
    tail = total[low:high, :].astype(F32)
    lane = lax.broadcasted_iota(jnp.int32, (1, lay.width), 1)
    place = jnp.where(lane < BITS, (1 << jnp.minimum(lane, BITS)).astype(F32), 0.0)
    count = jnp.sum(tail[2:3] * place, axis=-1, keepdims=True)
    factor = GRAD_SCALE * lax.rsqrt(count)
    head = lay.load_head(total)[:, : lay.bins].astype(F32)
    grads = [None] * 6
    for at, name in ((0, "table"), (1, "in"), (3, "up"), (4, "down")):
        low, high = lay.spots[name]
        grads[at] = total[low:high, :].astype(F32)
    grads[2] = tail[0:2]
    grads[5] = head
    for at, grad in enumerate(grads):
        weight, moment, average = ins[3 * at : 3 * at + 3]
        step_grad = grad * factor
        new_moment = MOMENTUM * moment[0] + step_grad
        new_weight = weight[0] - RATE * (step_grad + MOMENTUM * new_moment)
        out_moment, out_average, out_weight, out_copy = outs[4 * at : 4 * at + 4]
        out_moment[0] = new_moment
        out_average[0] = AVERAGE * average[0] + (1.0 - AVERAGE) * new_weight
        out_weight[0] = new_weight
        out_copy[0] = new_weight.astype(BF16)


def swap(value):
    return lax.ppermute(value, "section", [(0, 1), (1, 0)])


def reduce_all(value, length):
    levels = [1 << bit for bit in range(length.bit_length() - 1)]
    index = lax.axis_index("dp")

    def across(array, mask):
        return lax.ppermute(array, "dp", [(i, i ^ mask) for i in range(length)])

    halving, whole = levels[:2], levels[2:]
    current = value
    for mask in halving:
        half = current.shape[0] // 2
        upper = (index // mask) % 2 == 1
        low, high = current[:half], current[half:]
        sent = jnp.where(upper, low, high)
        kept = jnp.where(upper, high, low)
        current = (kept.astype(F32) + across(sent, mask).astype(F32)).astype(BF16)
    for mask in whole:
        current = (current.astype(F32) + across(current, mask).astype(F32)).astype(BF16)
    for mask in reversed(halving):
        upper = (index // mask) % 2 == 1
        other = across(current, mask)
        current = jnp.where(upper, jnp.concatenate([other, current]), jnp.concatenate([current, other]))
    return current


def on_device(block, length, latent, codes, targets, valid, *weights):
    section = lax.axis_index("section").astype(jnp.int32)
    rows, width = latent.shape
    steps = codes.shape[1]
    own_rows = rows // 2
    block = min(block, own_rows)
    blocks = own_rows // block
    table, w_in, gains, w_up, w_down, w_head = weights[0::3]
    lay = Layout(table.shape[1], width, w_head.shape[2])
    packed_shape = (lay.rows, width)
    roomy = pltpu.CompilerParams(vmem_limit_bytes=VMEM)
    mine = pl.pallas_call(
        functools.partial(pack_kernel, lay),
        out_shape=jax.ShapeDtypeStruct(packed_shape, BF16),
        compiler_params=roomy,
        name="pack",
    )(table, w_in, w_up, w_down, w_head, gains)
    theirs = swap(mine)

    def spec_rows(*shape):
        return pl.BlockSpec(shape, lambda i, which: (which[0] * blocks + i,) + (0,) * (len(shape) - 1))

    def spec_lanes(*shape):
        return pl.BlockSpec(shape, lambda i, which: (0,) * (len(shape) - 1) + (which[0] * blocks + i,))

    def spec_whole(*shape):
        return pl.BlockSpec(shape, lambda i, which: (0,) * len(shape))

    def spec_out(*shape):
        return pl.BlockSpec(shape, lambda i, which: (i, 0))

    ticks = 2 * steps
    square = (2, width, width)
    keep, send, ends_mine, ends_send = pl.pallas_call(
        functools.partial(towers_kernel, lay, steps, rows),
        grid_spec=pltpu.PrefetchScalarGridSpec(
            num_scalar_prefetch=1,
            grid=(blocks,),
            in_specs=[
                spec_rows(block, width),
                spec_lanes(2, steps, block),
                spec_lanes(2, steps, block),
                spec_lanes(steps, block),
                spec_whole(steps, rows),
                spec_whole(*packed_shape),
                spec_whole(*packed_shape),
            ],
            out_specs=[
                spec_whole(*packed_shape),
                spec_whole(*packed_shape),
                spec_out(block, width),
                spec_out(block, width),
            ],
            scratch_shapes=[
                pltpu.VMEM(square, BF16),
                pltpu.VMEM(square, BF16),
                pltpu.VMEM(square, BF16),
                pltpu.VMEM((2, width, lay.wide), BF16),
                pltpu.VMEM((2, lay.codes, width), BF16),
                pltpu.VMEM((2, 2, width), F32),
                pltpu.VMEM(square, F32),
                pltpu.VMEM(square, F32),
                pltpu.VMEM(square, F32),
                pltpu.VMEM((2, width, lay.wide), F32),
                pltpu.VMEM((2, lay.codes, width), F32),
                pltpu.VMEM((2, 2, width), F32),
                pltpu.VMEM((steps, block, 8), jnp.int32),
                pltpu.VMEM((ticks + 1, block, width), BF16),
                pltpu.VMEM((ticks, block, width), F32),
                pltpu.VMEM((ticks, block, width), F32),
                pltpu.VMEM((ticks, block, width), F32),
                pltpu.VMEM((ticks, block, width), F32),
                pltpu.VMEM((ticks, block, width), BF16),
                pltpu.VMEM((ticks, block, 1), F32),
                pltpu.VMEM((ticks, block, 1), F32),
                pltpu.VMEM((block, width), BF16),
                pltpu.VMEM((block, width), F32),
            ],
        ),
        out_shape=[
            jax.ShapeDtypeStruct(packed_shape, F32),
            jax.ShapeDtypeStruct(packed_shape, BF16),
            jax.ShapeDtypeStruct((own_rows, width), F32),
            jax.ShapeDtypeStruct((own_rows, width), BF16),
        ],
        compiler_params=roomy,
        name="towers",
    )(section[None], latent, codes, targets, valid, valid, mine, theirs)

    total = reduce_all((keep + swap(send).astype(F32)).astype(BF16), length)
    other = swap(ends_send).astype(F32)
    ends = jnp.where(
        section == 0,
        jnp.concatenate([ends_mine, other]),
        jnp.concatenate([other, ends_mine]),
    )[None]
    news = [
        jax.ShapeDtypeStruct(weights[3 * at].shape, kind)
        for at in range(6)
        for kind in (F32, F32, F32, BF16)
    ]
    updated = pl.pallas_call(
        functools.partial(update_kernel, lay),
        out_shape=news,
        compiler_params=roomy,
        name="update",
    )(total, *weights)
    table_out, in_out, gain_out, up_out, down_out, head_out = (updated[4 * at : 4 * at + 4] for at in range(6))
    return (ends, *table_out, *in_out, *gain_out, *up_out, *down_out, *head_out)


def solution(mesh):
    by_section = P("section", None, None)
    in_specs = (P("dp", None), P(None, None, "dp"), P(None, None, "dp"), P(None, "dp")) + (by_section,) * 18
    out_specs = (P("section", "dp", None),) + (by_section,) * 24
    return jax.shard_map(
        functools.partial(on_device, 512, mesh.shape["dp"]),
        mesh=mesh,
        in_specs=in_specs,
        out_specs=out_specs,
        check_vma=False,
    )
```

```python
import functools

import jax
import jax.numpy as jnp
from jax import lax
from jax.experimental import pallas as pl
from jax.experimental.pallas import tpu as pltpu
from jax.sharding import PartitionSpec as P

EPS = 1e-05
MOMENTUM = 0.5
AVERAGE = 0.9
RATE = 0.2
GRAD_SCALE = 4.0
GELU_LINE = 0.7978845608028654
GELU_CUBE = 0.7978845608028654 * 0.044715

BF16 = jnp.bfloat16
F32 = jnp.float32
LANES = 128
TILE = 16
BITS = 24
VMEM = 60 * 1024 * 1024


def dot(left, right):
    return jnp.dot(left, right, preferred_element_type=F32)


def dot_right_t(left, right):
    return lax.dot_general(left, right, (((1,), (1,)), ((), ())), preferred_element_type=F32)


def dot_left_t(left, right):
    return lax.dot_general(left, right, (((0,), (0,)), ((), ())), preferred_element_type=F32)


def gelu_and_slope(value):
    square = value * value
    half = 0.5 + 0.5 * jnp.tanh(value * (GELU_LINE + GELU_CUBE * square))
    result = value * half
    return result, half + result * (1.0 - half) * (2 * GELU_LINE + (6 * GELU_CUBE) * square)


def normalise(value):
    part = 1.0 / value.shape[-1]
    centered = value - jnp.sum(value, axis=-1, keepdims=True) * part
    scale = lax.rsqrt(jnp.sum(centered * centered, axis=-1, keepdims=True) * part + EPS)
    return centered * scale, scale


class Layout:
    def __init__(self, codes, width, bins):
        self.codes, self.width, self.bins = codes, width, bins
        self.wide = -(-bins // LANES) * LANES
        spots, at = {}, 0
        for name, rows in (("in", width), ("up", width), ("down", width), ("head", bins), ("table", codes), ("tail", TILE)):
            spots[name] = (at, at + rows)
            at += -(-rows // TILE) * TILE
        self.spots = spots
        self.used = at
        self.rows = -(-at // (4 * TILE)) * (4 * TILE)


def split_three(value):
    high = value.astype(BF16)
    left = value - high.astype(F32)
    middle = left.astype(BF16)
    low = (left - middle.astype(F32)).astype(BF16)
    return high, middle, low


def pack_kernel(lay, table, w_in, w_up, w_down, w_head, gains, out):
    for name, ref in (("in", w_in), ("up", w_up), ("down", w_down), ("table", table)):
        low, high = lay.spots[name]
        out[low:high, :] = ref[0].astype(BF16)
    low, high = lay.spots["head"]
    above = lay.spots["table"][0]
    head = jnp.concatenate([w_head[:, 0, :], jnp.zeros((above - high, lay.width), F32)], axis=0)
    out[low:above, :] = head.astype(BF16)
    low, high = lay.spots["tail"]
    pieces = [piece.astype(F32) for piece in split_three(gains[0])]
    pieces.append(jnp.zeros((high - low - 6, lay.width), F32))
    out[low:high, :] = jnp.concatenate(pieces, axis=0).astype(BF16)
    if lay.rows > lay.used:
        out[lay.used :, :] = jnp.zeros((lay.rows - lay.used, lay.width), BF16)


def row_sum(value):
    return jnp.sum(value, axis=-1, keepdims=True)


def interleave(streams, matmul_delay=220, vector_delay=60):
    clock = {"M": 0.0, "V": 0.0}
    live = []
    for rank, stream in enumerate(streams):
        live.append([stream, rank, next(stream), 0.0])
    while live:
        best = min(live, key=lambda entry: (max(clock[entry[2][0]], entry[3]), entry[1]))
        unit, cost = best[2]
        begin = max(clock[unit], best[3])
        clock[unit] = begin + cost
        best[3] = begin + cost + (matmul_delay if unit == "M" else vector_delay)
        best[2] = next(best[0], None)
        if best[2] is None:
            live.remove(best)


def in_turn(*streams):
    for stream in streams:
        yield from stream


def towers_kernel(lay, steps, chunk, which, latent, codes, targets, valid, whole_valid, mine, theirs,
                  keep, send, ends_mine, ends_send,
                  w_cat, w_up, w_down, w_head, gains,
                  g_cat, g_up, g_down, g_head, g_gain,
                  meta, inputs, unit_one, slope_one, unit_two, slope_two, active, normed,
                  scale_one, scale_two, head_part, logit_grads, branch_grads, inner_grads, pre_grads,
                  back, final):
    rows, width = latent.shape
    wide = lay.wide
    part = 1.0 / width
    section = which[0]
    chunks = [slice(at, at + chunk) for at in range(0, rows, chunk)]
    weight_of = chunk / 8

    @pl.when(pl.program_id(0) == 0)
    def start():
        for ref in (g_cat, g_up, g_down, g_head, g_gain):
            ref[...] = jnp.zeros_like(ref)
        for packed, slot in ((mine, section), (theirs, 1 - section)):
            for name, ref in (("up", w_up), ("down", w_down)):
                low, high = lay.spots[name]
                ref[slot] = packed[low:high, :]
            low, high = lay.spots["in"]
            w_cat[slot, :width] = packed[low:high, :]
            low, high = lay.spots["table"]
            w_cat[slot, width : width + lay.codes] = packed[low:high, :]
            w_cat[slot, width + lay.codes :] = jnp.zeros((LANES - lay.codes, width), BF16)
            low = lay.spots["head"][0]
            high = lay.spots["table"][0]
            w_head[slot, : high - low] = packed[low:high, :]
            w_head[slot, high - low :] = jnp.zeros((wide - high + low, width), BF16)
            low, high = lay.spots["tail"]
            tail = packed[low:high, :].astype(F32)
            gains[slot] = tail[0:2] + tail[2:4] + tail[4:6]

    lane = lax.broadcasted_iota(jnp.int32, (rows, LANES), 1)
    for step in range(steps):
        alive = valid[step : step + 1, :]
        line = [codes[step, tower : tower + 1, :] for tower in range(2)]
        line += [jnp.where(alive > 0, targets[step, tower : tower + 1, :], -1) for tower in range(2)]
        columns = jnp.concatenate(line + [jnp.zeros((4, rows), jnp.int32)], axis=0).T
        meta[step] = columns
        for tower in range(2):
            inputs[2 * step + tower, :, width:] = (columns[:, tower : tower + 1] == lane).astype(F32).astype(BF16)
    inputs[0, :, :width] = latent[...]

    def forward(step, tower):
        at = 2 * step + tower
        yield "M", rows / 2
        pre = dot(inputs[at], w_cat[tower])
        for where in chunks:
            yield "V", 8 * weight_of
            unit, scale = normalise(pre[where])
            unit_one[at, where, :] = unit
            scale_one[at, where, :] = jnp.broadcast_to(scale, (chunk, LANES))
            hidden, slope = gelu_and_slope(unit * gains[tower, 0:1, :])
            slope_one[at, where, :] = slope
            head_part[at, where, :] = hidden
            unit, scale = normalise(hidden)
            unit_two[at, where, :] = unit
            scale_two[at, where, :] = jnp.broadcast_to(scale, (chunk, LANES))
            normed[at, where, :] = (unit * gains[tower, 1:2, :]).astype(BF16)
        yield "M", rows / 4
        inner = dot(normed[at], w_up[tower])
        for where in chunks:
            yield "V", 4 * weight_of
            result, slope = gelu_and_slope(inner[where])
            slope_two[at, where, :] = slope
            active[at, where, :] = result.astype(BF16)
        yield "M", rows / 4
        branch = dot(active[at], w_down[tower])
        for where in chunks:
            yield "V", weight_of
            state = head_part[at, where, :] + branch[where]
            inputs[at + 1, where, :width] = state.astype(BF16)
            final[where, :] = state

    column = lax.broadcasted_iota(jnp.int32, (1, wide), 1)
    whole_lanes = wide - LANES
    inside = lax.broadcasted_iota(jnp.int32, (1, LANES), 1) < lay.bins - whole_lanes

    def head(step, tower):
        at = 2 * step + tower
        yield "M", 5 * rows / 8
        logits = dot_right_t(inputs[at + 1, :, :width], w_head[tower])
        for where in chunks:
            yield "V", 6 * weight_of
            some = logits[where]
            some = jnp.concatenate(
                [some[:, :whole_lanes], jnp.where(inside, some[:, whole_lanes:], -1e30)], axis=1
            )
            goal = meta[step, where, 2 + tower : 3 + tower]
            raised = jnp.exp(some - jnp.max(some, axis=-1, keepdims=True))
            ratio = jnp.where(goal >= 0, 1.0, 0.0) / row_sum(raised)
            logit_grads[tower, where, :] = (raised * ratio - jnp.where(column == goal, 1.0, 0.0)).astype(BF16)
        yield "M", 5 * rows / 8
        pulled = dot(logit_grads[tower], w_head[tower])
        for where in chunks:
            yield "V", weight_of
            head_part[at, where, :] = pulled[where]
        for low in range(0, wide, width):
            high = min(low + width, wide)
            yield "M", rows / 4 + 20
            some = dot_left_t(inputs[at + 1, :, :width], logit_grads[tower, :, low:high])
            yield "V", 32
            g_head[tower, :, low:high] += some

    def forward_step(step, carry):
        interleave([
            in_turn(forward(step, 0), forward(step, 1)),
            in_turn(head(step - 1, 0), head(step - 1, 1)),
        ])
        return carry

    interleave([in_turn(forward(0, 0), forward(0, 1))])
    lax.fori_loop(1, steps, forward_step, 0)
    interleave([head(steps - 1, 0), head(steps - 1, 1)])

    def both(value):
        return jnp.concatenate([value] * (width // LANES), axis=1)

    def backward(step, tower):
        at = 2 * step + tower
        for where in chunks:
            yield "V", 1.5 * weight_of
            state_grad = head_part[at, where, :] + back[where, :].astype(F32)
            head_part[at, where, :] = state_grad
            branch_grads[tower, where, :] = state_grad.astype(BF16)
        yield "M", rows / 4
        active_grad = dot_right_t(branch_grads[tower], w_down[tower])
        for where in chunks:
            yield "V", 1.5 * weight_of
            inner_grads[tower, where, :] = (active_grad[where] * slope_two[at, where, :]).astype(BF16)
        yield "M", rows / 4
        normed_grad = dot_right_t(inner_grads[tower], w_up[tower])
        for where in chunks:
            yield "V", 6 * weight_of
            unit = unit_two[at, where, :]
            scaled = normed_grad[where] * gains[tower, 1:2, :]
            first = row_sum(scaled) * part
            second = row_sum(scaled * unit) * part
            hidden_grad = head_part[at, where, :] + (scaled - first - unit * second) * both(scale_two[at, where, :])
            out_grad = hidden_grad * slope_one[at, where, :]
            unit = unit_one[at, where, :]
            product = out_grad * unit
            g_gain[tower] += jnp.sum(product.reshape(chunk // 8, 8, width), axis=0)
            gain = gains[tower, 0:1, :]
            scaled = out_grad * gain
            first = row_sum(scaled) * part
            second = row_sum(product * gain) * part
            pre_grads[tower, where, :] = (
                (scaled - first - unit * second) * both(scale_one[at, where, :])
            ).astype(BF16)
        yield "M", rows / 4
        input_grad = dot_right_t(pre_grads[tower], w_cat[tower, :width])
        for where in chunks:
            yield "V", 0.5 * weight_of
            back[where, :] = input_grad[where].astype(BF16)

    def weight_grads(step, tower):
        at = 2 * step + tower
        for left, right, total in (
            (active, branch_grads, g_down),
            (normed, inner_grads, g_up),
            (inputs, pre_grads, g_cat),
        ):
            size = left.shape[2] // LANES
            yield "M", size * (rows + 80) / 8
            some = dot_left_t(left[at], right[tower])
            yield "V", 16 * size
            total[tower] += some

    back[...] = jnp.zeros_like(back)
    for ref in (branch_grads, inner_grads, pre_grads):
        ref[0] = jnp.zeros((rows, width), BF16)

    def backward_step(turn, carry):
        step = steps - 1 - turn
        later = jnp.minimum(step + 1, steps - 1)
        interleave([backward(step, 1), weight_grads(later, 0)])
        interleave([backward(step, 0), weight_grads(step, 1)])
        return carry

    lax.fori_loop(0, steps, backward_step, 0)
    interleave([weight_grads(0, 0)])
    first = back[...].astype(F32)
    last = final[...]
    is_first = section == 0
    ends_mine[...] = jnp.where(is_first, first, last)
    ends_send[...] = jnp.where(is_first, last, first).astype(BF16)

    @pl.when(pl.program_id(0) == pl.num_programs(0) - 1)
    def finish():
        count = jnp.sum(whole_valid[...].astype(F32), axis=(0, 1), keepdims=True).astype(jnp.int32)
        spot = lax.broadcasted_iota(jnp.int32, (1, width), 1)
        bits = jnp.where(spot < BITS, (count >> jnp.minimum(spot, BITS)) & 1, 0).astype(F32)
        for packed, slot in ((keep, section), (send, 1 - section)):
            kind = packed.dtype
            for name, value in (
                ("in", g_cat[slot, :width]),
                ("up", g_up[slot]),
                ("down", g_down[slot]),
                ("table", g_cat[slot, width : width + lay.codes]),
            ):
                low, high = lay.spots[name]
                packed[low:high, :] = value.astype(kind)
            low = lay.spots["head"][0]
            high = lay.spots["table"][0]
            packed[low:high, :] = g_head[slot].T[: high - low].astype(kind)
            in_gain = jnp.sum(g_gain[slot], axis=0, keepdims=True)
            pulled = jnp.sum((w_up[slot].astype(F32) * g_up[slot]).T, axis=0, keepdims=True)
            block_gain = pulled / gains[slot, 1:2, :]
            low, high = lay.spots["tail"]
            own = bits if packed is keep else jnp.zeros_like(bits)
            tail = jnp.concatenate([in_gain, block_gain, own, jnp.zeros((high - low - 3, width), F32)], axis=0)
            packed[low:high, :] = tail.astype(kind)
            if lay.rows > lay.used:
                packed[lay.used :, :] = jnp.zeros((lay.rows - lay.used, width), kind)


def combine_kernel(parts, which, keep, received, *outs):
    rows = outs[0].shape[0]
    for turn, out in enumerate(outs):
        low = pl.multiple_of((which[0] ^ turn) * rows, TILE)
        value = keep[pl.ds(low, rows), :] + received[pl.ds(low, rows), :].astype(F32)
        out[...] = value.astype(out.dtype)


def update_kernel(lay, parts, which, *refs):
    pieces, ins, outs, total = refs[:parts], refs[parts : parts + 18], refs[parts + 18 : parts + 42], refs[-1]
    rows = pieces[0].shape[0]
    for turn, piece in enumerate(pieces):
        low = pl.multiple_of((which[0] ^ turn) * rows, TILE)
        total[pl.ds(low, rows), :] = piece[...]
    low, high = lay.spots["tail"]
    tail = total[low:high, :].astype(F32)
    lane = lax.broadcasted_iota(jnp.int32, (1, lay.width), 1)
    place = jnp.where(lane < BITS, (1 << jnp.minimum(lane, BITS)).astype(F32), 0.0)
    count = jnp.sum(tail[2:3] * place, axis=-1, keepdims=True)
    factor = GRAD_SCALE * lax.rsqrt(count)
    for at, name in enumerate(("table", "in", "gain", "up", "down", "head")):
        if name == "gain":
            grad = tail[0:2]
        else:
            low, high = lay.spots[name]
            grad = total[low:high, :].astype(F32)
        spot = (slice(None), 0) if name == "head" else (0,)
        weight, moment, average = ins[3 * at : 3 * at + 3]
        step_grad = grad * factor
        new_moment = MOMENTUM * moment[spot] + step_grad
        new_weight = weight[spot] - RATE * (step_grad + MOMENTUM * new_moment)
        out_moment, out_average, out_weight, out_copy = outs[4 * at : 4 * at + 4]
        out_moment[spot] = new_moment
        out_average[spot] = AVERAGE * average[spot] + (1.0 - AVERAGE) * new_weight
        out_weight[spot] = new_weight
        out_copy[0] = new_weight.astype(BF16)


def swap(value):
    return lax.ppermute(value, "section", [(0, 1), (1, 0)])


def across(array, mask, length):
    return lax.ppermute(array, "dp", [(i, i ^ mask) for i in range(length)])


def on_device(block, chunk, length, latent, codes, targets, valid, *weights):
    section = lax.axis_index("section").astype(jnp.int32)
    index = lax.axis_index("dp").astype(jnp.int32)
    rows, width = latent.shape
    steps = codes.shape[1]
    own_rows = rows // 2
    block = min(block, own_rows)
    blocks = own_rows // block
    bins = weights[15].shape[2]
    weights = weights[:15] + tuple(jnp.transpose(array, (2, 0, 1)) for array in weights[15:])
    codes, targets = jnp.swapaxes(codes, 0, 1), jnp.swapaxes(targets, 0, 1)
    table, w_in, gains, w_up, w_down, w_head = weights[0::3]
    lay = Layout(table.shape[1], width, bins)
    packed_shape = (lay.rows, width)
    roomy = pltpu.CompilerParams(vmem_limit_bytes=VMEM)
    mine = pl.pallas_call(
        functools.partial(pack_kernel, lay),
        out_shape=jax.ShapeDtypeStruct(packed_shape, BF16),
        compiler_params=roomy,
        name="pack",
    )(table, w_in, w_up, w_down, w_head, gains)
    theirs = swap(mine)

    def spec_rows(*shape):
        return pl.BlockSpec(shape, lambda i, which: (which[0] * blocks + i,) + (0,) * (len(shape) - 1))

    def spec_lanes(*shape):
        return pl.BlockSpec(shape, lambda i, which: (0,) * (len(shape) - 1) + (which[0] * blocks + i,))

    def spec_whole(*shape):
        return pl.BlockSpec(shape, lambda i, which: (0,) * len(shape))

    def spec_out(*shape):
        return pl.BlockSpec(shape, lambda i, which: (i, 0))

    ticks = 2 * steps
    square = (2, width, width)
    per_tick = (ticks, block, width)
    narrow = (ticks, block, LANES)
    pair = (2, block, width)
    keep, send, ends_mine, ends_send = pl.pallas_call(
        functools.partial(towers_kernel, lay, steps, chunk),
        grid_spec=pltpu.PrefetchScalarGridSpec(
            num_scalar_prefetch=1,
            grid=(blocks,),
            in_specs=[
                spec_rows(block, width),
                spec_lanes(steps, 2, block),
                spec_lanes(steps, 2, block),
                spec_lanes(steps, block),
                spec_whole(steps, rows),
                spec_whole(*packed_shape),
                spec_whole(*packed_shape),
            ],
            out_specs=[
                spec_whole(*packed_shape),
                spec_whole(*packed_shape),
                spec_out(block, width),
                spec_out(block, width),
            ],
            scratch_shapes=[
                pltpu.VMEM((2, width + LANES, width), BF16),
                pltpu.VMEM(square, BF16),
                pltpu.VMEM(square, BF16),
                pltpu.VMEM((2, lay.wide, width), BF16),
                pltpu.VMEM((2, 2, width), F32),
                pltpu.VMEM((2, width + LANES, width), F32),
                pltpu.VMEM(square, F32),
                pltpu.VMEM(square, F32),
                pltpu.VMEM((2, width, lay.wide), F32),
                pltpu.VMEM((2, 8, width), F32),
                pltpu.VMEM((steps, block, 8), jnp.int32),
                pltpu.VMEM((ticks + 1, block, width + LANES), BF16),
                pltpu.VMEM(per_tick, F32),
                pltpu.VMEM(per_tick, F32),
                pltpu.VMEM(per_tick, F32),
                pltpu.VMEM(per_tick, F32),
                pltpu.VMEM(per_tick, BF16),
                pltpu.VMEM(per_tick, BF16),
                pltpu.VMEM(narrow, F32),
                pltpu.VMEM(narrow, F32),
                pltpu.VMEM(per_tick, F32),
                pltpu.VMEM((2, block, lay.wide), BF16),
                pltpu.VMEM(pair, BF16),
                pltpu.VMEM(pair, BF16),
                pltpu.VMEM(pair, BF16),
                pltpu.VMEM((block, width), BF16),
                pltpu.VMEM((block, width), F32),
            ],
        ),
        out_shape=[
            jax.ShapeDtypeStruct(packed_shape, F32),
            jax.ShapeDtypeStruct(packed_shape, BF16),
            jax.ShapeDtypeStruct((own_rows, width), F32),
            jax.ShapeDtypeStruct((own_rows, width), BF16),
        ],
        compiler_params=roomy,
        name="towers",
    )(section[None], latent, codes, targets, valid, valid, mine, theirs)

    parts = min(4, length)
    place = (index % parts)[None]
    in_smem = pl.BlockSpec(memory_space=pltpu.SMEM)
    in_vmem = pl.BlockSpec(memory_space=pltpu.VMEM)
    part_shape = (lay.rows // parts, width)
    own, *others = pl.pallas_call(
        functools.partial(combine_kernel, parts),
        in_specs=[in_smem, in_vmem, in_vmem],
        out_shape=[jax.ShapeDtypeStruct(part_shape, F32)]
        + [jax.ShapeDtypeStruct(part_shape, BF16)] * (parts - 1),
        compiler_params=roomy,
        name="combine",
    )(place, keep, swap(send))
    current = own
    for arrived in [across(other, mask, length) for mask, other in enumerate(others, 1)]:
        current = current + arrived.astype(F32)
    current = current.astype(BF16)
    mask = parts
    while mask < length:
        current = (current.astype(F32) + across(current, mask, length).astype(F32)).astype(BF16)
        mask *= 2
    pieces = [current] + [across(current, mask, length) for mask in range(1, parts)]

    other = swap(ends_send).astype(F32)
    ends = jnp.where(
        section == 0,
        jnp.concatenate([ends_mine, other]),
        jnp.concatenate([other, ends_mine]),
    )[None]
    news = []
    for at in range(6):
        shape = weights[3 * at].shape
        news += [jax.ShapeDtypeStruct(shape, F32)] * 3
        news.append(jax.ShapeDtypeStruct((1, shape[0], width) if at == 5 else shape, BF16))
    updated = pl.pallas_call(
        functools.partial(update_kernel, lay, parts),
        in_specs=[in_smem] + [in_vmem] * (parts + 18),
        out_shape=news,
        scratch_shapes=[pltpu.VMEM(packed_shape, BF16)],
        compiler_params=roomy,
        name="update",
    )(place, *pieces, *weights)
    table_out, in_out, gain_out, up_out, down_out, head_out = (updated[4 * at : 4 * at + 4] for at in range(6))
    head_out = [jnp.transpose(array, (1, 2, 0)) for array in head_out[:3]] + [jnp.swapaxes(head_out[3], 1, 2)]
    return (ends, *table_out, *in_out, *gain_out, *up_out, *down_out, *head_out)


def solution(mesh):
    by_section = P("section", None, None)
    in_specs = (P("dp", None), P(None, None, "dp"), P(None, None, "dp"), P(None, "dp")) + (by_section,) * 18
    out_specs = (P("section", "dp", None),) + (by_section,) * 24
    return jax.shard_map(
        functools.partial(on_device, 512, 64, mesh.shape["dp"]),
        mesh=mesh,
        in_specs=in_specs,
        out_specs=out_specs,
        check_vma=False,
    )
```

```python
import functools

import jax
import jax.numpy as jnp
from jax import lax
from jax.experimental import pallas as pl
from jax.experimental.pallas import tpu as pltpu
from jax.sharding import PartitionSpec as P

EPS = 1e-05
MOMENTUM = 0.5
AVERAGE = 0.9
RATE = 0.2
GRAD_SCALE = 4.0
GELU_LINE = 0.7978845608028654
GELU_CUBE = 0.7978845608028654 * 0.044715

BF16 = jnp.bfloat16
F32 = jnp.float32
LANES = 128
TILE = 16
BITS = 24
FIRST, SECOND = 4, 4
SPARE = 7
STEPS = 4
VMEM = 63 * 1024 * 1024


def dot(left, right):
    return jnp.dot(left, right, preferred_element_type=F32)


def dot_right_t(left, right):
    return lax.dot_general(left, right, (((1,), (1,)), ((), ())), preferred_element_type=F32)


def dot_left_t(left, right):
    return lax.dot_general(left, right, (((0,), (0,)), ((), ())), preferred_element_type=F32)


def gelu_and_slope(value):
    square = value * value
    half = 0.5 + 0.5 * jnp.tanh(value * (GELU_LINE + GELU_CUBE * square))
    result = value * half
    return result, half + result * (1.0 - half) * (2 * GELU_LINE + (6 * GELU_CUBE) * square)


def normalise(value):
    part = 1.0 / value.shape[-1]
    centered = value - jnp.sum(value, axis=-1, keepdims=True) * part
    scale = lax.rsqrt(jnp.sum(centered * centered, axis=-1, keepdims=True) * part + EPS)
    return centered * scale, scale


class Layout:
    def __init__(self, codes, width, bins):
        self.codes, self.width, self.bins = codes, width, bins
        self.wide = -(-bins // LANES) * LANES
        spots, at = {}, 0
        sizes = (("in", width), ("up", width), ("down", width), ("head", bins + SPARE), ("table", codes))
        for name, rows in sizes:
            spots[name] = (at, at + -(-rows // TILE) * TILE)
            at = spots[name][1]
        spots["table"] = (spots["table"][0], spots["table"][0] + codes)
        self.tail = spots["head"][0] + bins
        self.spots = spots
        self.used = at
        self.rows = -(-at // (8 * TILE)) * (8 * TILE)

    def with_tail(self, head, *extra):
        low, high = self.spots["head"]
        left = high - low - self.bins - sum(rows.shape[0] for rows in extra)
        return jnp.concatenate([head[: self.bins], *extra, jnp.zeros((left, self.width), F32)], axis=0)


def split_three(value):
    high = value.astype(BF16)
    left = value - high.astype(F32)
    middle = left.astype(BF16)
    low = (left - middle.astype(F32)).astype(BF16)
    return high, middle, low


def pack_kernel(lay, table, w_in, w_up, w_down, w_head, gains, out):
    for name, ref in (("in", w_in), ("up", w_up), ("down", w_down), ("table", table)):
        low, high = lay.spots[name]
        out[low:high, :] = ref[0].astype(BF16)
    low, high = lay.spots["head"]
    pieces = [piece.astype(F32) for piece in split_three(gains[0])]
    out[low:high, :] = lay.with_tail(w_head[:, 0, :], *pieces).astype(BF16)
    if lay.rows > lay.used:
        out[lay.used :, :] = jnp.zeros((lay.rows - lay.used, lay.width), BF16)


def row_sum(value):
    return jnp.sum(value, axis=-1, keepdims=True)


def interleave(streams, matmul_delay=220, vector_delay=60):
    clock = {"M": 0.0, "V": 0.0}
    live = []
    for rank, stream in enumerate(streams):
        live.append([stream, rank, next(stream), 0.0])
    while live:
        best = min(live, key=lambda entry: (max(clock[entry[2][0]], entry[3]), entry[1]))
        unit, cost = best[2]
        begin = max(clock[unit], best[3])
        clock[unit] = begin + cost
        best[3] = begin + cost + (matmul_delay if unit == "M" else vector_delay)
        best[2] = next(best[0], None)
        if best[2] is None:
            live.remove(best)


def in_turn(*streams):
    for stream in streams:
        yield from stream


def towers_kernel(lay, steps, chunk, which, latent, codes, targets, valid, whole_valid, mine, theirs,
                  keep, send, ends_mine, ends_send,
                  w_cat, w_up, w_down, w_head, gains,
                  g_cat, g_up, g_down, g_head, g_gain,
                  meta, picks, low_state, unit_one, slope_one, unit_two, slope_two, active_now, normed_now, active, normed,
                  scale_one, scale_two, head_part, turned, turned_pick, logits_all, logit_grads, pre_grads, back):
    branch_grads = tuple(low_state.at[slot, : latent.shape[0]] for slot in range(2))
    inner_grads = (active_now, normed_now)
    rows, width = latent.shape
    wide = lay.wide
    part = 1.0 / width
    section = which[0]
    chunks = [slice(at, at + chunk) for at in range(0, rows, chunk)]
    weight_of = chunk / 8

    @pl.when(pl.program_id(0) == 0)
    def start():
        for ref in (g_cat, g_up, g_down, g_head, g_gain):
            ref[...] = jnp.zeros_like(ref)
        for packed, slot in ((mine, section), (theirs, 1 - section)):
            for name, ref in (("up", w_up), ("down", w_down)):
                low, high = lay.spots[name]
                ref[slot] = packed[low:high, :]
            low, high = lay.spots["in"]
            w_cat[slot, :width] = packed[low:high, :]
            low, high = lay.spots["table"]
            w_cat[slot, width : width + lay.codes] = packed[low:high, :]
            w_cat[slot, width + lay.codes :] = jnp.zeros((LANES - lay.codes, width), BF16)
            low, high = lay.spots["head"]
            w_head[slot] = jnp.zeros((wide, width), BF16)
            w_head[slot, : high - low] = packed[low:high, :]
            start_tail = (lay.tail - low) // TILE * TILE
            block = packed[low + start_tail : high, :].astype(F32)
            at = lay.tail - low - start_tail
            gains[slot] = block[at : at + 2] + block[at + 2 : at + 4] + block[at + 4 : at + 6]
            row = lax.broadcasted_iota(jnp.int32, block.shape, 0)
            w_head[slot, start_tail : high - low] = jnp.where(row < at, block, 0.0).astype(BF16)

    lane = lax.broadcasted_iota(jnp.int32, (rows, LANES), 1)
    upright = lax.broadcasted_iota(jnp.int32, (lay.codes, rows), 0)
    for step in range(steps):
        alive = valid[step : step + 1, :]
        line = [codes[step, tower : tower + 1, :] for tower in range(2)]
        line += [jnp.where(alive > 0, targets[step, tower : tower + 1, :], -1) for tower in range(2)]
        columns = jnp.concatenate(line + [jnp.zeros((4, rows), jnp.int32)], axis=0).T
        meta[step] = columns
        for tower in range(2):
            turned_pick[2 * step + tower] = (line[tower] == upright).astype(F32).astype(BF16)
            picks[2 * step + tower] = (columns[:, tower : tower + 1] == lane).astype(F32).astype(BF16)
    low_state[0, :rows] = latent[...]
    turned[0] = latent[...].T

    def forward(step, tower):
        at = 2 * step + tower
        yield "m1"
        pre = dot(jnp.concatenate([low_state[tower, :rows], picks[at]], axis=1), w_cat[tower])
        for where in chunks:
            yield "v1"
            unit, scale = normalise(pre[where])
            unit_one[at, where, :] = unit
            scale_one[at, where, :] = jnp.broadcast_to(scale, (chunk, LANES))
            hidden, slope = gelu_and_slope(unit * gains[tower, 0:1, :])
            slope_one[at, where, :] = slope
            head_part[at, where, :] = hidden
            unit, scale = normalise(hidden)
            unit_two[at, where, :] = unit
            scale_two[at, where, :] = jnp.broadcast_to(scale, (chunk, LANES))
            normed_now[where, :] = (unit * gains[tower, 1:2, :]).astype(BF16)
        yield "m2"
        inner = dot(normed_now[...], w_up[tower])
        normed[at] = normed_now[...].T
        for where in chunks:
            yield "v2"
            result, slope = gelu_and_slope(inner[where])
            slope_two[at, where, :] = slope
            active_now[where, :] = result.astype(BF16)
        yield "m3"
        branch = dot(active_now[...], w_down[tower])
        active[at] = active_now[...].T
        for where in chunks:
            yield "v3"
            state = head_part[at, where, :] + branch[where]
            low_state[1 - tower, where, :] = state.astype(BF16)
            ends_mine[where, :] = state
        yield "t"
        turned[at + 1] = low_state[1 - tower, :rows].T

    def hold_logits(tower, at, row):
        spot = pl.multiple_of(rows + 8 * section, 8)
        logits_all[tower, pl.ds(spot, 8), :LANES] = at[row : row + 8, :LANES].astype(F32)

    def hold_low(ref, slot, at, row):
        spot = pl.multiple_of(rows + TILE * section, TILE)
        ref[slot, pl.ds(spot, TILE), :LANES] = at[row : row + TILE, :LANES].astype(BF16)

    column = lax.broadcasted_iota(jnp.int32, (1, wide), 1)
    whole_lanes = wide - LANES
    inside = lax.broadcasted_iota(jnp.int32, (1, LANES), 1) < lay.bins - whole_lanes

    def head_logits(step, tower):
        yield "M", 5 * rows / 8
        logits = dot_right_t(low_state[1 - tower, :rows], w_head[tower])
        for where in chunks:
            yield "V", weight_of
            logits_all[tower, where, :] = logits[where]

    def head_softmax(step, tower):
        for where in chunks:
            yield "V", 14 * weight_of
            some = logits_all[tower, where, :]
            some = jnp.concatenate(
                [some[:, :whole_lanes], jnp.where(inside, some[:, whole_lanes:], -1e30)], axis=1
            )
            goal = meta[step, where, 2 + tower : 3 + tower]
            raised = jnp.exp(some - jnp.max(some, axis=-1, keepdims=True))
            ratio = jnp.where(goal >= 0, 1.0, 0.0) / row_sum(raised)
            logit_grads[tower, where, :] = (raised * ratio - jnp.where(column == goal, 1.0, 0.0)).astype(BF16)

    def head_products(step, tower):
        at = 2 * step + tower
        yield "M", 5 * rows / 8
        pulled = dot(logit_grads[tower, :rows], w_head[tower])
        for where in chunks:
            yield "V", weight_of
            head_part[at, where, :] = pulled[where]
        yield "M", 5 * rows / 8
        some = dot(turned[at + 1], logit_grads[tower, :rows])
        yield "V", 80
        g_head[tower] += some

    def tick(step, tower, stages="flsp"):
        at = 2 * step + tower
        count = len(chunks)
        streams = {}
        if "f" in stages:
            streams["f"] = forward(step, tower)
        if "s" in stages:
            streams["s"] = head_softmax(step - 1, tower)
        if "l" in stages:
            streams["l"] = head_logits(step - 1 + tower, 1 - tower)
        if "p" in stages:
            streams["p"] = head_products(step - 2 + tower, 1 - tower)
        for stream in streams.values():
            next(stream)

        def go(name, pieces=1):
            for _ in range(pieces):
                if name in streams:
                    next(streams[name], None)

        if "f" not in stages:
            for name in "spl":
                go(name, 100)
            return
        first, second = FIRST, SECOND
        go("f")
        go("s", first)
        go("f")
        if "p" in stages:
            hold_low(logit_grads, 1 - tower, unit_one.at[at], 0)
        if "l" in stages:
            hold_low(low_state, tower, unit_one.at[at], 0)
        for turn in range(1, count):
            go("f")
            if turn % 2 == 1:
                go("p")
                go("l")
        go("p", 100)
        go("l", 100)
        if "s" in stages:
            hold_logits(tower, unit_two.at[at], rows - 8)
        go("f")
        go("s", second)
        go("f", count)
        if "s" in stages:
            hold_logits(tower, slope_two.at[at], rows - 8)
        go("f")
        go("s", 100)
        go("f", 100)

    def forward_step(step, carry):
        tick(step, 0)
        tick(step, 1)
        return carry

    tick(0, 0, "f")
    tick(0, 1, "fl")
    tick(1, 0, "fls")
    tick(1, 1)
    lax.fori_loop(2, steps, forward_step, 0)
    tick(steps, 0, "lsp")
    tick(steps, 1, "sp")
    tick(steps + 1, 0, "p")

    def both(value):
        return jnp.concatenate([value] * (width // LANES), axis=1)

    def backward(step, tower):
        at = 2 * step + tower
        for where in chunks:
            yield "V", weight_of
            state_grad = head_part[at, where, :] + back[where, :].astype(F32)
            head_part[at, where, :] = state_grad
            branch_grads[tower][where, :] = state_grad.astype(BF16)
        yield "M", rows / 4
        active_grad = dot_right_t(branch_grads[tower][...], w_down[tower])
        for where in chunks:
            yield "V", weight_of
            inner_grads[tower][where, :] = (active_grad[where] * slope_two[at, where, :]).astype(BF16)
        yield "M", rows / 4
        normed_grad = dot_right_t(inner_grads[tower][...], w_up[tower])
        for where in chunks:
            yield "V", 12.5 * weight_of
            unit = unit_two[at, where, :]
            scaled = normed_grad[where] * gains[tower, 1:2, :]
            first = row_sum(scaled) * part
            second = row_sum(scaled * unit) * part
            hidden_grad = head_part[at, where, :] + (scaled - first - unit * second) * both(scale_two[at, where, :])
            out_grad = hidden_grad * slope_one[at, where, :]
            unit = unit_one[at, where, :]
            product = out_grad * unit
            g_gain[tower] += jnp.sum(product.reshape(chunk // 8, 8, width), axis=0)
            gain = gains[tower, 0:1, :]
            scaled = out_grad * gain
            first = row_sum(scaled) * part
            second = row_sum(product * gain) * part
            pre_grads[tower, where, :] = (
                (scaled - first - unit * second) * both(scale_one[at, where, :])
            ).astype(BF16)
        yield "M", rows / 4
        input_grad = dot_right_t(pre_grads[tower], w_cat[tower, :width])
        for where in chunks:
            yield "V", 0.5 * weight_of
            back[where, :] = input_grad[where].astype(BF16)

    def weight_grads(step, tower):
        at = 2 * step + tower
        for left, right, total in ((active, branch_grads, g_down), (normed, inner_grads, g_up)):
            yield "M", rows / 4 + 20
            some = dot(left[at], right[tower][...])
            yield "V", 32
            total[tower] += some
        yield "M", rows / 4 + 40
        some = dot(jnp.concatenate([turned[at], turned_pick[at]], axis=0), pre_grads[tower])
        yield "V", 36
        g_cat[tower] += some

    back[...] = jnp.zeros_like(back)
    for ref in (branch_grads[0], inner_grads[0], pre_grads.at[0]):
        ref[...] = jnp.zeros((rows, width), BF16)

    def backward_step(turn, carry):
        step = steps - 1 - turn
        later = jnp.minimum(step + 1, steps - 1)
        interleave([backward(step, 1), weight_grads(later, 0)])
        interleave([backward(step, 0), weight_grads(step, 1)])
        return carry

    lax.fori_loop(0, steps, backward_step, 0)
    interleave([weight_grads(0, 0)])
    first = back[...].astype(F32)
    last = ends_mine[...]
    is_first = section == 0
    ends_mine[...] = jnp.where(is_first, first, last)
    ends_send[...] = jnp.where(is_first, last, first).astype(BF16)

    @pl.when(pl.program_id(0) == pl.num_programs(0) - 1)
    def finish():
        count = jnp.sum(whole_valid[...].astype(F32), axis=(0, 1), keepdims=True).astype(jnp.int32)
        spot = lax.broadcasted_iota(jnp.int32, (1, width), 1)
        bits = jnp.where(spot < BITS, (count >> jnp.minimum(spot, BITS)) & 1, 0).astype(F32)
        for packed, slot in ((keep, section), (send, 1 - section)):
            kind = packed.dtype
            for name, value in (
                ("in", g_cat[slot, :width]),
                ("up", g_up[slot]),
                ("down", g_down[slot]),
                ("table", g_cat[slot, width : width + lay.codes]),
            ):
                low, high = lay.spots[name]
                packed[low:high, :] = value.astype(kind)
            in_gain = jnp.sum(g_gain[slot], axis=0, keepdims=True)
            pulled = jnp.sum((w_up[slot].astype(F32) * g_up[slot]).T, axis=0, keepdims=True)
            block_gain = pulled / gains[slot, 1:2, :]
            own = bits if packed is keep else jnp.zeros_like(bits)
            low, high = lay.spots["head"]
            packed[low:high, :] = lay.with_tail(g_head[slot].T, in_gain, block_gain, own).astype(kind)
            if lay.rows > lay.used:
                packed[lay.used :, :] = jnp.zeros((lay.rows - lay.used, width), kind)


def combine_kernel(parts, which, keep, received, *outs):
    rows = outs[0].shape[0]
    for turn, out in enumerate(outs):
        low = pl.multiple_of((which[0] ^ turn) * rows, TILE)
        value = keep[pl.ds(low, rows), :].astype(F32) + received[pl.ds(low, rows), :].astype(F32)
        out[...] = value.astype(out.dtype)


def update_kernel(lay, parts, which, *refs):
    pieces, ins, outs = refs[:parts], refs[parts : parts + 18], refs[parts + 18 : parts + 42]
    total, scale = refs[-2:]
    step = pl.program_id(0)

    def new(at, spot, grad):
        weight, moment, average = ins[3 * at : 3 * at + 3]
        step_grad = grad.astype(F32) * scale[0:1, 0:1]
        new_moment = MOMENTUM * moment[spot] + step_grad
        new_weight = weight[spot] - RATE * (step_grad + MOMENTUM * new_moment)
        out_moment, out_average, out_weight, out_copy = outs[4 * at : 4 * at + 4]
        out_moment[spot] = new_moment
        out_average[spot] = AVERAGE * average[spot] + (1.0 - AVERAGE) * new_weight
        out_weight[spot] = new_weight
        out_copy[0] = new_weight.astype(BF16)

    @pl.when(step == 0)
    def start():
        rows = pieces[0].shape[0]
        for turn, piece in enumerate(pieces):
            low = pl.multiple_of((which[0] ^ turn) * rows, TILE)
            total[pl.ds(low, rows), :] = piece[...]
        low = lay.tail // TILE * TILE
        high = lay.spots["head"][1]
        tail = total[low:high, :].astype(F32)[lay.tail - low : lay.tail - low + 3]
        lane = lax.broadcasted_iota(jnp.int32, (1, lay.width), 1)
        place = jnp.where(lane < BITS, (1 << jnp.minimum(lane, BITS)).astype(F32), 0.0)
        count = jnp.sum(tail[2:3] * place, axis=-1, keepdims=True)
        scale[...] = jnp.broadcast_to(GRAD_SCALE * lax.rsqrt(count), scale.shape)
        low, high = lay.spots["table"]
        new(0, (0,), total[low:high, :])
        new(2, (0,), tail[0:2])

    for at, name in ((1, "in"), (3, "up"), (4, "down")):
        rows = ins[3 * at].shape[1]
        low = pl.multiple_of(lay.spots[name][0] + step * rows, TILE)
        new(at, (0,), total[pl.ds(low, rows), :])
    rows = ins[15].shape[0]
    low = pl.multiple_of(lay.spots["head"][0] + step * rows, TILE)
    new(5, (slice(None), 0), total[pl.ds(low, rows), :])


def swap(value):
    return lax.ppermute(value, "section", [(0, 1), (1, 0)])


def across(array, mask, length):
    return lax.ppermute(array, "dp", [(i, i ^ mask) for i in range(length)])


def on_device(block, chunk, length, latent, codes, targets, valid, *weights):
    section = lax.axis_index("section").astype(jnp.int32)
    index = lax.axis_index("dp").astype(jnp.int32)
    rows, width = latent.shape
    steps = codes.shape[1]
    own_rows = rows // 2
    block = min(block, own_rows)
    blocks = own_rows // block
    bins = weights[15].shape[2]
    weights = weights[:15] + tuple(jnp.transpose(array, (2, 0, 1)) for array in weights[15:])
    codes, targets = jnp.swapaxes(codes, 0, 1), jnp.swapaxes(targets, 0, 1)
    table, w_in, gains, w_up, w_down, w_head = weights[0::3]
    lay = Layout(table.shape[1], width, bins)
    packed_shape = (lay.rows, width)
    roomy = pltpu.CompilerParams(vmem_limit_bytes=VMEM)
    mine = pl.pallas_call(
        functools.partial(pack_kernel, lay),
        out_shape=jax.ShapeDtypeStruct(packed_shape, BF16),
        compiler_params=roomy,
        name="pack",
    )(table, w_in, w_up, w_down, w_head, gains)
    theirs = swap(mine)

    def spec_rows(*shape):
        return pl.BlockSpec(shape, lambda i, which: (which[0] * blocks + i,) + (0,) * (len(shape) - 1))

    def spec_lanes(*shape):
        return pl.BlockSpec(shape, lambda i, which: (0,) * (len(shape) - 1) + (which[0] * blocks + i,))

    def spec_whole(*shape):
        return pl.BlockSpec(shape, lambda i, which: (0,) * len(shape))

    def spec_once(*shape):
        return pl.BlockSpec(shape, lambda i, which: (0,) * len(shape), pipeline_mode=pl.Buffered(1))

    def spec_out(*shape):
        return pl.BlockSpec(shape, lambda i, which: (i, 0))

    ticks = 2 * steps
    square = (2, width, width)
    per_tick = (ticks, block, width)
    narrow = (ticks, block, LANES)
    pair = (2, block, width)
    keep, send, ends_mine, ends_send = pl.pallas_call(
        functools.partial(towers_kernel, lay, steps, chunk),
        grid_spec=pltpu.PrefetchScalarGridSpec(
            num_scalar_prefetch=1,
            grid=(blocks,),
            in_specs=[
                spec_rows(block, width),
                spec_lanes(steps, 2, block),
                spec_lanes(steps, 2, block),
                spec_lanes(steps, block),
                spec_whole(steps, rows),
                spec_once(*packed_shape),
                spec_once(*packed_shape),
            ],
            out_specs=[
                spec_once(*packed_shape),
                spec_once(*packed_shape),
                spec_out(block, width),
                spec_out(block, width),
            ],
            scratch_shapes=[
                pltpu.VMEM((2, width + LANES, width), BF16),
                pltpu.VMEM(square, BF16),
                pltpu.VMEM(square, BF16),
                pltpu.VMEM((2, lay.wide, width), BF16),
                pltpu.VMEM((2, 2, width), F32),
                pltpu.VMEM((2, width + lay.codes, width), F32),
                pltpu.VMEM(square, F32),
                pltpu.VMEM(square, F32),
                pltpu.VMEM((2, width, lay.wide), F32),
                pltpu.VMEM((2, 8, width), F32),
                pltpu.VMEM((steps, block, 8), jnp.int32),
                pltpu.VMEM((ticks, block, LANES), BF16),
                pltpu.VMEM((2, block + 2 * TILE, width), BF16),
                pltpu.VMEM(per_tick, F32),
                pltpu.VMEM(per_tick, F32),
                pltpu.VMEM(per_tick, F32),
                pltpu.VMEM(per_tick, F32),
                pltpu.VMEM((block, width), BF16),
                pltpu.VMEM((block, width), BF16),
                pltpu.VMEM((ticks, width, block), BF16),
                pltpu.VMEM((ticks, width, block), BF16),
                pltpu.VMEM(narrow, F32),
                pltpu.VMEM(narrow, F32),
                pltpu.VMEM(per_tick, F32),
                pltpu.VMEM((ticks + 1, width, block), BF16),
                pltpu.VMEM((ticks, lay.codes, block), BF16),
                pltpu.VMEM((2, block + TILE, lay.wide), F32),
                pltpu.VMEM((2, block + 2 * TILE, lay.wide), BF16),
                pltpu.VMEM(pair, BF16),
                pltpu.VMEM((block, width), BF16),
            ],
        ),
        out_shape=[
            jax.ShapeDtypeStruct(packed_shape, BF16),
            jax.ShapeDtypeStruct(packed_shape, BF16),
            jax.ShapeDtypeStruct((own_rows, width), F32),
            jax.ShapeDtypeStruct((own_rows, width), BF16),
        ],
        compiler_params=roomy,
        name="towers",
    )(section[None], latent, codes, targets, valid, valid, mine, theirs)

    parts = min(4, length)
    place = (index % parts)[None]
    in_smem = pl.BlockSpec(memory_space=pltpu.SMEM)

    def spec_all(*shape):
        return pl.BlockSpec(shape, lambda *_: (0,) * len(shape))

    part_shape = (lay.rows // parts, width)
    own, *others = pl.pallas_call(
        functools.partial(combine_kernel, parts),
        in_specs=[in_smem, spec_all(*packed_shape), spec_all(*packed_shape)],
        out_shape=[jax.ShapeDtypeStruct(part_shape, F32)]
        + [jax.ShapeDtypeStruct(part_shape, BF16)] * (parts - 1),
        compiler_params=roomy,
        name="combine",
    )(place, keep, swap(send))
    current = own
    for arrived in [across(other, mask, length) for mask, other in enumerate(others, 1)]:
        current = current + arrived.astype(F32)
    current = current.astype(BF16)
    masks = [1 << bit for bit in range(length.bit_length() - 1)][parts.bit_length() - 1 :]
    halved = masks[:1] if len(masks) > 1 else []
    for mask in halved:
        half = current.shape[0] // 2
        upper = (index // mask) % 2 == 1
        sent = jnp.where(upper, current[:half], current[half:])
        kept = jnp.where(upper, current[half:], current[:half])
        current = (kept.astype(F32) + across(sent, mask, length).astype(F32)).astype(BF16)
    for mask in masks[len(halved) :]:
        current = (current.astype(F32) + across(current, mask, length).astype(F32)).astype(BF16)
    for mask in halved:
        upper = (index // mask) % 2 == 1
        found = across(current, mask, length)
        current = jnp.where(upper, jnp.concatenate([found, current]), jnp.concatenate([current, found]))
    pieces = [current] + [across(current, mask, length) for mask in range(1, parts)]

    other = swap(ends_send).astype(F32)
    ends = jnp.where(
        section == 0,
        jnp.concatenate([ends_mine, other]),
        jnp.concatenate([other, ends_mine]),
    )[None]
    head_rows = -(-bins // (STEPS * TILE)) * TILE
    news, in_specs, out_specs = [], [], []
    for at in range(6):
        shape = weights[3 * at].shape
        news += [jax.ShapeDtypeStruct(shape, F32)] * 3
        news.append(jax.ShapeDtypeStruct((1, shape[0], width) if at == 5 else shape, BF16))
        if at in (0, 2):
            spec = copy_spec = spec_all(*shape)
        elif at == 5:
            spec = pl.BlockSpec((head_rows, 1, width), lambda i: (i, 0, 0))
            copy_spec = pl.BlockSpec((1, head_rows, width), lambda i: (0, i, 0))
        else:
            spec = copy_spec = pl.BlockSpec((1, width // STEPS, width), lambda i: (0, i, 0))
        in_specs += [spec] * 3
        out_specs += [spec] * 3 + [copy_spec]
    total_rows = max(lay.rows, lay.spots["head"][0] + STEPS * head_rows)
    updated = pl.pallas_call(
        functools.partial(update_kernel, lay, parts),
        grid=(STEPS,),
        in_specs=[in_smem] + [spec_all(*part_shape)] * parts + in_specs,
        out_specs=out_specs,
        out_shape=news,
        scratch_shapes=[pltpu.VMEM((total_rows, width), BF16), pltpu.VMEM((8, LANES), F32)],
        compiler_params=roomy,
        name="update",
    )(place, *pieces, *weights)
    table_out, in_out, gain_out, up_out, down_out, head_out = (updated[4 * at : 4 * at + 4] for at in range(6))
    head_out = [jnp.transpose(array, (1, 2, 0)) for array in head_out[:3]] + [jnp.swapaxes(head_out[3], 1, 2)]
    return (ends, *table_out, *in_out, *gain_out, *up_out, *down_out, *head_out)


def solution(mesh):
    by_section = P("section", None, None)
    in_specs = (P("dp", None), P(None, None, "dp"), P(None, None, "dp"), P(None, "dp")) + (by_section,) * 18
    out_specs = (P("section", "dp", None),) + (by_section,) * 24
    return jax.shard_map(
        functools.partial(on_device, 512, 64, mesh.shape["dp"]),
        mesh=mesh,
        in_specs=in_specs,
        out_specs=out_specs,
        check_vma=False,
    )
```

```python
import functools

import jax
import jax.numpy as jnp
from jax import lax
from jax.experimental import pallas as pl
from jax.experimental.pallas import tpu as pltpu
from jax.sharding import PartitionSpec as P

EPS = 1e-05
MOMENTUM = 0.5
AVERAGE = 0.9
RATE = 0.2
GRAD_SCALE = 4.0
GELU_LINE = 0.7978845608028654
GELU_CUBE = 0.7978845608028654 * 0.044715

BF16 = jnp.bfloat16
F32 = jnp.float32
LANES = 128
TILE = 16
BITS = 24
FIRST, SECOND = 4, 4
SPARE = 7
STEPS = 4
SMALL = 16 * 1024 * 1024
VMEM = 63 * 1024 * 1024


def dot(left, right):
    return jnp.dot(left, right, preferred_element_type=F32)


def dot_right_t(left, right):
    return lax.dot_general(left, right, (((1,), (1,)), ((), ())), preferred_element_type=F32)


def dot_left_t(left, right):
    return lax.dot_general(left, right, (((0,), (0,)), ((), ())), preferred_element_type=F32)


def gelu_and_slope(value):
    square = value * value
    half = 0.5 + 0.5 * jnp.tanh(value * (GELU_LINE + GELU_CUBE * square))
    result = value * half
    return result, half + result * (1.0 - half) * (2 * GELU_LINE + (6 * GELU_CUBE) * square)


def normalise(value):
    part = 1.0 / value.shape[-1]
    centered = value - jnp.sum(value, axis=-1, keepdims=True) * part
    scale = lax.rsqrt(jnp.sum(centered * centered, axis=-1, keepdims=True) * part + EPS)
    return centered * scale, scale


class Layout:
    def __init__(self, codes, width, bins):
        self.codes, self.width, self.bins = codes, width, bins
        self.wide = -(-bins // LANES) * LANES
        spots, at = {}, 0
        sizes = (("in", width), ("up", width), ("down", width), ("head", bins + SPARE), ("table", codes))
        for name, rows in sizes:
            spots[name] = (at, at + -(-rows // TILE) * TILE)
            at = spots[name][1]
        spots["table"] = (spots["table"][0], spots["table"][0] + codes)
        self.tail = spots["head"][0] + bins
        self.spots = spots
        self.used = at
        self.rows = -(-at // (8 * TILE)) * (8 * TILE)

    def with_tail(self, head, *extra):
        low, high = self.spots["head"]
        left = high - low - self.bins - sum(rows.shape[0] for rows in extra)
        return jnp.concatenate([head[: self.bins], *extra, jnp.zeros((left, self.width), F32)], axis=0)


def split_three(value):
    high = value.astype(BF16)
    left = value - high.astype(F32)
    middle = left.astype(BF16)
    low = (left - middle.astype(F32)).astype(BF16)
    return high, middle, low


def pack_kernel(lay, table, w_in, w_up, w_down, w_head, gains, out):
    for name, ref in (("in", w_in), ("up", w_up), ("down", w_down), ("table", table)):
        low, high = lay.spots[name]
        out[low:high, :] = ref[0].astype(BF16)
    low, high = lay.spots["head"]
    pieces = [piece.astype(F32) for piece in split_three(gains[0])]
    out[low:high, :] = lay.with_tail(w_head[:, 0, :], *pieces).astype(BF16)
    if lay.rows > lay.used:
        out[lay.used :, :] = jnp.zeros((lay.rows - lay.used, lay.width), BF16)


def row_sum(value):
    return jnp.sum(value, axis=-1, keepdims=True)


def interleave(streams, matmul_delay=220, vector_delay=60):
    clock = {"M": 0.0, "V": 0.0}
    live = []
    for rank, stream in enumerate(streams):
        live.append([stream, rank, next(stream), 0.0])
    while live:
        best = min(live, key=lambda entry: (max(clock[entry[2][0]], entry[3]), entry[1]))
        unit, cost = best[2]
        begin = max(clock[unit], best[3])
        clock[unit] = begin + cost
        best[3] = begin + cost + (matmul_delay if unit == "M" else vector_delay)
        best[2] = next(best[0], None)
        if best[2] is None:
            live.remove(best)


def in_turn(*streams):
    for stream in streams:
        yield from stream


def towers_kernel(lay, steps, chunk, which, latent, codes, targets, valid, whole_valid, mine, theirs,
                  keep, send, ends_mine, ends_send,
                  w_cat, w_up, w_down, w_head, gains,
                  g_cat, g_up, g_down, g_head, g_gain,
                  meta, picks, low_state, unit_one, slope_one, unit_two, slope_two, active_now, normed_now, active, normed,
                  scale_one, scale_two, head_part, turned, turned_pick, logits_all, logit_grads, pre_grads, back):
    branch_grads = tuple(low_state.at[slot, : latent.shape[0]] for slot in range(2))
    inner_grads = (active_now, normed_now)
    rows, width = latent.shape
    wide = lay.wide
    part = 1.0 / width
    section = which[0]
    chunks = [slice(at, at + chunk) for at in range(0, rows, chunk)]
    weight_of = chunk / 8

    @pl.when(pl.program_id(0) == 0)
    def start():
        for ref in (g_cat, g_up, g_down, g_head, g_gain):
            ref[...] = jnp.zeros_like(ref)
        for packed, slot in ((mine, section), (theirs, 1 - section)):
            for name, ref in (("up", w_up), ("down", w_down)):
                low, high = lay.spots[name]
                ref[slot] = packed[low:high, :]
            low, high = lay.spots["in"]
            w_cat[slot, :width] = packed[low:high, :]
            low, high = lay.spots["table"]
            w_cat[slot, width : width + lay.codes] = packed[low:high, :]
            w_cat[slot, width + lay.codes :] = jnp.zeros((LANES - lay.codes, width), BF16)
            low, high = lay.spots["head"]
            w_head[slot] = jnp.zeros((wide, width), BF16)
            w_head[slot, : high - low] = packed[low:high, :]
            start_tail = (lay.tail - low) // TILE * TILE
            block = packed[low + start_tail : high, :].astype(F32)
            at = lay.tail - low - start_tail
            gains[slot] = block[at : at + 2] + block[at + 2 : at + 4] + block[at + 4 : at + 6]
            row = lax.broadcasted_iota(jnp.int32, block.shape, 0)
            w_head[slot, start_tail : high - low] = jnp.where(row < at, block, 0.0).astype(BF16)

    lane = lax.broadcasted_iota(jnp.int32, (rows, LANES), 1)
    upright = lax.broadcasted_iota(jnp.int32, (lay.codes, rows), 0)
    for step in range(steps):
        alive = valid[step : step + 1, :]
        line = [codes[step, tower : tower + 1, :] for tower in range(2)]
        line += [jnp.where(alive > 0, targets[step, tower : tower + 1, :], -1) for tower in range(2)]
        columns = jnp.concatenate(line + [jnp.zeros((4, rows), jnp.int32)], axis=0).T
        meta[step] = columns
        for tower in range(2):
            turned_pick[2 * step + tower] = (line[tower] == upright).astype(F32).astype(BF16)
            picks[2 * step + tower] = (columns[:, tower : tower + 1] == lane).astype(F32).astype(BF16)
    low_state[0, :rows] = latent[...]
    turned[0] = latent[...].T

    def forward(step, tower):
        at = 2 * step + tower
        yield "m1"
        pre = dot(jnp.concatenate([low_state[tower, :rows], picks[at]], axis=1), w_cat[tower])
        for where in chunks:
            yield "v1"
            unit, scale = normalise(pre[where])
            unit_one[at, where, :] = unit
            scale_one[at, where, :] = jnp.broadcast_to(scale, (chunk, LANES))
            hidden, slope = gelu_and_slope(unit * gains[tower, 0:1, :])
            slope_one[at, where, :] = slope
            head_part[at, where, :] = hidden
            unit, scale = normalise(hidden)
            unit_two[at, where, :] = unit
            scale_two[at, where, :] = jnp.broadcast_to(scale, (chunk, LANES))
            normed_now[where, :] = (unit * gains[tower, 1:2, :]).astype(BF16)
        yield "m2"
        inner = dot(normed_now[...], w_up[tower])
        normed[at] = normed_now[...].T
        for where in chunks:
            yield "v2"
            result, slope = gelu_and_slope(inner[where])
            slope_two[at, where, :] = slope
            active_now[where, :] = result.astype(BF16)
        yield "m3"
        branch = dot(active_now[...], w_down[tower])
        active[at] = active_now[...].T
        for where in chunks:
            yield "v3"
            state = head_part[at, where, :] + branch[where]
            low_state[1 - tower, where, :] = state.astype(BF16)
            ends_mine[where, :] = state
        yield "t"
        turned[at + 1] = low_state[1 - tower, :rows].T

    def hold_logits(tower, at, row):
        spot = pl.multiple_of(rows + 8 * section, 8)
        logits_all[tower, pl.ds(spot, 8), :LANES] = at[row : row + 8, :LANES].astype(F32)

    def hold_low(ref, slot, at, row):
        spot = pl.multiple_of(rows + TILE * section, TILE)
        ref[slot, pl.ds(spot, TILE), :LANES] = at[row : row + TILE, :LANES].astype(BF16)

    column = lax.broadcasted_iota(jnp.int32, (1, wide), 1)
    whole_lanes = wide - LANES
    inside = lax.broadcasted_iota(jnp.int32, (1, LANES), 1) < lay.bins - whole_lanes

    def head_logits(step, tower):
        yield "M", 5 * rows / 8
        logits = dot_right_t(low_state[1 - tower, :rows], w_head[tower])
        for where in chunks:
            yield "V", weight_of
            logits_all[tower, where, :] = logits[where]

    def head_softmax(step, tower):
        for where in chunks:
            yield "V", 14 * weight_of
            some = logits_all[tower, where, :]
            some = jnp.concatenate(
                [some[:, :whole_lanes], jnp.where(inside, some[:, whole_lanes:], -1e30)], axis=1
            )
            goal = meta[step, where, 2 + tower : 3 + tower]
            raised = jnp.exp(some - jnp.max(some, axis=-1, keepdims=True))
            ratio = jnp.where(goal >= 0, 1.0, 0.0) / row_sum(raised)
            logit_grads[tower, where, :] = (raised * ratio - jnp.where(column == goal, 1.0, 0.0)).astype(BF16)

    def head_products(step, tower):
        at = 2 * step + tower
        yield "M", 5 * rows / 8
        pulled = dot(logit_grads[tower, :rows], w_head[tower])
        for where in chunks:
            yield "V", weight_of
            head_part[at, where, :] = pulled[where]
        yield "M", 5 * rows / 8
        some = dot(turned[at + 1], logit_grads[tower, :rows])
        yield "V", 80
        g_head[tower] += some

    def tick(step, tower, stages="flsp"):
        at = 2 * step + tower
        count = len(chunks)
        streams = {}
        if "f" in stages:
            streams["f"] = forward(step, tower)
        if "s" in stages:
            streams["s"] = head_softmax(step - 1, tower)
        if "l" in stages:
            streams["l"] = head_logits(step - 1 + tower, 1 - tower)
        if "p" in stages:
            streams["p"] = head_products(step - 2 + tower, 1 - tower)
        for stream in streams.values():
            next(stream)

        def go(name, pieces=1):
            for _ in range(pieces):
                if name in streams:
                    next(streams[name], None)

        if "f" not in stages:
            for name in "spl":
                go(name, 100)
            return
        first, second = FIRST, SECOND
        go("f")
        go("s", first)
        go("f")
        if "p" in stages:
            hold_low(logit_grads, 1 - tower, unit_one.at[at], 0)
        if "l" in stages:
            hold_low(low_state, tower, unit_one.at[at], 0)
        for turn in range(1, count):
            go("f")
            if turn % 2 == 1:
                go("p")
                go("l")
        go("p", 100)
        go("l", 100)
        if "s" in stages:
            hold_logits(tower, unit_two.at[at], rows - 8)
        go("f")
        go("s", second)
        go("f", count)
        if "s" in stages:
            hold_logits(tower, slope_two.at[at], rows - 8)
        go("f")
        go("s", 100)
        go("f", 100)

    def forward_step(step, carry):
        tick(step, 0)
        tick(step, 1)
        return carry

    tick(0, 0, "f")
    tick(0, 1, "fl")
    tick(1, 0, "fls")
    tick(1, 1)
    lax.fori_loop(2, steps, forward_step, 0)
    tick(steps, 0, "lsp")
    tick(steps, 1, "sp")
    tick(steps + 1, 0, "p")

    def both(value):
        return jnp.concatenate([value] * (width // LANES), axis=1)

    def backward(step, tower):
        at = 2 * step + tower
        for where in chunks:
            yield "V", weight_of
            state_grad = head_part[at, where, :] + back[where, :].astype(F32)
            head_part[at, where, :] = state_grad
            branch_grads[tower][where, :] = state_grad.astype(BF16)
        yield "M", rows / 4
        active_grad = dot_right_t(branch_grads[tower][...], w_down[tower])
        for where in chunks:
            yield "V", weight_of
            inner_grads[tower][where, :] = (active_grad[where] * slope_two[at, where, :]).astype(BF16)
        yield "M", rows / 4
        normed_grad = dot_right_t(inner_grads[tower][...], w_up[tower])
        for where in chunks:
            yield "V", 12.5 * weight_of
            unit = unit_two[at, where, :]
            scaled = normed_grad[where] * gains[tower, 1:2, :]
            first = row_sum(scaled) * part
            second = row_sum(scaled * unit) * part
            hidden_grad = head_part[at, where, :] + (scaled - first - unit * second) * both(scale_two[at, where, :])
            out_grad = hidden_grad * slope_one[at, where, :]
            unit = unit_one[at, where, :]
            product = out_grad * unit
            g_gain[tower] += jnp.sum(product.reshape(chunk // 8, 8, width), axis=0)
            gain = gains[tower, 0:1, :]
            scaled = out_grad * gain
            first = row_sum(scaled) * part
            second = row_sum(product * gain) * part
            pre_grads[tower, where, :] = (
                (scaled - first - unit * second) * both(scale_one[at, where, :])
            ).astype(BF16)
        yield "M", rows / 4
        input_grad = dot_right_t(pre_grads[tower], w_cat[tower, :width])
        for where in chunks:
            yield "V", 0.5 * weight_of
            back[where, :] = input_grad[where].astype(BF16)

    def weight_grads(step, tower):
        at = 2 * step + tower
        for left, right, total in ((active, branch_grads, g_down), (normed, inner_grads, g_up)):
            yield "M", rows / 4 + 20
            some = dot(left[at], right[tower][...])
            yield "V", 32
            total[tower] += some
        yield "M", rows / 4 + 40
        some = dot(jnp.concatenate([turned[at], turned_pick[at]], axis=0), pre_grads[tower])
        yield "V", 36
        g_cat[tower] += some

    back[...] = jnp.zeros_like(back)
    for ref in (branch_grads[0], inner_grads[0], pre_grads.at[0]):
        ref[...] = jnp.zeros((rows, width), BF16)

    def backward_step(turn, carry):
        step = steps - 1 - turn
        later = jnp.minimum(step + 1, steps - 1)
        interleave([backward(step, 1), weight_grads(later, 0)])
        interleave([backward(step, 0), weight_grads(step, 1)])
        return carry

    lax.fori_loop(0, steps, backward_step, 0)
    interleave([weight_grads(0, 0)])
    first = back[...].astype(F32)
    last = ends_mine[...]
    is_first = section == 0
    ends_mine[...] = jnp.where(is_first, first, last)
    ends_send[...] = jnp.where(is_first, last, first).astype(BF16)

    @pl.when(pl.program_id(0) == pl.num_programs(0) - 1)
    def finish():
        count = jnp.sum(whole_valid[...].astype(F32), axis=(0, 1), keepdims=True).astype(jnp.int32)
        spot = lax.broadcasted_iota(jnp.int32, (1, width), 1)
        bits = jnp.where(spot < BITS, (count >> jnp.minimum(spot, BITS)) & 1, 0).astype(F32)
        for packed, slot in ((keep, section), (send, 1 - section)):
            kind = packed.dtype
            for name, value in (
                ("in", g_cat[slot, :width]),
                ("up", g_up[slot]),
                ("down", g_down[slot]),
                ("table", g_cat[slot, width : width + lay.codes]),
            ):
                low, high = lay.spots[name]
                packed[low:high, :] = value.astype(kind)
            in_gain = jnp.sum(g_gain[slot], axis=0, keepdims=True)
            pulled = jnp.sum((w_up[slot].astype(F32) * g_up[slot]).T, axis=0, keepdims=True)
            block_gain = pulled / gains[slot, 1:2, :]
            own = bits if packed is keep else jnp.zeros_like(bits)
            low, high = lay.spots["head"]
            packed[low:high, :] = lay.with_tail(g_head[slot].T, in_gain, block_gain, own).astype(kind)
            if lay.rows > lay.used:
                packed[lay.used :, :] = jnp.zeros((lay.rows - lay.used, width), kind)


def update_kernel(lay, parts, which, *refs):
    pieces, ins, outs = refs[:parts], refs[parts : parts + 18], refs[parts + 18 : parts + 42]
    stages, total, done = refs[parts + 42 : parts + 66], refs[-2], refs[-1]
    rows = pieces[0].shape[0]
    for turn, piece in enumerate(pieces):
        low = pl.multiple_of((which[0] ^ turn) * rows, TILE)
        total[pl.ds(low, rows), :] = piece[...]
    low = lay.tail // TILE * TILE
    tail = total[low : lay.spots["head"][1], :].astype(F32)[lay.tail - low : lay.tail - low + 3]
    lane = lax.broadcasted_iota(jnp.int32, (1, lay.width), 1)
    place = jnp.where(lane < BITS, (1 << jnp.minimum(lane, BITS)).astype(F32), 0.0)
    count = jnp.sum(tail[2:3] * place, axis=-1, keepdims=True)
    scale = GRAD_SCALE * lax.rsqrt(count)
    copies = []

    def new(at, spot, copy_spot, parts_of, grad):
        weight, moment, average = ins[3 * at : 3 * at + 3]
        step_grad = grad.astype(F32) * scale
        new_moment = MOMENTUM * moment[spot] + step_grad
        new_weight = weight[spot] - RATE * (step_grad + MOMENTUM * new_moment)
        new_average = AVERAGE * average[spot] + (1.0 - AVERAGE) * new_weight
        news = (new_moment, new_average, new_weight, new_weight.astype(BF16))
        for kind, value in enumerate(news):
            stage, out = stages[4 * at + kind], outs[4 * at + kind]
            stage[copy_spot if kind == 3 else spot] = value
            piece = parts_of[1 if kind == 3 else 0]
            copies.append(pltpu.make_async_copy(stage.at[piece], out.at[piece], done.at[len(copies)]))
            copies[-1].start()

    everything = (slice(None),)
    low, high = lay.spots["head"]
    step = -(-lay.bins // (STEPS * TILE)) * TILE
    for begin in range(0, lay.bins, step):
        end = min(begin + step, lay.bins)
        cover = min(-(-end // TILE) * TILE, high - low)
        grad = total[low + begin : low + cover, :].astype(F32)[: end - begin]
        new(5, (slice(begin, end), 0), (0, slice(begin, end)),
            ((slice(begin, end),), (slice(None), slice(begin, end))), grad)
    for at, name in ((1, "in"), (3, "up"), (4, "down"), (0, "table")):
        low, high = lay.spots[name]
        new(at, (0,), (0,), (everything, everything), total[low:high, :])
    new(2, (0,), (0,), (everything, everything), tail[0:2])
    for copy in copies:
        copy.wait()


def swap(value):
    return lax.ppermute(value, "section", [(0, 1), (1, 0)])


def across(array, mask, length):
    return lax.ppermute(array, "dp", [(i, i ^ mask) for i in range(length)])


def on_device(block, chunk, length, latent, codes, targets, valid, *weights):
    section = lax.axis_index("section").astype(jnp.int32)
    index = lax.axis_index("dp").astype(jnp.int32)
    rows, width = latent.shape
    steps = codes.shape[1]
    own_rows = rows // 2
    block = min(block, own_rows)
    blocks = own_rows // block
    bins = weights[15].shape[2]
    weights = weights[:15] + tuple(jnp.transpose(array, (2, 0, 1)) for array in weights[15:])
    codes, targets = jnp.swapaxes(codes, 0, 1), jnp.swapaxes(targets, 0, 1)
    table, w_in, gains, w_up, w_down, w_head = weights[0::3]
    lay = Layout(table.shape[1], width, bins)
    packed_shape = (lay.rows, width)
    roomy = pltpu.CompilerParams(vmem_limit_bytes=VMEM)
    mine = pl.pallas_call(
        functools.partial(pack_kernel, lay),
        out_shape=jax.ShapeDtypeStruct(packed_shape, BF16),
        compiler_params=roomy,
        name="pack",
    )(table, w_in, w_up, w_down, w_head, gains)
    theirs = swap(mine)

    def spec_rows(*shape):
        return pl.BlockSpec(shape, lambda i, which: (which[0] * blocks + i,) + (0,) * (len(shape) - 1))

    def spec_lanes(*shape):
        return pl.BlockSpec(shape, lambda i, which: (0,) * (len(shape) - 1) + (which[0] * blocks + i,))

    def spec_whole(*shape):
        return pl.BlockSpec(shape, lambda i, which: (0,) * len(shape))

    def spec_once(*shape):
        return pl.BlockSpec(shape, lambda i, which: (0,) * len(shape), pipeline_mode=pl.Buffered(1))

    def spec_out(*shape):
        return pl.BlockSpec(shape, lambda i, which: (i, 0))

    ticks = 2 * steps
    square = (2, width, width)
    per_tick = (ticks, block, width)
    narrow = (ticks, block, LANES)
    pair = (2, block, width)
    keep, send, ends_mine, ends_send = pl.pallas_call(
        functools.partial(towers_kernel, lay, steps, chunk),
        grid_spec=pltpu.PrefetchScalarGridSpec(
            num_scalar_prefetch=1,
            grid=(blocks,),
            in_specs=[
                spec_rows(block, width),
                spec_lanes(steps, 2, block),
                spec_lanes(steps, 2, block),
                spec_lanes(steps, block),
                spec_whole(steps, rows),
                spec_once(*packed_shape),
                spec_once(*packed_shape),
            ],
            out_specs=[
                spec_once(*packed_shape),
                spec_once(*packed_shape),
                spec_out(block, width),
                spec_out(block, width),
            ],
            scratch_shapes=[
                pltpu.VMEM((2, width + LANES, width), BF16),
                pltpu.VMEM(square, BF16),
                pltpu.VMEM(square, BF16),
                pltpu.VMEM((2, lay.wide, width), BF16),
                pltpu.VMEM((2, 2, width), F32),
                pltpu.VMEM((2, width + lay.codes, width), F32),
                pltpu.VMEM(square, F32),
                pltpu.VMEM(square, F32),
                pltpu.VMEM((2, width, lay.wide), F32),
                pltpu.VMEM((2, 8, width), F32),
                pltpu.VMEM((steps, block, 8), jnp.int32),
                pltpu.VMEM((ticks, block, LANES), BF16),
                pltpu.VMEM((2, block + 2 * TILE, width), BF16),
                pltpu.VMEM(per_tick, F32),
                pltpu.VMEM(per_tick, F32),
                pltpu.VMEM(per_tick, F32),
                pltpu.VMEM(per_tick, F32),
                pltpu.VMEM((block, width), BF16),
                pltpu.VMEM((block, width), BF16),
                pltpu.VMEM((ticks, width, block), BF16),
                pltpu.VMEM((ticks, width, block), BF16),
                pltpu.VMEM(narrow, F32),
                pltpu.VMEM(narrow, F32),
                pltpu.VMEM(per_tick, F32),
                pltpu.VMEM((ticks + 1, width, block), BF16),
                pltpu.VMEM((ticks, lay.codes, block), BF16),
                pltpu.VMEM((2, block + TILE, lay.wide), F32),
                pltpu.VMEM((2, block + 2 * TILE, lay.wide), BF16),
                pltpu.VMEM(pair, BF16),
                pltpu.VMEM((block, width), BF16),
            ],
        ),
        out_shape=[
            jax.ShapeDtypeStruct(packed_shape, BF16),
            jax.ShapeDtypeStruct(packed_shape, BF16),
            jax.ShapeDtypeStruct((own_rows, width), F32),
            jax.ShapeDtypeStruct((own_rows, width), BF16),
        ],
        compiler_params=roomy,
        name="towers",
    )(section[None], latent, codes, targets, valid, valid, mine, theirs)

    parts = min(4, length)
    place = (index % parts)[None]
    in_smem = pl.BlockSpec(memory_space=pltpu.SMEM)

    part_shape = (lay.rows // parts, width)
    both = keep.astype(F32) + swap(send).astype(F32)
    both = lax.optimization_barrier(both.reshape(parts, *part_shape))

    def part_for(mask):
        return lax.dynamic_index_in_dim(both, place[0] ^ mask, 0, keepdims=False)

    own = part_for(0)
    others = [part_for(mask).astype(BF16) for mask in range(1, parts)]
    current = own
    for arrived in [across(other, mask, length) for mask, other in enumerate(others, 1)]:
        current = current + arrived.astype(F32)
    current = current.astype(BF16)
    masks = [1 << bit for bit in range(length.bit_length() - 1)][parts.bit_length() - 1 :]
    halved = masks[:1] if len(masks) > 1 else []
    for mask in halved:
        half = current.shape[0] // 2
        upper = (index // mask) % 2 == 1
        sent = jnp.where(upper, current[:half], current[half:])
        kept = jnp.where(upper, current[half:], current[:half])
        current = (kept.astype(F32) + across(sent, mask, length).astype(F32)).astype(BF16)
    for mask in masks[len(halved) :]:
        current = (current.astype(F32) + across(current, mask, length).astype(F32)).astype(BF16)
    for mask in halved:
        upper = (index // mask) % 2 == 1
        found = across(current, mask, length)
        current = jnp.where(upper, jnp.concatenate([found, current]), jnp.concatenate([current, found]))
    pieces = [current] + [across(current, mask, length) for mask in range(1, parts)]

    other = swap(ends_send).astype(F32)
    ends = jnp.where(
        section == 0,
        jnp.concatenate([ends_mine, other]),
        jnp.concatenate([other, ends_mine]),
    )[None]
    news = []
    for at in range(6):
        shape = weights[3 * at].shape
        news += [jax.ShapeDtypeStruct(shape, F32)] * 3
        news.append(jax.ShapeDtypeStruct((1, shape[0], width) if at == 5 else shape, BF16))
    copy_count = 4 * (5 + -(-bins // (-(-bins // (STEPS * TILE)) * TILE)))
    updated = pl.pallas_call(
        functools.partial(update_kernel, lay, parts),
        in_specs=[in_smem] + [pl.BlockSpec(memory_space=pltpu.VMEM)] * (parts + 18),
        out_specs=[pl.BlockSpec(memory_space=pl.ANY)] * 24,
        out_shape=news,
        scratch_shapes=[pltpu.VMEM(new.shape, new.dtype) for new in news]
        + [pltpu.VMEM(packed_shape, BF16), pltpu.SemaphoreType.DMA((copy_count,))],
        compiler_params=pltpu.CompilerParams(vmem_limit_bytes=SMALL),
        name="update",
    )(place, *pieces, *weights)
    table_out, in_out, gain_out, up_out, down_out, head_out = (updated[4 * at : 4 * at + 4] for at in range(6))
    head_out = [jnp.transpose(array, (1, 2, 0)) for array in head_out[:3]] + [jnp.swapaxes(head_out[3], 1, 2)]
    return (ends, *table_out, *in_out, *gain_out, *up_out, *down_out, *head_out)


def solution(mesh):
    by_section = P("section", None, None)
    in_specs = (P("dp", None), P(None, None, "dp"), P(None, None, "dp"), P(None, "dp")) + (by_section,) * 18
    out_specs = (P("section", "dp", None),) + (by_section,) * 24
    return jax.shard_map(
        functools.partial(on_device, 512, 64, mesh.shape["dp"]),
        mesh=mesh,
        in_specs=in_specs,
        out_specs=out_specs,
        check_vma=False,
    )
```

```python
import functools

import jax
import jax.numpy as jnp
from jax import lax
from jax.experimental import pallas as pl
from jax.experimental.pallas import tpu as pltpu
from jax.sharding import PartitionSpec as P

EPS = 1e-05
MOMENTUM = 0.5
AVERAGE = 0.9
RATE = 0.2
GRAD_SCALE = 4.0
GELU_LINE = 0.7978845608028654
GELU_CUBE = 0.7978845608028654 * 0.044715

BF16 = jnp.bfloat16
F32 = jnp.float32
LANES = 128
TILE = 16
BITS = 24
FIRST, SECOND, HOLD_AT, BACK_FIRST = 4, 4, 1, 0
CHUNK_ONE, CHUNK_TWO, CHUNK_HEAD, CHUNK_BACK, CHUNK_COPY = 64, 64, 64, 64, 64
LOGITS_FIRST = False
SPARE = 7
STEPS = 4
SMALL = 16 * 1024 * 1024
VMEM = 63 * 1024 * 1024


def dot(left, right):
    return jnp.dot(left, right, preferred_element_type=F32)


def dot_right_t(left, right):
    return lax.dot_general(left, right, (((1,), (1,)), ((), ())), preferred_element_type=F32)


def dot_left_t(left, right):
    return lax.dot_general(left, right, (((0,), (0,)), ((), ())), preferred_element_type=F32)


def gelu_and_slope(value):
    square = value * value
    half = 0.5 + 0.5 * jnp.tanh(value * (GELU_LINE + GELU_CUBE * square))
    result = value * half
    return result, half + result * (1.0 - half) * (2 * GELU_LINE + (6 * GELU_CUBE) * square)


def normalise(value):
    part = 1.0 / value.shape[-1]
    centered = value - jnp.sum(value, axis=-1, keepdims=True) * part
    scale = lax.rsqrt(jnp.sum(centered * centered, axis=-1, keepdims=True) * part + EPS)
    return centered * scale, scale


class Layout:
    def __init__(self, codes, width, bins):
        self.codes, self.width, self.bins = codes, width, bins
        self.wide = -(-bins // LANES) * LANES
        spots, at = {}, 0
        sizes = (("in", width), ("up", width), ("down", width), ("head", bins + SPARE), ("table", codes))
        for name, rows in sizes:
            spots[name] = (at, at + -(-rows // TILE) * TILE)
            at = spots[name][1]
        spots["table"] = (spots["table"][0], spots["table"][0] + codes)
        self.tail = spots["head"][0] + bins
        self.spots = spots
        self.used = at
        self.rows = -(-at // (8 * TILE)) * (8 * TILE)

    def with_tail(self, head, *extra):
        low, high = self.spots["head"]
        left = high - low - self.bins - sum(rows.shape[0] for rows in extra)
        return jnp.concatenate([head[: self.bins], *extra, jnp.zeros((left, self.width), F32)], axis=0)


def split_three(value):
    high = value.astype(BF16)
    left = value - high.astype(F32)
    middle = left.astype(BF16)
    low = (left - middle.astype(F32)).astype(BF16)
    return high, middle, low


def pack_kernel(lay, table, w_in, w_up, w_down, w_head, gains, out):
    for name, ref in (("in", w_in), ("up", w_up), ("down", w_down), ("table", table)):
        low, high = lay.spots[name]
        out[low:high, :] = ref[0].astype(BF16)
    low, high = lay.spots["head"]
    pieces = [piece.astype(F32) for piece in split_three(gains[0])]
    out[low:high, :] = lay.with_tail(w_head[:, 0, :], *pieces).astype(BF16)
    if lay.rows > lay.used:
        out[lay.used :, :] = jnp.zeros((lay.rows - lay.used, lay.width), BF16)


def row_sum(value):
    return jnp.sum(value, axis=-1, keepdims=True)


def interleave(streams, matmul_delay=220, vector_delay=60):
    clock = {"M": 0.0, "V": 0.0}
    live = []
    for rank, stream in enumerate(streams):
        live.append([stream, rank, next(stream), 0.0])
    while live:
        best = min(live, key=lambda entry: (max(clock[entry[2][0]], entry[3]), entry[1]))
        unit, cost = best[2]
        begin = max(clock[unit], best[3])
        clock[unit] = begin + cost
        best[3] = begin + cost + (matmul_delay if unit == "M" else vector_delay)
        best[2] = next(best[0], None)
        if best[2] is None:
            live.remove(best)


def in_turn(*streams):
    for stream in streams:
        yield from stream


def towers_kernel(lay, steps, chunk, which, latent, codes, targets, valid, whole_valid, mine, theirs,
                  keep, send, ends_mine, ends_send,
                  w_cat, w_up, w_down, w_head, gains,
                  g_cat, g_up, g_down, g_head, g_gain,
                  meta, picks, low_state, unit_one, slope_one, unit_two, slope_two, active_now, normed_now, active, normed,
                  scale_one, scale_two, head_part, turned, turned_pick, logits_all, logit_grads, pre_pair, back):
    branch_grads = (low_state.at[0], low_state.at[1])
    inner_grads = (active_now, normed_now)
    pre_grads = (pre_pair.at[0], pre_pair.at[1])
    rows, width = latent.shape
    wide = lay.wide
    part = 1.0 / width
    section = which[0]
    def cut(size):
        return [slice(at, at + size) for at in range(0, rows, size)]

    chunks_one, chunks_two, chunks_head, chunks_back, chunks_copy = (
        cut(size) for size in (CHUNK_ONE, CHUNK_TWO, CHUNK_HEAD, CHUNK_BACK, CHUNK_COPY)
    )

    @pl.when(pl.program_id(0) == 0)
    def start():
        for ref in (g_cat, g_up, g_down, g_head, g_gain):
            ref[...] = jnp.zeros_like(ref)
        for packed, slot in ((mine, section), (theirs, 1 - section)):
            for name, ref in (("up", w_up), ("down", w_down)):
                low, high = lay.spots[name]
                ref[slot] = packed[low:high, :]
            low, high = lay.spots["in"]
            w_cat[slot, :width] = packed[low:high, :]
            low, high = lay.spots["table"]
            w_cat[slot, width : width + lay.codes] = packed[low:high, :]
            w_cat[slot, width + lay.codes :] = jnp.zeros((LANES - lay.codes, width), BF16)
            low, high = lay.spots["head"]
            w_head[slot] = jnp.zeros((wide, width), BF16)
            w_head[slot, : high - low] = packed[low:high, :]
            start_tail = (lay.tail - low) // TILE * TILE
            block = packed[low + start_tail : high, :].astype(F32)
            at = lay.tail - low - start_tail
            gains[slot] = block[at : at + 2] + block[at + 2 : at + 4] + block[at + 4 : at + 6]
            row = lax.broadcasted_iota(jnp.int32, block.shape, 0)
            w_head[slot, start_tail : high - low] = jnp.where(row < at, block, 0.0).astype(BF16)

    lane = lax.broadcasted_iota(jnp.int32, (rows, LANES), 1)
    upright = lax.broadcasted_iota(jnp.int32, (lay.codes, rows), 0)
    for step in range(steps):
        alive = valid[step : step + 1, :]
        line = [codes[step, tower : tower + 1, :] for tower in range(2)]
        line += [jnp.where(alive > 0, targets[step, tower : tower + 1, :], -1) for tower in range(2)]
        columns = jnp.concatenate(line + [jnp.zeros((4, rows), jnp.int32)], axis=0).T
        meta[step] = columns
        for tower in range(2):
            turned_pick[2 * step + tower] = (line[tower] == upright).astype(F32).astype(BF16)
            picks[2 * step + tower] = (columns[:, tower : tower + 1] == lane).astype(F32).astype(BF16)
    low_state[0, :rows] = latent[...]
    turned[0] = latent[...].T

    def forward(step, tower):
        at = 2 * step + tower
        yield "m1"
        pre = dot(picks[at], w_cat[tower, width:]) + dot(low_state[tower, :rows], w_cat[tower, :width])
        for where in chunks_one:
            yield "v1"
            unit, scale = normalise(pre[where])
            unit_one[at, where, :] = unit
            scale_one[at, where, :] = jnp.broadcast_to(scale, (CHUNK_ONE, LANES))
            hidden, slope = gelu_and_slope(unit * gains[tower, 0:1, :])
            slope_one[at, where, :] = slope
            head_part[at, where, :] = hidden
            unit, scale = normalise(hidden)
            unit_two[at, where, :] = unit
            scale_two[at, where, :] = jnp.broadcast_to(scale, (CHUNK_ONE, LANES))
            normed_now[where, :] = (unit * gains[tower, 1:2, :]).astype(BF16)
        yield "m2"
        inner = dot(normed_now[:rows, :], w_up[tower])
        normed[at] = normed_now[:rows, :].T
        for where in chunks_two:
            yield "v2"
            result, slope = gelu_and_slope(inner[where])
            slope_two[at, where, :] = slope
            active_now[where, :] = result.astype(BF16)
        yield "m3"
        branch = dot(active_now[:rows, :], w_down[tower])
        active[at] = active_now[:rows, :].T
        for where in chunks_two:
            yield "v3"
            state = head_part[at, where, :] + branch[where]
            low_state[1 - tower, where, :] = state.astype(BF16)
            ends_mine[where, :] = state
        yield "t"
        turned[at + 1] = low_state[1 - tower, :rows].T

    def hold_logits(tower, at, row):
        spot = pl.multiple_of(rows + 8 * section, 8)
        logits_all[tower, pl.ds(spot, 8), :LANES] = at[row : row + 8, :LANES].astype(F32)

    def hold_low(ref, slot, at, row):
        spot = pl.multiple_of(rows + TILE * section, TILE)
        ref[slot, pl.ds(spot, TILE), :LANES] = at[row : row + TILE, :LANES].astype(BF16)

    column = lax.broadcasted_iota(jnp.int32, (1, wide), 1)
    whole_lanes = wide - LANES
    inside = lax.broadcasted_iota(jnp.int32, (1, LANES), 1) < lay.bins - whole_lanes

    def head_logits(step, tower):
        yield "M", 5 * rows / 8
        logits = dot_right_t(low_state[1 - tower, :rows], w_head[tower])
        for where in chunks_copy:
            yield "V", 1
            logits_all[tower, where, :] = logits[where]

    def head_softmax(step, tower):
        for where in chunks_head:
            yield "V", 14 * 1
            some = logits_all[tower, where, :]
            some = jnp.concatenate(
                [some[:, :whole_lanes], jnp.where(inside, some[:, whole_lanes:], -1e30)], axis=1
            )
            goal = meta[step, where, 2 + tower : 3 + tower]
            raised = jnp.exp(some - jnp.max(some, axis=-1, keepdims=True))
            ratio = jnp.where(goal >= 0, 1.0, 0.0) / row_sum(raised)
            logit_grads[tower, where, :] = (raised * ratio - jnp.where(column == goal, 1.0, 0.0)).astype(BF16)

    def head_products(step, tower):
        at = 2 * step + tower
        yield "M", 5 * rows / 8
        pulled = dot(logit_grads[tower, :rows], w_head[tower])
        for where in chunks_copy:
            yield "V", 1
            head_part[at, where, :] = pulled[where]
        yield "M", 5 * rows / 8
        some = dot(turned[at + 1], logit_grads[tower, :rows])
        yield "V", 80
        g_head[tower] += some

    def tick(step, tower, stages="flsp"):
        at = 2 * step + tower
        count, later = len(chunks_one), len(chunks_two)
        streams = {}
        if "f" in stages:
            streams["f"] = forward(step, tower)
        if "s" in stages:
            streams["s"] = head_softmax(step - 1, tower)
        if "l" in stages:
            streams["l"] = head_logits(step - 1 + tower, 1 - tower)
        if "p" in stages:
            streams["p"] = head_products(step - 2 + tower, 1 - tower)
        for stream in streams.values():
            next(stream)

        def go(name, pieces=1):
            for _ in range(pieces):
                if name in streams:
                    next(streams[name], None)

        if "f" not in stages:
            for name in "spl":
                go(name, 100)
            return
        first, second = FIRST, SECOND
        go("f")
        go("s", first)
        go("f", HOLD_AT)
        if "p" in stages:
            hold_low(logit_grads, 1 - tower, unit_one.at[at], 0)
        if "l" in stages:
            hold_low(low_state, tower, unit_one.at[at], 0)
        if LOGITS_FIRST:
            go("l", 100)
        for turn in range(HOLD_AT, count):
            go("f")
            if turn % 2 == 1:
                go("p")
                go("l")
        go("p", 100)
        go("l", 100)
        if "s" in stages:
            hold_logits(tower, unit_two.at[at], rows - 8)
        go("f")
        go("s", second)
        go("f", later)
        if "s" in stages:
            hold_logits(tower, slope_two.at[at], rows - 8)
        go("f")
        go("s", 100)
        go("f", 100)

    def forward_step(step, carry):
        tick(step, 0)
        tick(step, 1)
        return carry

    tick(0, 0, "f")
    tick(0, 1, "fl")
    tick(1, 0, "fls")
    tick(1, 1)
    lax.fori_loop(2, steps, forward_step, 0)
    tick(steps, 0, "lsp")
    tick(steps, 1, "sp")
    tick(steps + 1, 0, "p")

    def both(value):
        return jnp.concatenate([value] * (width // LANES), axis=1)

    def backward(step, tower):
        at = 2 * step + tower
        for where in chunks_back:
            yield "V", 1
            state_grad = head_part[at, where, :] + back[where, :].astype(F32)
            head_part[at, where, :] = state_grad
            branch_grads[tower][where, :] = state_grad.astype(BF16)
        yield "M", rows / 4
        active_grad = dot_right_t(branch_grads[tower][:rows, :], w_down[tower])
        for where in chunks_back:
            yield "V", 1
            inner_grads[tower][where, :] = (active_grad[where] * slope_two[at, where, :]).astype(BF16)
        yield "M", rows / 4
        normed_grad = dot_right_t(inner_grads[tower][:rows, :], w_up[tower])
        for where in chunks_back:
            yield "V", 12.5 * 1
            unit = unit_two[at, where, :]
            scaled = normed_grad[where] * gains[tower, 1:2, :]
            first = row_sum(scaled) * part
            second = row_sum(scaled * unit) * part
            hidden_grad = head_part[at, where, :] + (scaled - first - unit * second) * both(scale_two[at, where, :])
            out_grad = hidden_grad * slope_one[at, where, :]
            unit = unit_one[at, where, :]
            product = out_grad * unit
            g_gain[tower] += jnp.sum(product.reshape(CHUNK_BACK // 8, 8, width), axis=0)
            gain = gains[tower, 0:1, :]
            scaled = out_grad * gain
            first = row_sum(scaled) * part
            second = row_sum(product * gain) * part
            pre_grads[tower][where, :] = (
                (scaled - first - unit * second) * both(scale_one[at, where, :])
            ).astype(BF16)
        yield "M", rows / 4
        input_grad = dot_right_t(pre_grads[tower][:rows, :], w_cat[tower, :width])
        for where in chunks_back:
            yield "V", 0.5 * 1
            back[where, :] = input_grad[where].astype(BF16)

    def weight_grads(step, tower):
        at = 2 * step + tower
        for left, right, total in ((active, branch_grads, g_down), (normed, inner_grads, g_up)):
            yield "M", rows / 4 + 20
            some = dot(left[at], right[tower][:rows, :])
            yield "V", 32
            total[tower] += some
        yield "M", rows / 4 + 40
        some = dot(jnp.concatenate([turned[at], turned_pick[at]], axis=0), pre_grads[tower][:rows, :])
        yield "V", 36
        g_cat[tower] += some

    back[...] = jnp.zeros_like(back)
    for ref in (branch_grads[0], inner_grads[0], pre_grads[0]):
        ref[:rows, :] = jnp.zeros((rows, width), BF16)

    def back_tick(step, tower, before):
        at = 2 * step + tower
        chain = backward(step, tower)
        next(chain)
        products = weight_grads(before, 1 - tower)
        next(products)
        for _ in range(2 * len(chunks_back) + 2 + BACK_FIRST):
            next(chain)
        spot = pl.multiple_of(rows + TILE * section, TILE)
        for ref in (branch_grads, inner_grads, pre_grads):
            ref[1 - tower][pl.ds(spot, TILE), :LANES] = unit_two[at, :TILE, :LANES].astype(BF16)
        for _ in products:
            next(chain, None)
        for _ in chain:
            pass

    def backward_step(turn, carry):
        step = steps - 1 - turn
        back_tick(step, 1, jnp.minimum(step + 1, steps - 1))
        back_tick(step, 0, step)
        return carry

    lax.fori_loop(0, steps, backward_step, 0)
    interleave([weight_grads(0, 0)])
    first = back[...].astype(F32)
    last = ends_mine[...]
    is_first = section == 0
    ends_mine[...] = jnp.where(is_first, first, last)
    ends_send[...] = jnp.where(is_first, last, first).astype(BF16)

    @pl.when(pl.program_id(0) == pl.num_programs(0) - 1)
    def finish():
        count = jnp.sum(whole_valid[...].astype(F32), axis=(0, 1), keepdims=True).astype(jnp.int32)
        spot = lax.broadcasted_iota(jnp.int32, (1, width), 1)
        bits = jnp.where(spot < BITS, (count >> jnp.minimum(spot, BITS)) & 1, 0).astype(F32)
        for packed, slot in ((keep, section), (send, 1 - section)):
            kind = packed.dtype
            for name, value in (
                ("in", g_cat[slot, :width]),
                ("up", g_up[slot]),
                ("down", g_down[slot]),
                ("table", g_cat[slot, width : width + lay.codes]),
            ):
                low, high = lay.spots[name]
                packed[low:high, :] = value.astype(kind)
            in_gain = jnp.sum(g_gain[slot], axis=0, keepdims=True)
            pulled = jnp.sum((w_up[slot].astype(F32) * g_up[slot]).T, axis=0, keepdims=True)
            block_gain = pulled / gains[slot, 1:2, :]
            own = bits if packed is keep else jnp.zeros_like(bits)
            low, high = lay.spots["head"]
            packed[low:high, :] = lay.with_tail(g_head[slot].T, in_gain, block_gain, own).astype(kind)
            if lay.rows > lay.used:
                packed[lay.used :, :] = jnp.zeros((lay.rows - lay.used, width), kind)


def update_kernel(lay, parts, which, *refs):
    pieces, ins, outs = refs[:parts], refs[parts : parts + 18], refs[parts + 18 : parts + 42]
    stages, total, done = refs[parts + 42 : parts + 66], refs[-2], refs[-1]
    rows = pieces[0].shape[0]
    for turn, piece in enumerate(pieces):
        low = pl.multiple_of((which[0] ^ turn) * rows, TILE)
        total[pl.ds(low, rows), :] = piece[...]
    low = lay.tail // TILE * TILE
    tail = total[low : lay.spots["head"][1], :].astype(F32)[lay.tail - low : lay.tail - low + 3]
    lane = lax.broadcasted_iota(jnp.int32, (1, lay.width), 1)
    place = jnp.where(lane < BITS, (1 << jnp.minimum(lane, BITS)).astype(F32), 0.0)
    count = jnp.sum(tail[2:3] * place, axis=-1, keepdims=True)
    scale = GRAD_SCALE * lax.rsqrt(count)
    copies = []

    def new(at, spot, copy_spot, parts_of, grad):
        weight, moment, average = ins[3 * at : 3 * at + 3]
        step_grad = grad.astype(F32) * scale
        new_moment = MOMENTUM * moment[spot] + step_grad
        new_weight = weight[spot] - RATE * (step_grad + MOMENTUM * new_moment)
        new_average = AVERAGE * average[spot] + (1.0 - AVERAGE) * new_weight
        news = (new_moment, new_average, new_weight, new_weight.astype(BF16))
        for kind, value in enumerate(news):
            stage, out = stages[4 * at + kind], outs[4 * at + kind]
            stage[copy_spot if kind == 3 else spot] = value
            piece = parts_of[1 if kind == 3 else 0]
            copies.append(pltpu.make_async_copy(stage.at[piece], out.at[piece], done.at[len(copies)]))
            copies[-1].start()

    everything = (slice(None),)
    low, high = lay.spots["head"]
    step = -(-lay.bins // (STEPS * TILE)) * TILE
    for begin in range(0, lay.bins, step):
        end = min(begin + step, lay.bins)
        cover = min(-(-end // TILE) * TILE, high - low)
        grad = total[low + begin : low + cover, :].astype(F32)[: end - begin]
        new(5, (slice(begin, end), 0), (0, slice(begin, end)),
            ((slice(begin, end),), (slice(None), slice(begin, end))), grad)
    for at, name in ((1, "in"), (3, "up"), (4, "down"), (0, "table")):
        low, high = lay.spots[name]
        new(at, (0,), (0,), (everything, everything), total[low:high, :])
    new(2, (0,), (0,), (everything, everything), tail[0:2])
    for copy in copies:
        copy.wait()


def swap(value):
    return lax.ppermute(value, "section", [(0, 1), (1, 0)])


def across(array, mask, length):
    return lax.ppermute(array, "dp", [(i, i ^ mask) for i in range(length)])


def on_device(block, chunk, length, latent, codes, targets, valid, *weights):
    section = lax.axis_index("section").astype(jnp.int32)
    index = lax.axis_index("dp").astype(jnp.int32)
    rows, width = latent.shape
    steps = codes.shape[1]
    own_rows = rows // 2
    block = min(block, own_rows)
    blocks = own_rows // block
    bins = weights[15].shape[2]
    weights = weights[:15] + tuple(jnp.transpose(array, (2, 0, 1)) for array in weights[15:])
    codes, targets = jnp.swapaxes(codes, 0, 1), jnp.swapaxes(targets, 0, 1)
    table, w_in, gains, w_up, w_down, w_head = weights[0::3]
    lay = Layout(table.shape[1], width, bins)
    packed_shape = (lay.rows, width)
    roomy = pltpu.CompilerParams(vmem_limit_bytes=VMEM)
    mine = pl.pallas_call(
        functools.partial(pack_kernel, lay),
        out_shape=jax.ShapeDtypeStruct(packed_shape, BF16),
        compiler_params=roomy,
        name="pack",
    )(table, w_in, w_up, w_down, w_head, gains)
    theirs = swap(mine)

    def spec_rows(*shape):
        return pl.BlockSpec(shape, lambda i, which: (which[0] * blocks + i,) + (0,) * (len(shape) - 1))

    def spec_lanes(*shape):
        return pl.BlockSpec(shape, lambda i, which: (0,) * (len(shape) - 1) + (which[0] * blocks + i,))

    def spec_whole(*shape):
        return pl.BlockSpec(shape, lambda i, which: (0,) * len(shape))

    def spec_once(*shape):
        return pl.BlockSpec(shape, lambda i, which: (0,) * len(shape), pipeline_mode=pl.Buffered(1))

    def spec_out(*shape):
        return pl.BlockSpec(shape, lambda i, which: (i, 0))

    ticks = 2 * steps
    square = (2, width, width)
    per_tick = (ticks, block, width)
    narrow = (ticks, block, LANES)
    keep, send, ends_mine, ends_send = pl.pallas_call(
        functools.partial(towers_kernel, lay, steps, chunk),
        grid_spec=pltpu.PrefetchScalarGridSpec(
            num_scalar_prefetch=1,
            grid=(blocks,),
            in_specs=[
                spec_rows(block, width),
                spec_lanes(steps, 2, block),
                spec_lanes(steps, 2, block),
                spec_lanes(steps, block),
                spec_whole(steps, rows),
                spec_once(*packed_shape),
                spec_once(*packed_shape),
            ],
            out_specs=[
                spec_once(*packed_shape),
                spec_once(*packed_shape),
                spec_out(block, width),
                spec_out(block, width),
            ],
            scratch_shapes=[
                pltpu.VMEM((2, width + LANES, width), BF16),
                pltpu.VMEM(square, BF16),
                pltpu.VMEM(square, BF16),
                pltpu.VMEM((2, lay.wide, width), BF16),
                pltpu.VMEM((2, 2, width), F32),
                pltpu.VMEM((2, width + lay.codes, width), F32),
                pltpu.VMEM(square, F32),
                pltpu.VMEM(square, F32),
                pltpu.VMEM((2, width, lay.wide), F32),
                pltpu.VMEM((2, 8, width), F32),
                pltpu.VMEM((steps, block, 8), jnp.int32),
                pltpu.VMEM((ticks, block, LANES), BF16),
                pltpu.VMEM((2, block + 2 * TILE, width), BF16),
                pltpu.VMEM(per_tick, F32),
                pltpu.VMEM(per_tick, F32),
                pltpu.VMEM(per_tick, F32),
                pltpu.VMEM(per_tick, F32),
                pltpu.VMEM((block + 2 * TILE, width), BF16),
                pltpu.VMEM((block + 2 * TILE, width), BF16),
                pltpu.VMEM((ticks, width, block), BF16),
                pltpu.VMEM((ticks, width, block), BF16),
                pltpu.VMEM(narrow, F32),
                pltpu.VMEM(narrow, F32),
                pltpu.VMEM(per_tick, F32),
                pltpu.VMEM((ticks + 1, width, block), BF16),
                pltpu.VMEM((ticks, lay.codes, block), BF16),
                pltpu.VMEM((2, block + TILE, lay.wide), F32),
                pltpu.VMEM((2, block + 2 * TILE, lay.wide), BF16),
                pltpu.VMEM((2, block + 2 * TILE, width), BF16),
                pltpu.VMEM((block, width), BF16),
            ],
        ),
        out_shape=[
            jax.ShapeDtypeStruct(packed_shape, BF16),
            jax.ShapeDtypeStruct(packed_shape, BF16),
            jax.ShapeDtypeStruct((own_rows, width), F32),
            jax.ShapeDtypeStruct((own_rows, width), BF16),
        ],
        compiler_params=roomy,
        name="towers",
    )(section[None], latent, codes, targets, valid, valid, mine, theirs)

    parts = min(4, length)
    place = (index % parts)[None]
    in_smem = pl.BlockSpec(memory_space=pltpu.SMEM)

    part_shape = (lay.rows // parts, width)
    both = lax.optimization_barrier(keep.astype(F32)) + swap(send).astype(F32)
    both = lax.optimization_barrier(both.reshape(parts, *part_shape))

    def part_for(mask):
        return lax.dynamic_index_in_dim(both, place[0] ^ mask, 0, keepdims=False)

    own = lax.optimization_barrier(part_for(0))
    others = [part_for(mask).astype(BF16) for mask in range(1, parts)]
    current = own
    for arrived in [across(other, mask, length) for mask, other in enumerate(others, 1)]:
        current = current + arrived.astype(F32)
    current = current.astype(BF16)
    masks = [1 << bit for bit in range(length.bit_length() - 1)][parts.bit_length() - 1 :]
    halved = masks[:1] if len(masks) > 1 else []
    for mask in halved:
        half = current.shape[0] // 2
        upper = (index // mask) % 2 == 1
        sent = jnp.where(upper, current[:half], current[half:])
        kept = jnp.where(upper, current[half:], current[:half])
        current = (kept.astype(F32) + across(sent, mask, length).astype(F32)).astype(BF16)
    for mask in masks[len(halved) :]:
        current = (current.astype(F32) + across(current, mask, length).astype(F32)).astype(BF16)
    for mask in halved:
        upper = (index // mask) % 2 == 1
        found = across(current, mask, length)
        current = jnp.where(upper, jnp.concatenate([found, current]), jnp.concatenate([current, found]))
    pieces = [current] + [across(current, mask, length) for mask in range(1, parts)]

    other = swap(ends_send).astype(F32)
    ends = jnp.where(
        section == 0,
        jnp.concatenate([ends_mine, other]),
        jnp.concatenate([other, ends_mine]),
    )[None]
    news = []
    for at in range(6):
        shape = weights[3 * at].shape
        news += [jax.ShapeDtypeStruct(shape, F32)] * 3
        news.append(jax.ShapeDtypeStruct((1, shape[0], width) if at == 5 else shape, BF16))
    copy_count = 4 * (5 + -(-bins // (-(-bins // (STEPS * TILE)) * TILE)))
    updated = pl.pallas_call(
        functools.partial(update_kernel, lay, parts),
        in_specs=[in_smem] + [pl.BlockSpec(memory_space=pltpu.VMEM)] * (parts + 18),
        out_specs=[pl.BlockSpec(memory_space=pl.ANY)] * 24,
        out_shape=news,
        scratch_shapes=[pltpu.VMEM(new.shape, new.dtype) for new in news]
        + [pltpu.VMEM(packed_shape, BF16), pltpu.SemaphoreType.DMA((copy_count,))],
        compiler_params=pltpu.CompilerParams(vmem_limit_bytes=SMALL),
        name="update",
    )(place, *pieces, *weights)
    table_out, in_out, gain_out, up_out, down_out, head_out = (updated[4 * at : 4 * at + 4] for at in range(6))
    head_out = [jnp.transpose(array, (1, 2, 0)) for array in head_out[:3]] + [jnp.swapaxes(head_out[3], 1, 2)]
    return (ends, *table_out, *in_out, *gain_out, *up_out, *down_out, *head_out)


def solution(mesh):
    by_section = P("section", None, None)
    in_specs = (P("dp", None), P(None, None, "dp"), P(None, None, "dp"), P(None, "dp")) + (by_section,) * 18
    out_specs = (P("section", "dp", None),) + (by_section,) * 24
    return jax.shard_map(
        functools.partial(on_device, 512, 64, mesh.shape["dp"]),
        mesh=mesh,
        in_specs=in_specs,
        out_specs=out_specs,
        check_vma=False,
    )
```

```python
import functools
import math

import jax
import jax.numpy as jnp
from jax import lax
from jax.experimental import pallas as pl
from jax.experimental.pallas import tpu as pltpu
from jax.sharding import PartitionSpec as P

EPS = 1e-05
MOMENTUM = 0.5
AVERAGE = 0.9
RATE = 0.2
GRAD_SCALE = 4.0
GELU_LINE = 0.7978845608028654
GELU_CUBE = 0.7978845608028654 * 0.044715

BF16 = jnp.bfloat16
F32 = jnp.float32
LANES = 128
TILE = 16
BITS = 24
FIRST, SECOND, HOLD_AT, BACK_FIRST = 4, 4, 1, 0
CHUNK_ONE, CHUNK_TWO, CHUNK_HEAD, CHUNK_BACK, CHUNK_COPY = 64, 64, 64, 64, 64
LOGITS_FIRST = False
SPARE = 7
STEPS = 4
SMALL = 16 * 1024 * 1024
VMEM = 63 * 1024 * 1024


def dot(left, right):
    return jnp.dot(left, right, preferred_element_type=F32)


def dot_right_t(left, right):
    return lax.dot_general(left, right, (((1,), (1,)), ((), ())), preferred_element_type=F32)


def dot_left_t(left, right):
    return lax.dot_general(left, right, (((0,), (0,)), ((), ())), preferred_element_type=F32)


def gelu_and_slope(half):
    square = half * half
    bend = jnp.tanh(half * (2 * GELU_LINE + (8 * GELU_CUBE) * square))
    raised = 1.0 + bend
    result = half * raised
    return result, raised + result * (1.0 - bend) * (2 * GELU_LINE + (24 * GELU_CUBE) * square)


def normalise(value):
    width = value.shape[-1]
    centered = value - jnp.sum(value, axis=-1, keepdims=True) * (1.0 / width)
    scale = lax.rsqrt(jnp.sum(centered * centered, axis=-1, keepdims=True) + EPS * width)
    return centered * scale, scale


class Layout:
    def __init__(self, codes, width, bins):
        self.codes, self.width, self.bins = codes, width, bins
        self.wide = -(-bins // LANES) * LANES
        spots, at = {}, 0
        sizes = (("in", width), ("up", width), ("down", width), ("head", bins + SPARE), ("table", codes))
        for name, rows in sizes:
            spots[name] = (at, at + -(-rows // TILE) * TILE)
            at = spots[name][1]
        spots["table"] = (spots["table"][0], spots["table"][0] + codes)
        self.tail = spots["head"][0] + bins
        self.spots = spots
        self.used = at
        self.rows = -(-at // (8 * TILE)) * (8 * TILE)

    def with_tail(self, head, *extra):
        low, high = self.spots["head"]
        left = high - low - self.bins - sum(rows.shape[0] for rows in extra)
        return jnp.concatenate([head[: self.bins], *extra, jnp.zeros((left, self.width), F32)], axis=0)


def split_three(value):
    high = value.astype(BF16)
    left = value - high.astype(F32)
    middle = left.astype(BF16)
    low = (left - middle.astype(F32)).astype(BF16)
    return high, middle, low


def pack_kernel(lay, table, w_in, w_up, w_down, w_head, gains, out):
    for name, ref in (("in", w_in), ("up", w_up), ("down", w_down), ("table", table)):
        low, high = lay.spots[name]
        out[low:high, :] = ref[0].astype(BF16)
    low, high = lay.spots["head"]
    pieces = [piece.astype(F32) for piece in split_three(gains[0])]
    out[low:high, :] = lay.with_tail(w_head[:, 0, :], *pieces).astype(BF16)
    if lay.rows > lay.used:
        out[lay.used :, :] = jnp.zeros((lay.rows - lay.used, lay.width), BF16)


def row_sum(value):
    return jnp.sum(value, axis=-1, keepdims=True)


def interleave(streams, matmul_delay=220, vector_delay=60):
    clock = {"M": 0.0, "V": 0.0}
    live = []
    for rank, stream in enumerate(streams):
        live.append([stream, rank, next(stream), 0.0])
    while live:
        best = min(live, key=lambda entry: (max(clock[entry[2][0]], entry[3]), entry[1]))
        unit, cost = best[2]
        begin = max(clock[unit], best[3])
        clock[unit] = begin + cost
        best[3] = begin + cost + (matmul_delay if unit == "M" else vector_delay)
        best[2] = next(best[0], None)
        if best[2] is None:
            live.remove(best)


def in_turn(*streams):
    for stream in streams:
        yield from stream


def towers_kernel(lay, steps, chunk, which, latent, codes, targets, valid, whole_valid, mine, theirs,
                  keep, send, ends_mine, ends_send,
                  w_cat, w_up, w_down, w_head, gains,
                  g_cat, g_up, g_down, g_head, g_gain,
                  meta, picks, low_state, unit_one, slope_one, unit_two, slope_two, active_now, normed_now, active, normed,
                  scale_one, scale_two, head_part, turned, turned_pick, logits_all, logit_grads, pre_pair, back):
    branch_grads = (low_state.at[0], low_state.at[1])
    inner_grads = (active_now, normed_now)
    pre_grads = (pre_pair.at[0], pre_pair.at[1])
    rows, width = latent.shape
    wide = lay.wide
    part = 1.0 / width
    root = math.sqrt(width)
    section = which[0]
    def cut(size):
        return [slice(at, at + size) for at in range(0, rows, size)]

    chunks_one, chunks_two, chunks_head, chunks_back, chunks_copy = (
        cut(size) for size in (CHUNK_ONE, CHUNK_TWO, CHUNK_HEAD, CHUNK_BACK, CHUNK_COPY)
    )

    @pl.when(pl.program_id(0) == 0)
    def start():
        for ref in (g_cat, g_up, g_down, g_head, g_gain):
            ref[...] = jnp.zeros_like(ref)
        for packed, slot in ((mine, section), (theirs, 1 - section)):
            for name, ref in (("up", w_up), ("down", w_down)):
                low, high = lay.spots[name]
                ref[slot] = (packed[low:high, :].astype(F32) * (0.5 if name == "up" else 1.0)).astype(BF16)
            low, high = lay.spots["in"]
            w_cat[slot, :width] = packed[low:high, :]
            low, high = lay.spots["table"]
            w_cat[slot, width : width + lay.codes] = packed[low:high, :]
            w_cat[slot, width + lay.codes :] = jnp.zeros((LANES - lay.codes, width), BF16)
            low, high = lay.spots["head"]
            w_head[slot] = jnp.zeros((wide, width), BF16)
            w_head[slot, : high - low] = packed[low:high, :]
            start_tail = (lay.tail - low) // TILE * TILE
            block = packed[low + start_tail : high, :].astype(F32)
            at = lay.tail - low - start_tail
            pair = block[at : at + 2] + block[at + 2 : at + 4] + block[at + 4 : at + 6]
            gains[slot] = pair * jnp.where(lax.broadcasted_iota(jnp.int32, pair.shape, 0) == 0, root / 2, root)
            row = lax.broadcasted_iota(jnp.int32, block.shape, 0)
            w_head[slot, start_tail : high - low] = jnp.where(row < at, block, 0.0).astype(BF16)

    lane = lax.broadcasted_iota(jnp.int32, (rows, LANES), 1)
    upright = lax.broadcasted_iota(jnp.int32, (lay.codes, rows), 0)
    for step in range(steps):
        alive = valid[step : step + 1, :]
        line = [codes[step, tower : tower + 1, :] for tower in range(2)]
        line += [jnp.where(alive > 0, targets[step, tower : tower + 1, :], -1) for tower in range(2)]
        columns = jnp.concatenate(line + [jnp.zeros((4, rows), jnp.int32)], axis=0).T
        meta[step] = columns
        for tower in range(2):
            turned_pick[2 * step + tower] = (line[tower] == upright).astype(F32).astype(BF16)
            picks[2 * step + tower] = (columns[:, tower : tower + 1] == lane).astype(F32).astype(BF16)
    low_state[0, :rows] = latent[...]
    turned[0] = latent[...].T

    def forward(step, tower):
        at = 2 * step + tower
        yield "m1"
        pre = dot(picks[at], w_cat[tower, width:]) + dot(low_state[tower, :rows], w_cat[tower, :width])
        for where in chunks_one:
            yield "v1"
            unit, scale = normalise(pre[where])
            unit_one[at, where, :] = unit
            scale_one[at, where, :] = jnp.broadcast_to(scale, (CHUNK_ONE, LANES))
            hidden, slope = gelu_and_slope(unit * gains[tower, 0:1, :])
            slope_one[at, where, :] = slope
            head_part[at, where, :] = hidden
            unit, scale = normalise(hidden)
            unit_two[at, where, :] = unit
            scale_two[at, where, :] = jnp.broadcast_to(scale, (CHUNK_ONE, LANES))
            normed_now[where, :] = (unit * gains[tower, 1:2, :]).astype(BF16)
        yield "m2"
        inner = dot(normed_now[:rows, :], w_up[tower])
        normed[at] = normed_now[:rows, :].T
        for where in chunks_two:
            yield "v2"
            result, slope = gelu_and_slope(inner[where])
            slope_two[at, where, :] = slope
            active_now[where, :] = result.astype(BF16)
        yield "m3"
        branch = dot(active_now[:rows, :], w_down[tower])
        active[at] = active_now[:rows, :].T
        for where in chunks_two:
            yield "v3"
            state = head_part[at, where, :] + branch[where]
            low_state[1 - tower, where, :] = state.astype(BF16)
            ends_mine[where, :] = state
        yield "t"
        turned[at + 1] = low_state[1 - tower, :rows].T

    def hold_logits(tower, at, row):
        spot = pl.multiple_of(rows + 8 * section, 8)
        logits_all[tower, pl.ds(spot, 8), :LANES] = at[row : row + 8, :LANES].astype(F32)

    def hold_low(ref, slot, at, row):
        spot = pl.multiple_of(rows + TILE * section, TILE)
        ref[slot, pl.ds(spot, TILE), :LANES] = at[row : row + TILE, :LANES].astype(BF16)

    column = lax.broadcasted_iota(jnp.int32, (1, wide), 1)
    whole_lanes = wide - LANES
    inside = lax.broadcasted_iota(jnp.int32, (1, LANES), 1) < lay.bins - whole_lanes

    def head_logits(step, tower):
        yield "M", 5 * rows / 8
        logits = dot_right_t(low_state[1 - tower, :rows], w_head[tower])
        for where in chunks_copy:
            yield "V", 1
            logits_all[tower, where, :] = logits[where]

    def head_softmax(step, tower):
        for where in chunks_head:
            yield "V", 14 * 1
            some = logits_all[tower, where, :]
            some = jnp.concatenate(
                [some[:, :whole_lanes], jnp.where(inside, some[:, whole_lanes:], -1e30)], axis=1
            )
            goal = meta[step, where, 2 + tower : 3 + tower]
            raised = jnp.exp(some - jnp.max(some, axis=-1, keepdims=True))
            ratio = jnp.where(goal >= 0, 1.0, 0.0) / row_sum(raised)
            logit_grads[tower, where, :] = (raised * ratio - jnp.where(column == goal, 1.0, 0.0)).astype(BF16)

    def head_products(step, tower):
        at = 2 * step + tower
        yield "M", 5 * rows / 8
        pulled = dot(logit_grads[tower, :rows], w_head[tower])
        for where in chunks_copy:
            yield "V", 1
            head_part[at, where, :] = pulled[where]
        yield "M", 5 * rows / 8
        some = dot(turned[at + 1], logit_grads[tower, :rows])
        yield "V", 80
        g_head[tower] += some

    def tick(step, tower, stages="flsp"):
        at = 2 * step + tower
        count, later = len(chunks_one), len(chunks_two)
        streams = {}
        if "f" in stages:
            streams["f"] = forward(step, tower)
        if "s" in stages:
            streams["s"] = head_softmax(step - 1, tower)
        if "l" in stages:
            streams["l"] = head_logits(step - 1 + tower, 1 - tower)
        if "p" in stages:
            streams["p"] = head_products(step - 2 + tower, 1 - tower)
        for stream in streams.values():
            next(stream)

        def go(name, pieces=1):
            for _ in range(pieces):
                if name in streams:
                    next(streams[name], None)

        if "f" not in stages:
            for name in "spl":
                go(name, 100)
            return
        first, second = FIRST, SECOND
        go("f")
        go("s", first)
        go("f", HOLD_AT)
        if "p" in stages:
            hold_low(logit_grads, 1 - tower, unit_one.at[at], 0)
        if "l" in stages:
            hold_low(low_state, tower, unit_one.at[at], 0)
        if LOGITS_FIRST:
            go("l", 100)
        for turn in range(HOLD_AT, count):
            go("f")
            if turn % 2 == 1:
                go("p")
                go("l")
        go("p", 100)
        go("l", 100)
        if "s" in stages:
            hold_logits(tower, unit_two.at[at], rows - 8)
        go("f")
        go("s", second)
        go("f", later)
        if "s" in stages:
            hold_logits(tower, slope_two.at[at], rows - 8)
        go("f")
        go("s", 100)
        go("f", 100)

    def forward_step(step, carry):
        tick(step, 0)
        tick(step, 1)
        return carry

    tick(0, 0, "f")
    tick(0, 1, "fl")
    tick(1, 0, "fls")
    tick(1, 1)
    lax.fori_loop(2, steps, forward_step, 0)
    tick(steps, 0, "lsp")
    tick(steps, 1, "sp")
    tick(steps + 1, 0, "p")

    def both(value):
        return jnp.concatenate([value] * (width // LANES), axis=1)

    def backward(step, tower):
        at = 2 * step + tower
        for where in chunks_back:
            yield "V", 1
            state_grad = head_part[at, where, :] + back[where, :].astype(F32)
            head_part[at, where, :] = state_grad
            branch_grads[tower][where, :] = state_grad.astype(BF16)
        yield "M", rows / 4
        active_grad = dot_right_t(branch_grads[tower][:rows, :], w_down[tower])
        for where in chunks_back:
            yield "V", 1
            inner_grads[tower][where, :] = (active_grad[where] * slope_two[at, where, :]).astype(BF16)
        yield "M", rows / 4
        normed_grad = dot_right_t(inner_grads[tower][:rows, :], w_up[tower])
        for where in chunks_back:
            yield "V", 12.5 * 1
            unit = unit_two[at, where, :]
            scaled = normed_grad[where] * gains[tower, 1:2, :]
            first = row_sum(scaled) * part
            second = row_sum(scaled * unit)
            hidden_grad = head_part[at, where, :] + (scaled - first - unit * second) * both(scale_two[at, where, :])
            out_grad = hidden_grad * slope_one[at, where, :]
            unit = unit_one[at, where, :]
            product = out_grad * unit
            g_gain[tower] += jnp.sum(product.reshape(CHUNK_BACK // 8, 8, width), axis=0)
            gain = gains[tower, 0:1, :]
            scaled = out_grad * gain
            first = row_sum(scaled) * part
            second = row_sum(product * gain)
            pre_grads[tower][where, :] = (
                (scaled - first - unit * second) * both(scale_one[at, where, :])
            ).astype(BF16)
        yield "M", rows / 4
        input_grad = dot_right_t(pre_grads[tower][:rows, :], w_cat[tower, :width])
        for where in chunks_back:
            yield "V", 0.5 * 1
            back[where, :] = input_grad[where].astype(BF16)

    def weight_grads(step, tower):
        at = 2 * step + tower
        for left, right, total in ((active, branch_grads, g_down), (normed, inner_grads, g_up)):
            yield "M", rows / 4 + 20
            some = dot(left[at], right[tower][:rows, :])
            yield "V", 32
            total[tower] += some
        yield "M", rows / 4 + 40
        some = dot(jnp.concatenate([turned[at], turned_pick[at]], axis=0), pre_grads[tower][:rows, :])
        yield "V", 36
        g_cat[tower] += some

    back[...] = jnp.zeros_like(back)
    for ref in (branch_grads[0], inner_grads[0], pre_grads[0]):
        ref[:rows, :] = jnp.zeros((rows, width), BF16)

    def back_tick(step, tower, before):
        at = 2 * step + tower
        chain = backward(step, tower)
        next(chain)
        products = weight_grads(before, 1 - tower)
        next(products)
        for _ in range(2 * len(chunks_back) + 2 + BACK_FIRST):
            next(chain)
        spot = pl.multiple_of(rows + TILE * section, TILE)
        for ref in (branch_grads, inner_grads, pre_grads):
            ref[1 - tower][pl.ds(spot, TILE), :LANES] = unit_two[at, :TILE, :LANES].astype(BF16)
        for _ in products:
            next(chain, None)
        for _ in chain:
            pass

    def backward_step(turn, carry):
        step = steps - 1 - turn
        back_tick(step, 1, jnp.minimum(step + 1, steps - 1))
        back_tick(step, 0, step)
        return carry

    lax.fori_loop(0, steps, backward_step, 0)
    interleave([weight_grads(0, 0)])
    first = back[...].astype(F32)
    last = ends_mine[...]
    is_first = section == 0
    ends_mine[...] = jnp.where(is_first, first, last)
    ends_send[...] = jnp.where(is_first, last, first).astype(BF16)

    @pl.when(pl.program_id(0) == pl.num_programs(0) - 1)
    def finish():
        count = jnp.sum(whole_valid[...].astype(F32), axis=(0, 1), keepdims=True).astype(jnp.int32)
        spot = lax.broadcasted_iota(jnp.int32, (1, width), 1)
        bits = jnp.where(spot < BITS, (count >> jnp.minimum(spot, BITS)) & 1, 0).astype(F32)
        for packed, slot in ((keep, section), (send, 1 - section)):
            kind = packed.dtype
            for name, value in (
                ("in", g_cat[slot, :width]),
                ("up", g_up[slot] * 0.5),
                ("down", g_down[slot]),
                ("table", g_cat[slot, width : width + lay.codes]),
            ):
                low, high = lay.spots[name]
                packed[low:high, :] = value.astype(kind)
            in_gain = jnp.sum(g_gain[slot], axis=0, keepdims=True) * (root / 2)
            pulled = jnp.sum((w_up[slot].astype(F32) * g_up[slot]).T, axis=0, keepdims=True)
            block_gain = pulled * root / gains[slot, 1:2, :]
            own = bits if packed is keep else jnp.zeros_like(bits)
            low, high = lay.spots["head"]
            packed[low:high, :] = lay.with_tail(g_head[slot].T, in_gain, block_gain, own).astype(kind)
            if lay.rows > lay.used:
                packed[lay.used :, :] = jnp.zeros((lay.rows - lay.used, width), kind)


def update_kernel(lay, parts, which, *refs):
    pieces, ins, outs = refs[:parts], refs[parts : parts + 18], refs[parts + 18 : parts + 42]
    stages, total, done = refs[parts + 42 : parts + 66], refs[-2], refs[-1]
    rows = pieces[0].shape[0]
    for turn, piece in enumerate(pieces):
        low = pl.multiple_of((which[0] ^ turn) * rows, TILE)
        total[pl.ds(low, rows), :] = piece[...]
    low = lay.tail // TILE * TILE
    tail = total[low : lay.spots["head"][1], :].astype(F32)[lay.tail - low : lay.tail - low + 3]
    lane = lax.broadcasted_iota(jnp.int32, (1, lay.width), 1)
    place = jnp.where(lane < BITS, (1 << jnp.minimum(lane, BITS)).astype(F32), 0.0)
    count = jnp.sum(tail[2:3] * place, axis=-1, keepdims=True)
    scale = GRAD_SCALE * lax.rsqrt(count)
    copies = []

    def new(at, spot, copy_spot, parts_of, grad):
        weight, moment, average = ins[3 * at : 3 * at + 3]
        step_grad = grad.astype(F32) * scale
        new_moment = MOMENTUM * moment[spot] + step_grad
        new_weight = weight[spot] - RATE * (step_grad + MOMENTUM * new_moment)
        new_average = AVERAGE * average[spot] + (1.0 - AVERAGE) * new_weight
        news = (new_moment, new_average, new_weight, new_weight.astype(BF16))
        for kind, value in enumerate(news):
            stage, out = stages[4 * at + kind], outs[4 * at + kind]
            stage[copy_spot if kind == 3 else spot] = value
            piece = parts_of[1 if kind == 3 else 0]
            copies.append(pltpu.make_async_copy(stage.at[piece], out.at[piece], done.at[len(copies)]))
            copies[-1].start()

    everything = (slice(None),)
    low, high = lay.spots["head"]
    step = -(-lay.bins // (STEPS * TILE)) * TILE
    for begin in range(0, lay.bins, step):
        end = min(begin + step, lay.bins)
        cover = min(-(-end // TILE) * TILE, high - low)
        grad = total[low + begin : low + cover, :].astype(F32)[: end - begin]
        new(5, (slice(begin, end), 0), (0, slice(begin, end)),
            ((slice(begin, end),), (slice(None), slice(begin, end))), grad)
    for at, name in ((1, "in"), (3, "up"), (4, "down"), (0, "table")):
        low, high = lay.spots[name]
        new(at, (0,), (0,), (everything, everything), total[low:high, :])
    new(2, (0,), (0,), (everything, everything), tail[0:2])
    for copy in copies:
        copy.wait()


def swap(value):
    return lax.ppermute(value, "section", [(0, 1), (1, 0)])


def across(array, mask, length):
    return lax.ppermute(array, "dp", [(i, i ^ mask) for i in range(length)])


def on_device(block, chunk, length, latent, codes, targets, valid, *weights):
    section = lax.axis_index("section").astype(jnp.int32)
    index = lax.axis_index("dp").astype(jnp.int32)
    rows, width = latent.shape
    steps = codes.shape[1]
    own_rows = rows // 2
    block = min(block, own_rows)
    blocks = own_rows // block
    bins = weights[15].shape[2]
    weights = weights[:15] + tuple(jnp.transpose(array, (2, 0, 1)) for array in weights[15:])
    codes, targets = jnp.swapaxes(codes, 0, 1), jnp.swapaxes(targets, 0, 1)
    table, w_in, gains, w_up, w_down, w_head = weights[0::3]
    lay = Layout(table.shape[1], width, bins)
    packed_shape = (lay.rows, width)
    roomy = pltpu.CompilerParams(vmem_limit_bytes=VMEM)
    mine = pl.pallas_call(
        functools.partial(pack_kernel, lay),
        out_shape=jax.ShapeDtypeStruct(packed_shape, BF16),
        compiler_params=roomy,
        name="pack",
    )(table, w_in, w_up, w_down, w_head, gains)
    theirs = swap(mine)

    def spec_rows(*shape):
        return pl.BlockSpec(shape, lambda i, which: (which[0] * blocks + i,) + (0,) * (len(shape) - 1))

    def spec_lanes(*shape):
        return pl.BlockSpec(shape, lambda i, which: (0,) * (len(shape) - 1) + (which[0] * blocks + i,))

    def spec_whole(*shape):
        return pl.BlockSpec(shape, lambda i, which: (0,) * len(shape))

    def spec_once(*shape):
        return pl.BlockSpec(shape, lambda i, which: (0,) * len(shape), pipeline_mode=pl.Buffered(1))

    def spec_out(*shape):
        return pl.BlockSpec(shape, lambda i, which: (i, 0))

    ticks = 2 * steps
    square = (2, width, width)
    per_tick = (ticks, block, width)
    narrow = (ticks, block, LANES)
    keep, send, ends_mine, ends_send = pl.pallas_call(
        functools.partial(towers_kernel, lay, steps, chunk),
        grid_spec=pltpu.PrefetchScalarGridSpec(
            num_scalar_prefetch=1,
            grid=(blocks,),
            in_specs=[
                spec_rows(block, width),
                spec_lanes(steps, 2, block),
                spec_lanes(steps, 2, block),
                spec_lanes(steps, block),
                spec_whole(steps, rows),
                spec_once(*packed_shape),
                spec_once(*packed_shape),
            ],
            out_specs=[
                spec_once(*packed_shape),
                spec_once(*packed_shape),
                spec_out(block, width),
                spec_out(block, width),
            ],
            scratch_shapes=[
                pltpu.VMEM((2, width + LANES, width), BF16),
                pltpu.VMEM(square, BF16),
                pltpu.VMEM(square, BF16),
                pltpu.VMEM((2, lay.wide, width), BF16),
                pltpu.VMEM((2, 2, width), F32),
                pltpu.VMEM((2, width + lay.codes, width), F32),
                pltpu.VMEM(square, F32),
                pltpu.VMEM(square, F32),
                pltpu.VMEM((2, width, lay.wide), F32),
                pltpu.VMEM((2, 8, width), F32),
                pltpu.VMEM((steps, block, 8), jnp.int32),
                pltpu.VMEM((ticks, block, LANES), BF16),
                pltpu.VMEM((2, block + 2 * TILE, width), BF16),
                pltpu.VMEM(per_tick, F32),
                pltpu.VMEM(per_tick, F32),
                pltpu.VMEM(per_tick, F32),
                pltpu.VMEM(per_tick, F32),
                pltpu.VMEM((block + 2 * TILE, width), BF16),
                pltpu.VMEM((block + 2 * TILE, width), BF16),
                pltpu.VMEM((ticks, width, block), BF16),
                pltpu.VMEM((ticks, width, block), BF16),
                pltpu.VMEM(narrow, F32),
                pltpu.VMEM(narrow, F32),
                pltpu.VMEM(per_tick, F32),
                pltpu.VMEM((ticks + 1, width, block), BF16),
                pltpu.VMEM((ticks, lay.codes, block), BF16),
                pltpu.VMEM((2, block + TILE, lay.wide), F32),
                pltpu.VMEM((2, block + 2 * TILE, lay.wide), BF16),
                pltpu.VMEM((2, block + 2 * TILE, width), BF16),
                pltpu.VMEM((block, width), BF16),
            ],
        ),
        out_shape=[
            jax.ShapeDtypeStruct(packed_shape, BF16),
            jax.ShapeDtypeStruct(packed_shape, BF16),
            jax.ShapeDtypeStruct((own_rows, width), F32),
            jax.ShapeDtypeStruct((own_rows, width), BF16),
        ],
        compiler_params=roomy,
        name="towers",
    )(section[None], latent, codes, targets, valid, valid, mine, theirs)

    parts = min(4, length)
    place = (index % parts)[None]
    in_smem = pl.BlockSpec(memory_space=pltpu.SMEM)

    part_shape = (lay.rows // parts, width)
    both = lax.optimization_barrier(keep.astype(F32)) + swap(send).astype(F32)
    both = lax.optimization_barrier(both.reshape(parts, *part_shape))

    def part_for(mask):
        return lax.dynamic_index_in_dim(both, place[0] ^ mask, 0, keepdims=False)

    own = lax.optimization_barrier(part_for(0))
    others = [part_for(mask).astype(BF16) for mask in range(1, parts)]
    current = own
    for arrived in [across(other, mask, length) for mask, other in enumerate(others, 1)]:
        current = current + arrived.astype(F32)
    current = current.astype(BF16)
    masks = [1 << bit for bit in range(length.bit_length() - 1)][parts.bit_length() - 1 :]
    halved = masks[:1] if len(masks) > 1 else []
    for mask in halved:
        half = current.shape[0] // 2
        upper = (index // mask) % 2 == 1
        sent = jnp.where(upper, current[:half], current[half:])
        kept = jnp.where(upper, current[half:], current[:half])
        current = (kept.astype(F32) + across(sent, mask, length).astype(F32)).astype(BF16)
    for mask in masks[len(halved) :]:
        current = (current.astype(F32) + across(current, mask, length).astype(F32)).astype(BF16)
    for mask in halved:
        upper = (index // mask) % 2 == 1
        found = across(current, mask, length)
        current = jnp.where(upper, jnp.concatenate([found, current]), jnp.concatenate([current, found]))
    pieces = [current] + [across(current, mask, length) for mask in range(1, parts)]

    other = swap(ends_send).astype(F32)
    ends = jnp.where(
        section == 0,
        jnp.concatenate([ends_mine, other]),
        jnp.concatenate([other, ends_mine]),
    )[None]
    news = []
    for at in range(6):
        shape = weights[3 * at].shape
        news += [jax.ShapeDtypeStruct(shape, F32)] * 3
        news.append(jax.ShapeDtypeStruct((1, shape[0], width) if at == 5 else shape, BF16))
    copy_count = 4 * (5 + -(-bins // (-(-bins // (STEPS * TILE)) * TILE)))
    updated = pl.pallas_call(
        functools.partial(update_kernel, lay, parts),
        in_specs=[in_smem] + [pl.BlockSpec(memory_space=pltpu.VMEM)] * (parts + 18),
        out_specs=[pl.BlockSpec(memory_space=pl.ANY)] * 24,
        out_shape=news,
        scratch_shapes=[pltpu.VMEM(new.shape, new.dtype) for new in news]
        + [pltpu.VMEM(packed_shape, BF16), pltpu.SemaphoreType.DMA((copy_count,))],
        compiler_params=pltpu.CompilerParams(vmem_limit_bytes=SMALL),
        name="update",
    )(place, *pieces, *weights)
    table_out, in_out, gain_out, up_out, down_out, head_out = (updated[4 * at : 4 * at + 4] for at in range(6))
    head_out = [jnp.transpose(array, (1, 2, 0)) for array in head_out[:3]] + [jnp.swapaxes(head_out[3], 1, 2)]
    return (ends, *table_out, *in_out, *gain_out, *up_out, *down_out, *head_out)


def solution(mesh):
    by_section = P("section", None, None)
    in_specs = (P("dp", None), P(None, None, "dp"), P(None, None, "dp"), P(None, "dp")) + (by_section,) * 18
    out_specs = (P("section", "dp", None),) + (by_section,) * 24
    return jax.shard_map(
        functools.partial(on_device, 512, 64, mesh.shape["dp"]),
        mesh=mesh,
        in_specs=in_specs,
        out_specs=out_specs,
        check_vma=False,
    )
```

```python
import functools
import math

import jax
import jax.numpy as jnp
from jax import lax
from jax.experimental import pallas as pl
from jax.experimental.pallas import tpu as pltpu
from jax.sharding import PartitionSpec as P

EPS = 1e-05
MOMENTUM = 0.5
AVERAGE = 0.9
RATE = 0.2
GRAD_SCALE = 4.0
GELU_LINE = 0.7978845608028654
GELU_CUBE = 0.7978845608028654 * 0.044715

BF16 = jnp.bfloat16
F32 = jnp.float32
LANES = 128
TILE = 16
BITS = 24
FIRST, SECOND, HOLD_AT, BACK_FIRST = 2, 2, 1, 0
CHUNK_ONE, CHUNK_TWO, CHUNK_HEAD, CHUNK_BACK, CHUNK_COPY = 128, 128, 128, 64, 128
LOGITS_FIRST = False
SPARE = 7
STEPS = 4
SMALL = 16 * 1024 * 1024
VMEM = 63 * 1024 * 1024


def dot(left, right):
    return jnp.dot(left, right, preferred_element_type=F32)


def dot_right_t(left, right):
    return lax.dot_general(left, right, (((1,), (1,)), ((), ())), preferred_element_type=F32)


def dot_left_t(left, right):
    return lax.dot_general(left, right, (((0,), (0,)), ((), ())), preferred_element_type=F32)


def gelu_and_slope(half):
    square = half * half
    bend = jnp.tanh(half * (2 * GELU_LINE + (8 * GELU_CUBE) * square))
    raised = 1.0 + bend
    result = half * raised
    return result, raised + result * (1.0 - bend) * (2 * GELU_LINE + (24 * GELU_CUBE) * square)


def normalise(value):
    width = value.shape[-1]
    centered = value - jnp.sum(value, axis=-1, keepdims=True) * (1.0 / width)
    scale = lax.rsqrt(jnp.sum(centered * centered, axis=-1, keepdims=True) + EPS * width)
    return centered * scale, scale


class Layout:
    def __init__(self, codes, width, bins):
        self.codes, self.width, self.bins = codes, width, bins
        self.wide = -(-bins // LANES) * LANES
        spots, at = {}, 0
        sizes = (("in", width), ("up", width), ("down", width), ("head", bins + SPARE), ("table", codes))
        for name, rows in sizes:
            spots[name] = (at, at + -(-rows // TILE) * TILE)
            at = spots[name][1]
        spots["table"] = (spots["table"][0], spots["table"][0] + codes)
        self.tail = spots["head"][0] + bins
        self.spots = spots
        self.used = at
        self.rows = -(-at // (8 * TILE)) * (8 * TILE)

    def with_tail(self, head, *extra):
        low, high = self.spots["head"]
        left = high - low - self.bins - sum(rows.shape[0] for rows in extra)
        return jnp.concatenate([head[: self.bins], *extra, jnp.zeros((left, self.width), F32)], axis=0)


def split_three(value):
    high = value.astype(BF16)
    left = value - high.astype(F32)
    middle = left.astype(BF16)
    low = (left - middle.astype(F32)).astype(BF16)
    return high, middle, low


def pack_kernel(lay, table, w_in, w_up, w_down, w_head, gains, out):
    for name, ref in (("in", w_in), ("up", w_up), ("down", w_down), ("table", table)):
        low, high = lay.spots[name]
        out[low:high, :] = ref[0].astype(BF16)
    low, high = lay.spots["head"]
    pieces = [piece.astype(F32) for piece in split_three(gains[0])]
    out[low:high, :] = lay.with_tail(w_head[:, 0, :], *pieces).astype(BF16)
    if lay.rows > lay.used:
        out[lay.used :, :] = jnp.zeros((lay.rows - lay.used, lay.width), BF16)


def row_sum(value):
    return jnp.sum(value, axis=-1, keepdims=True)


def interleave(streams, matmul_delay=220, vector_delay=60):
    clock = {"M": 0.0, "V": 0.0}
    live = []
    for rank, stream in enumerate(streams):
        live.append([stream, rank, next(stream), 0.0])
    while live:
        best = min(live, key=lambda entry: (max(clock[entry[2][0]], entry[3]), entry[1]))
        unit, cost = best[2]
        begin = max(clock[unit], best[3])
        clock[unit] = begin + cost
        best[3] = begin + cost + (matmul_delay if unit == "M" else vector_delay)
        best[2] = next(best[0], None)
        if best[2] is None:
            live.remove(best)


def in_turn(*streams):
    for stream in streams:
        yield from stream


def towers_kernel(lay, steps, chunk, which, latent, codes, targets, valid, whole_valid, mine, theirs,
                  keep, send, ends_mine, ends_send,
                  w_cat, w_up, w_down, w_head, gains,
                  g_cat, g_up, g_down, g_head, g_gain,
                  meta, picks, low_state, unit_one, slope_one, unit_two, slope_two, active_now, normed_now, active, normed,
                  scale_one, scale_two, head_part, turned, turned_pick, logits_all, logit_grads, pre_pair, back):
    branch_grads = (low_state.at[0], low_state.at[1])
    inner_grads = (active_now, normed_now)
    pre_grads = (pre_pair.at[0], pre_pair.at[1])
    rows, width = latent.shape
    wide = lay.wide
    part = 1.0 / width
    root = math.sqrt(width)
    section = which[0]
    def cut(size):
        return [slice(at, at + size) for at in range(0, rows, size)]

    chunks_one, chunks_two, chunks_head, chunks_back, chunks_copy = (
        cut(size) for size in (CHUNK_ONE, CHUNK_TWO, CHUNK_HEAD, CHUNK_BACK, CHUNK_COPY)
    )

    @pl.when(pl.program_id(0) == 0)
    def start():
        for ref in (g_cat, g_up, g_down, g_head, g_gain):
            ref[...] = jnp.zeros_like(ref)
        for packed, slot in ((mine, section), (theirs, 1 - section)):
            for name, ref in (("up", w_up), ("down", w_down)):
                low, high = lay.spots[name]
                ref[slot] = (packed[low:high, :].astype(F32) * (0.5 if name == "up" else 1.0)).astype(BF16)
            low, high = lay.spots["in"]
            w_cat[slot, :width] = packed[low:high, :]
            low, high = lay.spots["table"]
            w_cat[slot, width : width + lay.codes] = packed[low:high, :]
            w_cat[slot, width + lay.codes :] = jnp.zeros((LANES - lay.codes, width), BF16)
            low, high = lay.spots["head"]
            w_head[slot] = jnp.zeros((wide, width), BF16)
            w_head[slot, : high - low] = packed[low:high, :]
            start_tail = (lay.tail - low) // TILE * TILE
            block = packed[low + start_tail : high, :].astype(F32)
            at = lay.tail - low - start_tail
            pair = block[at : at + 2] + block[at + 2 : at + 4] + block[at + 4 : at + 6]
            gains[slot] = pair * jnp.where(lax.broadcasted_iota(jnp.int32, pair.shape, 0) == 0, root / 2, root)
            row = lax.broadcasted_iota(jnp.int32, block.shape, 0)
            w_head[slot, start_tail : high - low] = jnp.where(row < at, block, 0.0).astype(BF16)

    lane = lax.broadcasted_iota(jnp.int32, (rows, LANES), 1)
    upright = lax.broadcasted_iota(jnp.int32, (lay.codes, rows), 0)
    for step in range(steps):
        alive = valid[step : step + 1, :]
        line = [codes[step, tower : tower + 1, :] for tower in range(2)]
        line += [jnp.where(alive > 0, targets[step, tower : tower + 1, :], -1) for tower in range(2)]
        columns = jnp.concatenate(line + [jnp.zeros((4, rows), jnp.int32)], axis=0).T
        meta[step] = columns
        for tower in range(2):
            turned_pick[2 * step + tower] = (line[tower] == upright).astype(F32).astype(BF16)
            picks[2 * step + tower] = (columns[:, tower : tower + 1] == lane).astype(F32).astype(BF16)
    low_state[0, :rows] = latent[...]
    turned[0] = latent[...].T

    def forward(step, tower):
        at = 2 * step + tower
        yield "m1"
        pre = dot(picks[at], w_cat[tower, width:]) + dot(low_state[tower, :rows], w_cat[tower, :width])
        for where in chunks_one:
            yield "v1"
            unit, scale = normalise(pre[where])
            unit_one[at, where, :] = unit
            scale_one[at, where, :] = jnp.broadcast_to(scale, (CHUNK_ONE, LANES))
            hidden, slope = gelu_and_slope(unit * gains[tower, 0:1, :])
            slope_one[at, where, :] = slope
            head_part[at, where, :] = hidden
            unit, scale = normalise(hidden)
            unit_two[at, where, :] = unit
            scale_two[at, where, :] = jnp.broadcast_to(scale, (CHUNK_ONE, LANES))
            normed_now[where, :] = (unit * gains[tower, 1:2, :]).astype(BF16)
        yield "m2"
        inner = dot(normed_now[:rows, :], w_up[tower])
        normed[at] = normed_now[:rows, :].T
        for where in chunks_two:
            yield "v2"
            result, slope = gelu_and_slope(inner[where])
            slope_two[at, where, :] = slope
            active_now[where, :] = result.astype(BF16)
        yield "m3"
        branch = dot(active_now[:rows, :], w_down[tower])
        active[at] = active_now[:rows, :].T
        for where in chunks_two:
            yield "v3"
            state = head_part[at, where, :] + branch[where]
            low_state[1 - tower, where, :] = state.astype(BF16)
            ends_mine[where, :] = state
        yield "t"
        turned[at + 1] = low_state[1 - tower, :rows].T

    def hold_logits(tower, at, row):
        spot = pl.multiple_of(rows + 8 * section, 8)
        logits_all[tower, pl.ds(spot, 8), :LANES] = at[row : row + 8, :LANES].astype(F32)

    def hold_low(ref, slot, at, row):
        spot = pl.multiple_of(rows + TILE * section, TILE)
        ref[slot, pl.ds(spot, TILE), :LANES] = at[row : row + TILE, :LANES].astype(BF16)

    column = lax.broadcasted_iota(jnp.int32, (1, wide), 1)
    whole_lanes = wide - LANES
    inside = lax.broadcasted_iota(jnp.int32, (1, LANES), 1) < lay.bins - whole_lanes

    def head_logits(step, tower):
        yield "M", 5 * rows / 8
        logits = dot_right_t(low_state[1 - tower, :rows], w_head[tower])
        for where in chunks_copy:
            yield "V", 1
            logits_all[tower, where, :] = logits[where]

    def head_softmax(step, tower):
        for where in chunks_head:
            yield "V", 14 * 1
            some = logits_all[tower, where, :]
            some = jnp.concatenate(
                [some[:, :whole_lanes], jnp.where(inside, some[:, whole_lanes:], -1e30)], axis=1
            )
            goal = meta[step, where, 2 + tower : 3 + tower]
            raised = jnp.exp(some - jnp.max(some, axis=-1, keepdims=True))
            ratio = jnp.where(goal >= 0, 1.0, 0.0) / row_sum(raised)
            logit_grads[tower, where, :] = (raised * ratio - jnp.where(column == goal, 1.0, 0.0)).astype(BF16)

    def head_products(step, tower):
        at = 2 * step + tower
        yield "M", 5 * rows / 8
        pulled = dot(logit_grads[tower, :rows], w_head[tower])
        for where in chunks_copy:
            yield "V", 1
            head_part[at, where, :] = pulled[where]
        yield "M", 5 * rows / 8
        some = dot(turned[at + 1], logit_grads[tower, :rows])
        yield "V", 80
        g_head[tower] += some

    def tick(step, tower, stages="flsp"):
        at = 2 * step + tower
        count, later = len(chunks_one), len(chunks_two)
        streams = {}
        if "f" in stages:
            streams["f"] = forward(step, tower)
        if "s" in stages:
            streams["s"] = head_softmax(step - 1, tower)
        if "l" in stages:
            streams["l"] = head_logits(step - 1 + tower, 1 - tower)
        if "p" in stages:
            streams["p"] = head_products(step - 2 + tower, 1 - tower)
        for stream in streams.values():
            next(stream)

        def go(name, pieces=1):
            for _ in range(pieces):
                if name in streams:
                    next(streams[name], None)

        if "f" not in stages:
            for name in "spl":
                go(name, 100)
            return
        first, second = FIRST, SECOND
        go("f")
        go("s", first)
        go("f", HOLD_AT)
        if "p" in stages:
            hold_low(logit_grads, 1 - tower, unit_one.at[at], 0)
        if "l" in stages:
            hold_low(low_state, tower, unit_one.at[at], 0)
        if LOGITS_FIRST:
            go("l", 100)
        for turn in range(HOLD_AT, count):
            go("f")
            if turn % 2 == 1:
                go("p")
                go("l")
        go("p", 100)
        go("l", 100)
        if "s" in stages:
            hold_logits(tower, unit_two.at[at], rows - 8)
        go("f")
        go("s", second)
        go("f", later)
        if "s" in stages:
            hold_logits(tower, slope_two.at[at], rows - 8)
        go("f")
        go("s", 100)
        go("f", 100)

    def forward_step(step, carry):
        tick(step, 0)
        tick(step, 1)
        return carry

    tick(0, 0, "f")
    tick(0, 1, "fl")
    tick(1, 0, "fls")
    tick(1, 1)
    lax.fori_loop(2, steps, forward_step, 0)
    tick(steps, 0, "lsp")
    tick(steps, 1, "sp")
    tick(steps + 1, 0, "p")

    def both(value):
        return jnp.concatenate([value] * (width // LANES), axis=1)

    def backward(step, tower):
        at = 2 * step + tower
        for where in chunks_back:
            yield "V", 1
            state_grad = head_part[at, where, :] + back[where, :].astype(F32)
            head_part[at, where, :] = state_grad
            branch_grads[tower][where, :] = state_grad.astype(BF16)
        yield "M", rows / 4
        active_grad = dot_right_t(branch_grads[tower][:rows, :], w_down[tower])
        for where in chunks_back:
            yield "V", 1
            inner_grads[tower][where, :] = (active_grad[where] * slope_two[at, where, :]).astype(BF16)
        yield "M", rows / 4
        normed_grad = dot_right_t(inner_grads[tower][:rows, :], w_up[tower])
        for where in chunks_back:
            yield "V", 12.5 * 1
            unit = unit_two[at, where, :]
            scaled = normed_grad[where] * gains[tower, 1:2, :]
            first = row_sum(scaled) * part
            second = row_sum(scaled * unit)
            hidden_grad = head_part[at, where, :] + (scaled - first - unit * second) * both(scale_two[at, where, :])
            out_grad = hidden_grad * slope_one[at, where, :]
            unit = unit_one[at, where, :]
            product = out_grad * unit
            g_gain[tower] += jnp.sum(product.reshape(CHUNK_BACK // 8, 8, width), axis=0)
            gain = gains[tower, 0:1, :]
            scaled = out_grad * gain
            first = row_sum(scaled) * part
            second = row_sum(product * gain)
            pre_grads[tower][where, :] = (
                (scaled - first - unit * second) * both(scale_one[at, where, :])
            ).astype(BF16)
        yield "M", rows / 4
        input_grad = dot_right_t(pre_grads[tower][:rows, :], w_cat[tower, :width])
        for where in chunks_back:
            yield "V", 0.5 * 1
            back[where, :] = input_grad[where].astype(BF16)

    def weight_grads(step, tower):
        at = 2 * step + tower
        for left, right, total in ((active, branch_grads, g_down), (normed, inner_grads, g_up)):
            yield "M", rows / 4 + 20
            some = dot(left[at], right[tower][:rows, :])
            yield "V", 32
            total[tower] += some
        yield "M", rows / 4 + 40
        some = dot(jnp.concatenate([turned[at], turned_pick[at]], axis=0), pre_grads[tower][:rows, :])
        yield "V", 36
        g_cat[tower] += some

    back[...] = jnp.zeros_like(back)
    for ref in (branch_grads[0], inner_grads[0], pre_grads[0]):
        ref[:rows, :] = jnp.zeros((rows, width), BF16)

    def back_tick(step, tower, before):
        at = 2 * step + tower
        chain = backward(step, tower)
        next(chain)
        products = weight_grads(before, 1 - tower)
        next(products)
        for _ in range(2 * len(chunks_back) + 2 + BACK_FIRST):
            next(chain)
        spot = pl.multiple_of(rows + TILE * section, TILE)
        for ref in (branch_grads, inner_grads, pre_grads):
            ref[1 - tower][pl.ds(spot, TILE), :LANES] = unit_two[at, :TILE, :LANES].astype(BF16)
        for _ in products:
            next(chain, None)
        for _ in chain:
            pass

    def backward_step(turn, carry):
        step = steps - 1 - turn
        back_tick(step, 1, jnp.minimum(step + 1, steps - 1))
        back_tick(step, 0, step)
        return carry

    lax.fori_loop(0, steps, backward_step, 0)
    interleave([weight_grads(0, 0)])
    first = back[...].astype(F32)
    last = ends_mine[...]
    is_first = section == 0
    ends_mine[...] = jnp.where(is_first, first, last)
    ends_send[...] = jnp.where(is_first, last, first).astype(BF16)

    @pl.when(pl.program_id(0) == pl.num_programs(0) - 1)
    def finish():
        count = jnp.sum(whole_valid[...].astype(F32), axis=(0, 1), keepdims=True).astype(jnp.int32)
        spot = lax.broadcasted_iota(jnp.int32, (1, width), 1)
        bits = jnp.where(spot < BITS, (count >> jnp.minimum(spot, BITS)) & 1, 0).astype(F32)
        for packed, slot in ((keep, section), (send, 1 - section)):
            kind = packed.dtype
            for name, value in (
                ("in", g_cat[slot, :width]),
                ("up", g_up[slot] * 0.5),
                ("down", g_down[slot]),
                ("table", g_cat[slot, width : width + lay.codes]),
            ):
                low, high = lay.spots[name]
                packed[low:high, :] = value.astype(kind)
            in_gain = jnp.sum(g_gain[slot], axis=0, keepdims=True) * (root / 2)
            pulled = jnp.sum((w_up[slot].astype(F32) * g_up[slot]).T, axis=0, keepdims=True)
            block_gain = pulled * root / gains[slot, 1:2, :]
            own = bits if packed is keep else jnp.zeros_like(bits)
            low, high = lay.spots["head"]
            packed[low:high, :] = lay.with_tail(g_head[slot].T, in_gain, block_gain, own).astype(kind)
            if lay.rows > lay.used:
                packed[lay.used :, :] = jnp.zeros((lay.rows - lay.used, width), kind)


def update_kernel(lay, parts, which, *refs):
    pieces, ins, outs = refs[:parts], refs[parts : parts + 18], refs[parts + 18 : parts + 42]
    stages, total, done = refs[parts + 42 : parts + 66], refs[-2], refs[-1]
    rows = pieces[0].shape[0]
    for turn, piece in enumerate(pieces):
        low = pl.multiple_of((which[0] ^ turn) * rows, TILE)
        total[pl.ds(low, rows), :] = piece[...]
    low = lay.tail // TILE * TILE
    tail = total[low : lay.spots["head"][1], :].astype(F32)[lay.tail - low : lay.tail - low + 3]
    lane = lax.broadcasted_iota(jnp.int32, (1, lay.width), 1)
    place = jnp.where(lane < BITS, (1 << jnp.minimum(lane, BITS)).astype(F32), 0.0)
    count = jnp.sum(tail[2:3] * place, axis=-1, keepdims=True)
    scale = GRAD_SCALE * lax.rsqrt(count)
    copies = []

    def new(at, spot, copy_spot, parts_of, grad):
        weight, moment, average = ins[3 * at : 3 * at + 3]
        step_grad = grad.astype(F32) * scale
        new_moment = MOMENTUM * moment[spot] + step_grad
        new_weight = weight[spot] - RATE * (step_grad + MOMENTUM * new_moment)
        new_average = AVERAGE * average[spot] + (1.0 - AVERAGE) * new_weight
        news = (new_moment, new_average, new_weight, new_weight.astype(BF16))
        for kind, value in enumerate(news):
            stage, out = stages[4 * at + kind], outs[4 * at + kind]
            stage[copy_spot if kind == 3 else spot] = value
            piece = parts_of[1 if kind == 3 else 0]
            copies.append(pltpu.make_async_copy(stage.at[piece], out.at[piece], done.at[len(copies)]))
            copies[-1].start()

    everything = (slice(None),)
    low, high = lay.spots["head"]
    step = -(-lay.bins // (STEPS * TILE)) * TILE
    for begin in range(0, lay.bins, step):
        end = min(begin + step, lay.bins)
        cover = min(-(-end // TILE) * TILE, high - low)
        grad = total[low + begin : low + cover, :].astype(F32)[: end - begin]
        new(5, (slice(begin, end), 0), (0, slice(begin, end)),
            ((slice(begin, end),), (slice(None), slice(begin, end))), grad)
    for at, name in ((1, "in"), (3, "up"), (4, "down"), (0, "table")):
        low, high = lay.spots[name]
        new(at, (0,), (0,), (everything, everything), total[low:high, :])
    new(2, (0,), (0,), (everything, everything), tail[0:2])
    for copy in copies:
        copy.wait()


def swap(value):
    return lax.ppermute(value, "section", [(0, 1), (1, 0)])


def across(array, mask, length):
    return lax.ppermute(array, "dp", [(i, i ^ mask) for i in range(length)])


def on_device(block, chunk, length, latent, codes, targets, valid, *weights):
    section = lax.axis_index("section").astype(jnp.int32)
    index = lax.axis_index("dp").astype(jnp.int32)
    rows, width = latent.shape
    steps = codes.shape[1]
    own_rows = rows // 2
    block = min(block, own_rows)
    blocks = own_rows // block
    bins = weights[15].shape[2]
    weights = weights[:15] + tuple(jnp.transpose(array, (2, 0, 1)) for array in weights[15:])
    codes, targets = jnp.swapaxes(codes, 0, 1), jnp.swapaxes(targets, 0, 1)
    table, w_in, gains, w_up, w_down, w_head = weights[0::3]
    lay = Layout(table.shape[1], width, bins)
    packed_shape = (lay.rows, width)
    roomy = pltpu.CompilerParams(vmem_limit_bytes=VMEM)
    mine = pl.pallas_call(
        functools.partial(pack_kernel, lay),
        out_shape=jax.ShapeDtypeStruct(packed_shape, BF16),
        compiler_params=roomy,
        name="pack",
    )(table, w_in, w_up, w_down, w_head, gains)
    theirs = swap(mine)

    def spec_rows(*shape):
        return pl.BlockSpec(shape, lambda i, which: (which[0] * blocks + i,) + (0,) * (len(shape) - 1))

    def spec_lanes(*shape):
        return pl.BlockSpec(shape, lambda i, which: (0,) * (len(shape) - 1) + (which[0] * blocks + i,))

    def spec_whole(*shape):
        return pl.BlockSpec(shape, lambda i, which: (0,) * len(shape))

    def spec_once(*shape):
        return pl.BlockSpec(shape, lambda i, which: (0,) * len(shape), pipeline_mode=pl.Buffered(1))

    def spec_out(*shape):
        return pl.BlockSpec(shape, lambda i, which: (i, 0))

    ticks = 2 * steps
    square = (2, width, width)
    per_tick = (ticks, block, width)
    narrow = (ticks, block, LANES)
    keep, send, ends_mine, ends_send = pl.pallas_call(
        functools.partial(towers_kernel, lay, steps, chunk),
        grid_spec=pltpu.PrefetchScalarGridSpec(
            num_scalar_prefetch=1,
            grid=(blocks,),
            in_specs=[
                spec_rows(block, width),
                spec_lanes(steps, 2, block),
                spec_lanes(steps, 2, block),
                spec_lanes(steps, block),
                spec_whole(steps, rows),
                spec_once(*packed_shape),
                spec_once(*packed_shape),
            ],
            out_specs=[
                spec_once(*packed_shape),
                spec_once(*packed_shape),
                spec_out(block, width),
                spec_out(block, width),
            ],
            scratch_shapes=[
                pltpu.VMEM((2, width + LANES, width), BF16),
                pltpu.VMEM(square, BF16),
                pltpu.VMEM(square, BF16),
                pltpu.VMEM((2, lay.wide, width), BF16),
                pltpu.VMEM((2, 2, width), F32),
                pltpu.VMEM((2, width + lay.codes, width), F32),
                pltpu.VMEM(square, F32),
                pltpu.VMEM(square, F32),
                pltpu.VMEM((2, width, lay.wide), F32),
                pltpu.VMEM((2, 8, width), F32),
                pltpu.VMEM((steps, block, 8), jnp.int32),
                pltpu.VMEM((ticks, block, LANES), BF16),
                pltpu.VMEM((2, block + 2 * TILE, width), BF16),
                pltpu.VMEM(per_tick, F32),
                pltpu.VMEM(per_tick, F32),
                pltpu.VMEM(per_tick, F32),
                pltpu.VMEM(per_tick, F32),
                pltpu.VMEM((block + 2 * TILE, width), BF16),
                pltpu.VMEM((block + 2 * TILE, width), BF16),
                pltpu.VMEM((ticks, width, block), BF16),
                pltpu.VMEM((ticks, width, block), BF16),
                pltpu.VMEM(narrow, F32),
                pltpu.VMEM(narrow, F32),
                pltpu.VMEM(per_tick, F32),
                pltpu.VMEM((ticks + 1, width, block), BF16),
                pltpu.VMEM((ticks, lay.codes, block), BF16),
                pltpu.VMEM((2, block + TILE, lay.wide), F32),
                pltpu.VMEM((2, block + 2 * TILE, lay.wide), BF16),
                pltpu.VMEM((2, block + 2 * TILE, width), BF16),
                pltpu.VMEM((block, width), BF16),
            ],
        ),
        out_shape=[
            jax.ShapeDtypeStruct(packed_shape, BF16),
            jax.ShapeDtypeStruct(packed_shape, BF16),
            jax.ShapeDtypeStruct((own_rows, width), F32),
            jax.ShapeDtypeStruct((own_rows, width), BF16),
        ],
        compiler_params=roomy,
        name="towers",
    )(section[None], latent, codes, targets, valid, valid, mine, theirs)

    parts = min(4, length)
    place = (index % parts)[None]
    in_smem = pl.BlockSpec(memory_space=pltpu.SMEM)

    part_shape = (lay.rows // parts, width)
    both = lax.optimization_barrier(keep.astype(F32)) + swap(send).astype(F32)
    both = lax.optimization_barrier(both.reshape(parts, *part_shape))

    def part_for(mask):
        return lax.dynamic_index_in_dim(both, place[0] ^ mask, 0, keepdims=False)

    own = lax.optimization_barrier(part_for(0))
    others = [part_for(mask).astype(BF16) for mask in range(1, parts)]
    current = own
    for arrived in [across(other, mask, length) for mask, other in enumerate(others, 1)]:
        current = current + arrived.astype(F32)
    current = current.astype(BF16)
    masks = [1 << bit for bit in range(length.bit_length() - 1)][parts.bit_length() - 1 :]
    halved = masks[:1] if len(masks) > 1 else []
    for mask in halved:
        half = current.shape[0] // 2
        upper = (index // mask) % 2 == 1
        sent = jnp.where(upper, current[:half], current[half:])
        kept = jnp.where(upper, current[half:], current[:half])
        current = (kept.astype(F32) + across(sent, mask, length).astype(F32)).astype(BF16)
    for mask in masks[len(halved) :]:
        current = (current.astype(F32) + across(current, mask, length).astype(F32)).astype(BF16)
    for mask in halved:
        upper = (index // mask) % 2 == 1
        found = across(current, mask, length)
        current = jnp.where(upper, jnp.concatenate([found, current]), jnp.concatenate([current, found]))
    pieces = [current] + [across(current, mask, length) for mask in range(1, parts)]

    other = swap(ends_send).astype(F32)
    ends = jnp.where(
        section == 0,
        jnp.concatenate([ends_mine, other]),
        jnp.concatenate([other, ends_mine]),
    )[None]
    news = []
    for at in range(6):
        shape = weights[3 * at].shape
        news += [jax.ShapeDtypeStruct(shape, F32)] * 3
        news.append(jax.ShapeDtypeStruct((1, shape[0], width) if at == 5 else shape, BF16))
    copy_count = 4 * (5 + -(-bins // (-(-bins // (STEPS * TILE)) * TILE)))
    updated = pl.pallas_call(
        functools.partial(update_kernel, lay, parts),
        in_specs=[in_smem] + [pl.BlockSpec(memory_space=pltpu.VMEM)] * (parts + 18),
        out_specs=[pl.BlockSpec(memory_space=pl.ANY)] * 24,
        out_shape=news,
        scratch_shapes=[pltpu.VMEM(new.shape, new.dtype) for new in news]
        + [pltpu.VMEM(packed_shape, BF16), pltpu.SemaphoreType.DMA((copy_count,))],
        compiler_params=pltpu.CompilerParams(vmem_limit_bytes=SMALL),
        name="update",
    )(place, *pieces, *weights)
    table_out, in_out, gain_out, up_out, down_out, head_out = (updated[4 * at : 4 * at + 4] for at in range(6))
    head_out = [jnp.transpose(array, (1, 2, 0)) for array in head_out[:3]] + [jnp.swapaxes(head_out[3], 1, 2)]
    return (ends, *table_out, *in_out, *gain_out, *up_out, *down_out, *head_out)


def solution(mesh):
    by_section = P("section", None, None)
    in_specs = (P("dp", None), P(None, None, "dp"), P(None, None, "dp"), P(None, "dp")) + (by_section,) * 18
    out_specs = (P("section", "dp", None),) + (by_section,) * 24
    return jax.shard_map(
        functools.partial(on_device, 512, 64, mesh.shape["dp"]),
        mesh=mesh,
        in_specs=in_specs,
        out_specs=out_specs,
        check_vma=False,
    )
```

```python
import functools
import math

import jax
import jax.numpy as jnp
from jax import lax
from jax.experimental import pallas as pl
from jax.experimental.pallas import tpu as pltpu
from jax.sharding import PartitionSpec as P

EPS = 1e-05
MOMENTUM = 0.5
AVERAGE = 0.9
RATE = 0.2
GRAD_SCALE = 4.0
GELU_LINE = 0.7978845608028654
GELU_CUBE = 0.7978845608028654 * 0.044715

BF16 = jnp.bfloat16
F32 = jnp.float32
LANES = 128
TILE = 16
BITS = 24
FIRST, SECOND, HOLD_AT, BACK_FIRST = 2, 2, 1, 0
CHUNK_ONE, CHUNK_TWO, CHUNK_HEAD, CHUNK_BACK, CHUNK_COPY = 128, 128, 128, 64, 128
LOGITS_FIRST = False
SPARE = 7
STEPS = 4
SMALL = 16 * 1024 * 1024
VMEM = 63 * 1024 * 1024


def dot(left, right):
    return jnp.dot(left, right, preferred_element_type=F32)


def dot_right_t(left, right):
    return lax.dot_general(left, right, (((1,), (1,)), ((), ())), preferred_element_type=F32)


def dot_left_t(left, right):
    return lax.dot_general(left, right, (((0,), (0,)), ((), ())), preferred_element_type=F32)


def gelu_and_slope(half):
    square = half * half
    bend = jnp.tanh(half * (2 * GELU_LINE + (8 * GELU_CUBE) * square))
    raised = 1.0 + bend
    result = half * raised
    return result, raised + result * (1.0 - bend) * (2 * GELU_LINE + (24 * GELU_CUBE) * square)


def normalise(value):
    width = value.shape[-1]
    centered = value - jnp.sum(value, axis=-1, keepdims=True) * (1.0 / width)
    scale = lax.rsqrt(jnp.sum(centered * centered, axis=-1, keepdims=True) + EPS * width)
    return centered * scale, scale


class Layout:
    def __init__(self, codes, width, bins):
        self.codes, self.width, self.bins = codes, width, bins
        self.wide = -(-bins // LANES) * LANES
        spots, at = {}, 0
        sizes = (("in", width), ("up", width), ("down", width), ("head", bins + SPARE), ("table", codes))
        for name, rows in sizes:
            spots[name] = (at, at + -(-rows // TILE) * TILE)
            at = spots[name][1]
        spots["table"] = (spots["table"][0], spots["table"][0] + codes)
        self.tail = spots["head"][0] + bins
        self.spots = spots
        self.used = at
        self.rows = -(-at // (8 * TILE)) * (8 * TILE)

    def with_tail(self, head, *extra):
        low, high = self.spots["head"]
        left = high - low - self.bins - sum(rows.shape[0] for rows in extra)
        return jnp.concatenate([head[: self.bins], *extra, jnp.zeros((left, self.width), F32)], axis=0)


def split_three(value):
    high = value.astype(BF16)
    left = value - high.astype(F32)
    middle = left.astype(BF16)
    low = (left - middle.astype(F32)).astype(BF16)
    return high, middle, low


def pack_kernel(lay, table, w_in, w_up, w_down, w_head, gains, out):
    for name, ref in (("in", w_in), ("up", w_up), ("down", w_down), ("table", table)):
        low, high = lay.spots[name]
        out[low:high, :] = ref[0].astype(BF16)
    low, high = lay.spots["head"]
    pieces = [piece.astype(F32) for piece in split_three(gains[0])]
    out[low:high, :] = lay.with_tail(w_head[:, 0, :], *pieces).astype(BF16)
    if lay.rows > lay.used:
        out[lay.used :, :] = jnp.zeros((lay.rows - lay.used, lay.width), BF16)


def row_sum(value):
    return jnp.sum(value, axis=-1, keepdims=True)


def interleave(streams, matmul_delay=220, vector_delay=60):
    clock = {"M": 0.0, "V": 0.0}
    live = []
    for rank, stream in enumerate(streams):
        live.append([stream, rank, next(stream), 0.0])
    while live:
        best = min(live, key=lambda entry: (max(clock[entry[2][0]], entry[3]), entry[1]))
        unit, cost = best[2]
        begin = max(clock[unit], best[3])
        clock[unit] = begin + cost
        best[3] = begin + cost + (matmul_delay if unit == "M" else vector_delay)
        best[2] = next(best[0], None)
        if best[2] is None:
            live.remove(best)


def in_turn(*streams):
    for stream in streams:
        yield from stream


def towers_kernel(lay, steps, chunk, which, latent, codes, targets, valid, whole_valid, mine, theirs,
                  keep, send, ends_mine, ends_send,
                  w_cat, w_up, w_down, w_head, gains,
                  g_cat, g_up, g_down, g_head, g_gain,
                  meta, picks, low_state, unit_one, slope_one, unit_two, slope_two, active_now, normed_now, active, normed,
                  scale_one, scale_two, head_part, turned, turned_pick, logits_all, logit_grads, pre_pair, back):
    branch_grads = (low_state.at[0], low_state.at[1])
    inner_grads = (active_now, normed_now)
    pre_grads = (pre_pair.at[0], pre_pair.at[1])
    rows, width = latent.shape
    wide = lay.wide
    part = 1.0 / width
    root = math.sqrt(width)
    section = which[0]
    def cut(size):
        return [slice(at, at + size) for at in range(0, rows, size)]

    chunks_one, chunks_two, chunks_head, chunks_back, chunks_copy = (
        cut(size) for size in (CHUNK_ONE, CHUNK_TWO, CHUNK_HEAD, CHUNK_BACK, CHUNK_COPY)
    )

    @pl.when(pl.program_id(0) == 0)
    def start():
        for ref in (g_cat, g_up, g_down, g_head, g_gain):
            ref[...] = jnp.zeros_like(ref)
        for packed, slot in ((mine, section), (theirs, 1 - section)):
            for name, ref in (("up", w_up), ("down", w_down)):
                low, high = lay.spots[name]
                ref[slot] = (packed[low:high, :].astype(F32) * (0.5 if name == "up" else 1.0)).astype(BF16)
            low, high = lay.spots["in"]
            w_cat[slot, :width] = packed[low:high, :]
            low, high = lay.spots["table"]
            w_cat[slot, width : width + lay.codes] = packed[low:high, :]
            w_cat[slot, width + lay.codes :] = jnp.zeros((LANES - lay.codes, width), BF16)
            low, high = lay.spots["head"]
            w_head[slot] = jnp.zeros((wide, width), BF16)
            w_head[slot, : high - low] = packed[low:high, :]
            start_tail = (lay.tail - low) // TILE * TILE
            block = packed[low + start_tail : high, :].astype(F32)
            at = lay.tail - low - start_tail
            pair = block[at : at + 2] + block[at + 2 : at + 4] + block[at + 4 : at + 6]
            gains[slot] = pair * jnp.where(lax.broadcasted_iota(jnp.int32, pair.shape, 0) == 0, root / 2, root)
            row = lax.broadcasted_iota(jnp.int32, block.shape, 0)
            w_head[slot, start_tail : high - low] = jnp.where(row < at, block, 0.0).astype(BF16)

    lane = lax.broadcasted_iota(jnp.int32, (rows, LANES), 1)
    upright = lax.broadcasted_iota(jnp.int32, (lay.codes, rows), 0)
    for step in range(steps):
        alive = valid[step : step + 1, :]
        line = [codes[step, tower : tower + 1, :] for tower in range(2)]
        line += [jnp.where(alive > 0, targets[step, tower : tower + 1, :], -1) for tower in range(2)]
        columns = jnp.concatenate(line + [jnp.zeros((4, rows), jnp.int32)], axis=0).T
        meta[step] = columns
        for tower in range(2):
            turned_pick[2 * step + tower] = (line[tower] == upright).astype(F32).astype(BF16)
            picks[2 * step + tower] = (columns[:, tower : tower + 1] == lane).astype(F32).astype(BF16)
    low_state[0, :rows] = latent[...]
    turned[0] = latent[...].T

    def forward(step, tower):
        at = 2 * step + tower
        yield "m1"
        pre = dot(picks[at], w_cat[tower, width:]) + dot(low_state[tower, :rows], w_cat[tower, :width])
        for where in chunks_one:
            yield "v1"
            unit, scale = normalise(pre[where])
            unit_one[at, where, :] = unit
            scale_one[at, where, :] = jnp.broadcast_to(scale, (CHUNK_ONE, LANES))
            hidden, slope = gelu_and_slope(unit * gains[tower, 0:1, :])
            slope_one[at, where, :] = slope
            head_part[at, where, :] = hidden
            unit, scale = normalise(hidden)
            unit_two[at, where, :] = unit
            scale_two[at, where, :] = jnp.broadcast_to(scale, (CHUNK_ONE, LANES))
            normed_now[where, :] = (unit * gains[tower, 1:2, :]).astype(BF16)
        yield "m2"
        inner = dot(normed_now[:rows, :], w_up[tower])
        normed[at] = normed_now[:rows, :].T
        for where in chunks_two:
            yield "v2"
            result, slope = gelu_and_slope(inner[where])
            slope_two[at, where, :] = slope
            active_now[where, :] = result.astype(BF16)
        yield "m3"
        branch = dot(active_now[:rows, :], w_down[tower])
        active[at] = active_now[:rows, :].T
        for where in chunks_two:
            yield "v3"
            state = head_part[at, where, :] + branch[where]
            low_state[1 - tower, where, :] = state.astype(BF16)
            ends_mine[where, :] = state
        yield "t"
        turned[at + 1] = low_state[1 - tower, :rows].T

    def hold_logits(tower, at, row):
        spot = pl.multiple_of(rows + 8 * section, 8)
        logits_all[tower, pl.ds(spot, 8), :LANES] = at[row : row + 8, :LANES].astype(F32)

    def hold_low(ref, slot, at, row):
        spot = pl.multiple_of(rows + TILE * section, TILE)
        ref[slot, pl.ds(spot, TILE), :LANES] = at[row : row + TILE, :LANES].astype(BF16)

    column = lax.broadcasted_iota(jnp.int32, (1, wide), 1)
    whole_lanes = wide - LANES
    inside = lax.broadcasted_iota(jnp.int32, (1, LANES), 1) < lay.bins - whole_lanes

    def head_logits(step, tower):
        yield "M", 5 * rows / 8
        logits = dot_right_t(low_state[1 - tower, :rows], w_head[tower])
        for where in chunks_copy:
            yield "V", 1
            logits_all[tower, where, :] = logits[where]

    def head_softmax(step, tower):
        for where in chunks_head:
            yield "V", 14 * 1
            some = logits_all[tower, where, :]
            some = jnp.concatenate(
                [some[:, :whole_lanes], jnp.where(inside, some[:, whole_lanes:], -1e30)], axis=1
            )
            goal = meta[step, where, 2 + tower : 3 + tower]
            raised = jnp.exp(some - jnp.max(some, axis=-1, keepdims=True))
            ratio = jnp.where(goal >= 0, 1.0, 0.0) / row_sum(raised)
            logit_grads[tower, where, :] = (raised * ratio - jnp.where(column == goal, 1.0, 0.0)).astype(BF16)

    def head_products(step, tower):
        at = 2 * step + tower
        yield "M", 5 * rows / 8
        pulled = dot(logit_grads[tower, :rows], w_head[tower])
        for where in chunks_copy:
            yield "V", 1
            head_part[at, where, :] = pulled[where]
        yield "M", 5 * rows / 8
        some = dot(turned[at + 1], logit_grads[tower, :rows])
        yield "V", 80
        g_head[tower] += some

    def tick(step, tower, stages="flsp"):
        at = 2 * step + tower
        count, later = len(chunks_one), len(chunks_two)
        streams = {}
        if "f" in stages:
            streams["f"] = forward(step, tower)
        if "s" in stages:
            streams["s"] = head_softmax(step - 1, tower)
        if "l" in stages:
            streams["l"] = head_logits(step - 1 + tower, 1 - tower)
        if "p" in stages:
            streams["p"] = head_products(step - 2 + tower, 1 - tower)
        for stream in streams.values():
            next(stream)

        def go(name, pieces=1):
            for _ in range(pieces):
                if name in streams:
                    next(streams[name], None)

        if "f" not in stages:
            for name in "spl":
                go(name, 100)
            return
        first, second = FIRST, SECOND
        go("f")
        go("s", first)
        go("f", HOLD_AT)
        if "p" in stages:
            hold_low(logit_grads, 1 - tower, unit_one.at[at], 0)
        if "l" in stages:
            hold_low(low_state, tower, unit_one.at[at], 0)
        if LOGITS_FIRST:
            go("l", 100)
        for turn in range(HOLD_AT, count):
            go("f")
            if turn % 2 == 1:
                go("p")
                go("l")
        go("p", 100)
        go("l", 100)
        if "s" in stages:
            hold_logits(tower, unit_two.at[at], rows - 8)
        go("f")
        go("s", second)
        go("f", later)
        if "s" in stages:
            hold_logits(tower, slope_two.at[at], rows - 8)
        go("f")
        go("s", 100)
        go("f", 100)

    def forward_step(step, carry):
        tick(step, 0)
        tick(step, 1)
        return carry

    tick(0, 0, "f")
    tick(0, 1, "fl")
    tick(1, 0, "fls")
    tick(1, 1)
    lax.fori_loop(2, steps, forward_step, 0)
    tick(steps, 0, "lsp")
    tick(steps, 1, "sp")
    tick(steps + 1, 0, "p")

    def both(value):
        return jnp.concatenate([value] * (width // LANES), axis=1)

    def backward(step, tower):
        at = 2 * step + tower
        for where in chunks_back:
            yield "V", 1
            state_grad = head_part[at, where, :] + back[where, :].astype(F32)
            head_part[at, where, :] = state_grad
            branch_grads[tower][where, :] = state_grad.astype(BF16)
        yield "M", rows / 4
        active_grad = dot_right_t(branch_grads[tower][:rows, :], w_down[tower])
        for where in chunks_back:
            yield "V", 1
            inner_grads[tower][where, :] = (active_grad[where] * slope_two[at, where, :]).astype(BF16)
        yield "M", rows / 4
        normed_grad = dot_right_t(inner_grads[tower][:rows, :], w_up[tower])
        for where in chunks_back:
            yield "V", 12.5 * 1
            unit = unit_two[at, where, :]
            scaled = normed_grad[where] * gains[tower, 1:2, :]
            first = row_sum(scaled) * part
            second = row_sum(scaled * unit)
            hidden_grad = head_part[at, where, :] + (scaled - first - unit * second) * both(scale_two[at, where, :])
            out_grad = hidden_grad * slope_one[at, where, :]
            unit = unit_one[at, where, :]
            product = out_grad * unit
            g_gain[tower] += jnp.sum(product.reshape(CHUNK_BACK // 8, 8, width), axis=0)
            gain = gains[tower, 0:1, :]
            scaled = out_grad * gain
            first = row_sum(scaled) * part
            second = row_sum(product * gain)
            pre_grads[tower][where, :] = (
                (scaled - first - unit * second) * both(scale_one[at, where, :])
            ).astype(BF16)
        yield "M", rows / 4
        input_grad = dot_right_t(pre_grads[tower][:rows, :], w_cat[tower, :width])
        for where in chunks_back:
            yield "V", 0.5 * 1
            back[where, :] = input_grad[where].astype(BF16)

    def weight_grads(step, tower):
        at = 2 * step + tower
        for left, right, total in ((active, branch_grads, g_down), (normed, inner_grads, g_up)):
            yield "M", rows / 4 + 20
            some = dot(left[at], right[tower][:rows, :])
            yield "V", 32
            total[tower] += some
        yield "M", rows / 4 + 40
        some = dot(jnp.concatenate([turned[at], turned_pick[at]], axis=0), pre_grads[tower][:rows, :])
        yield "V", 36
        g_cat[tower] += some

    back[...] = jnp.zeros_like(back)
    for ref in (branch_grads[0], inner_grads[0], pre_grads[0]):
        ref[:rows, :] = jnp.zeros((rows, width), BF16)

    def back_tick(step, tower, before):
        at = 2 * step + tower
        chain = backward(step, tower)
        next(chain)
        products = weight_grads(before, 1 - tower)
        next(products)
        for _ in range(2 * len(chunks_back) + 2 + BACK_FIRST):
            next(chain)
        spot = pl.multiple_of(rows + TILE * section, TILE)
        for ref in (branch_grads, inner_grads, pre_grads):
            ref[1 - tower][pl.ds(spot, TILE), :LANES] = unit_two[at, :TILE, :LANES].astype(BF16)
        for _ in products:
            next(chain, None)
        for _ in chain:
            pass

    def backward_step(turn, carry):
        step = steps - 1 - turn
        back_tick(step, 1, jnp.minimum(step + 1, steps - 1))
        back_tick(step, 0, step)
        return carry

    lax.fori_loop(0, steps, backward_step, 0)
    interleave([weight_grads(0, 0)])
    first = back[...].astype(F32)
    last = ends_mine[...]
    is_first = section == 0
    ends_mine[...] = jnp.where(is_first, first, last)
    ends_send[...] = jnp.where(is_first, last, first).astype(BF16)

    @pl.when(pl.program_id(0) == pl.num_programs(0) - 1)
    def finish():
        count = jnp.sum(whole_valid[...].astype(F32), axis=(0, 1), keepdims=True).astype(jnp.int32)
        spot = lax.broadcasted_iota(jnp.int32, (1, width), 1)
        bits = jnp.where(spot < BITS, (count >> jnp.minimum(spot, BITS)) & 1, 0).astype(F32)
        for packed, slot in ((keep, section), (send, 1 - section)):
            kind = packed.dtype
            for name, value in (
                ("in", g_cat[slot, :width]),
                ("up", g_up[slot] * 0.5),
                ("down", g_down[slot]),
                ("table", g_cat[slot, width : width + lay.codes]),
            ):
                low, high = lay.spots[name]
                packed[low:high, :] = value.astype(kind)
            in_gain = jnp.sum(g_gain[slot], axis=0, keepdims=True) * (root / 2)
            pulled = jnp.sum((w_up[slot].astype(F32) * g_up[slot]).T, axis=0, keepdims=True)
            block_gain = pulled * root / gains[slot, 1:2, :]
            own = bits if packed is keep else jnp.zeros_like(bits)
            low, high = lay.spots["head"]
            packed[low:high, :] = lay.with_tail(g_head[slot].T, in_gain, block_gain, own).astype(kind)
            if lay.rows > lay.used:
                packed[lay.used :, :] = jnp.zeros((lay.rows - lay.used, width), kind)


def update_kernel(lay, parts, which, *refs):
    pieces, ins, outs = refs[:parts], refs[parts : parts + 18], refs[parts + 18 : parts + 42]
    stages, total, done = refs[parts + 42 : parts + 66], refs[-2], refs[-1]
    rows = pieces[0].shape[0]
    for turn, piece in enumerate(pieces):
        low = pl.multiple_of((which[0] ^ turn) * rows, TILE)
        total[pl.ds(low, rows), :] = piece[...]
    low = lay.tail // TILE * TILE
    tail = total[low : lay.spots["head"][1], :].astype(F32)[lay.tail - low : lay.tail - low + 3]
    lane = lax.broadcasted_iota(jnp.int32, (1, lay.width), 1)
    place = jnp.where(lane < BITS, (1 << jnp.minimum(lane, BITS)).astype(F32), 0.0)
    count = jnp.sum(tail[2:3] * place, axis=-1, keepdims=True)
    scale = GRAD_SCALE * lax.rsqrt(count)
    copies = []

    def new(at, spot, copy_spot, parts_of, grad):
        weight, moment, average = ins[3 * at : 3 * at + 3]
        step_grad = grad.astype(F32) * scale
        new_moment = MOMENTUM * moment[spot] + step_grad
        new_weight = weight[spot] - RATE * (step_grad + MOMENTUM * new_moment)
        new_average = AVERAGE * average[spot] + (1.0 - AVERAGE) * new_weight
        news = (new_moment, new_average, new_weight, new_weight.astype(BF16))
        for kind, value in enumerate(news):
            stage, out = stages[4 * at + kind], outs[4 * at + kind]
            stage[copy_spot if kind == 3 else spot] = value
            piece = parts_of[1 if kind == 3 else 0]
            copies.append(pltpu.make_async_copy(stage.at[piece], out.at[piece], done.at[len(copies)]))
            copies[-1].start()

    everything = (slice(None),)
    low, high = lay.spots["head"]
    step = -(-lay.bins // (STEPS * TILE)) * TILE
    for begin in range(0, lay.bins, step):
        end = min(begin + step, lay.bins)
        cover = min(-(-end // TILE) * TILE, high - low)
        grad = total[low + begin : low + cover, :].astype(F32)[: end - begin]
        new(5, (slice(begin, end), 0), (0, slice(begin, end)),
            ((slice(begin, end),), (slice(None), slice(begin, end))), grad)
    for at, name in ((1, "in"), (3, "up"), (4, "down"), (0, "table")):
        low, high = lay.spots[name]
        new(at, (0,), (0,), (everything, everything), total[low:high, :])
    new(2, (0,), (0,), (everything, everything), tail[0:2])
    for copy in copies:
        copy.wait()


def swap(value):
    return lax.ppermute(value, "section", [(0, 1), (1, 0)])


def across(array, mask, length):
    return lax.ppermute(array, "dp", [(i, i ^ mask) for i in range(length)])


def on_device(block, chunk, length, latent, codes, targets, valid, *weights):
    section = lax.axis_index("section").astype(jnp.int32)
    index = lax.axis_index("dp").astype(jnp.int32)
    rows, width = latent.shape
    steps = codes.shape[1]
    own_rows = rows // 2
    block = min(block, own_rows)
    blocks = own_rows // block
    bins = weights[15].shape[2]
    weights = weights[:15] + tuple(jnp.transpose(array, (2, 0, 1)) for array in weights[15:])
    codes, targets = jnp.swapaxes(codes, 0, 1), jnp.swapaxes(targets, 0, 1)
    table, w_in, gains, w_up, w_down, w_head = weights[0::3]
    lay = Layout(table.shape[1], width, bins)
    packed_shape = (lay.rows, width)
    roomy = pltpu.CompilerParams(vmem_limit_bytes=VMEM)
    mine = pl.pallas_call(
        functools.partial(pack_kernel, lay),
        out_shape=jax.ShapeDtypeStruct(packed_shape, BF16),
        compiler_params=roomy,
        name="pack",
    )(table, w_in, w_up, w_down, w_head, gains)
    theirs = swap(mine)

    def spec_rows(*shape):
        return pl.BlockSpec(shape, lambda i, which: (which[0] * blocks + i,) + (0,) * (len(shape) - 1))

    def spec_lanes(*shape):
        return pl.BlockSpec(shape, lambda i, which: (0,) * (len(shape) - 1) + (which[0] * blocks + i,))

    def spec_whole(*shape):
        return pl.BlockSpec(shape, lambda i, which: (0,) * len(shape))

    def spec_once(*shape):
        return pl.BlockSpec(shape, lambda i, which: (0,) * len(shape), pipeline_mode=pl.Buffered(1))

    def spec_out(*shape):
        return pl.BlockSpec(shape, lambda i, which: (i, 0))

    ticks = 2 * steps
    square = (2, width, width)
    per_tick = (ticks, block, width)
    narrow = (ticks, block, LANES)
    keep, send, ends_mine, ends_send = pl.pallas_call(
        functools.partial(towers_kernel, lay, steps, chunk),
        grid_spec=pltpu.PrefetchScalarGridSpec(
            num_scalar_prefetch=1,
            grid=(blocks,),
            in_specs=[
                spec_rows(block, width),
                spec_lanes(steps, 2, block),
                spec_lanes(steps, 2, block),
                spec_lanes(steps, block),
                spec_whole(steps, rows),
                spec_once(*packed_shape),
                spec_once(*packed_shape),
            ],
            out_specs=[
                spec_once(*packed_shape),
                spec_once(*packed_shape),
                spec_out(block, width),
                spec_out(block, width),
            ],
            scratch_shapes=[
                pltpu.VMEM((2, width + LANES, width), BF16),
                pltpu.VMEM(square, BF16),
                pltpu.VMEM(square, BF16),
                pltpu.VMEM((2, lay.wide, width), BF16),
                pltpu.VMEM((2, 2, width), F32),
                pltpu.VMEM((2, width + lay.codes, width), F32),
                pltpu.VMEM(square, F32),
                pltpu.VMEM(square, F32),
                pltpu.VMEM((2, width, lay.wide), F32),
                pltpu.VMEM((2, 8, width), F32),
                pltpu.VMEM((steps, block, 8), jnp.int32),
                pltpu.VMEM((ticks, block, LANES), BF16),
                pltpu.VMEM((2, block + 2 * TILE, width), BF16),
                pltpu.VMEM(per_tick, F32),
                pltpu.VMEM(per_tick, F32),
                pltpu.VMEM(per_tick, F32),
                pltpu.VMEM(per_tick, F32),
                pltpu.VMEM((block + 2 * TILE, width), BF16),
                pltpu.VMEM((block + 2 * TILE, width), BF16),
                pltpu.VMEM((ticks, width, block), BF16),
                pltpu.VMEM((ticks, width, block), BF16),
                pltpu.VMEM(narrow, F32),
                pltpu.VMEM(narrow, F32),
                pltpu.VMEM(per_tick, F32),
                pltpu.VMEM((ticks + 1, width, block), BF16),
                pltpu.VMEM((ticks, lay.codes, block), BF16),
                pltpu.VMEM((2, block + TILE, lay.wide), F32),
                pltpu.VMEM((2, block + 2 * TILE, lay.wide), BF16),
                pltpu.VMEM((2, block + 2 * TILE, width), BF16),
                pltpu.VMEM((block, width), BF16),
            ],
        ),
        out_shape=[
            jax.ShapeDtypeStruct(packed_shape, BF16),
            jax.ShapeDtypeStruct(packed_shape, BF16),
            jax.ShapeDtypeStruct((own_rows, width), F32),
            jax.ShapeDtypeStruct((own_rows, width), BF16),
        ],
        compiler_params=roomy,
        name="towers",
    )(section[None], latent, codes, targets, valid, valid, mine, theirs)

    parts = min(4, length)
    place = (index % parts)[None]
    in_smem = pl.BlockSpec(memory_space=pltpu.SMEM)

    part_shape = (lay.rows // parts, width)
    both = lax.optimization_barrier(keep.astype(F32)) + swap(send).astype(F32)
    both = lax.optimization_barrier(both.reshape(parts, *part_shape))

    def part_for(mask):
        return lax.dynamic_index_in_dim(both, place[0] ^ mask, 0, keepdims=False)

    own = lax.optimization_barrier(part_for(0))
    others = [part_for(mask).astype(BF16) for mask in range(1, parts)]
    current = own
    for arrived in [across(other, mask, length) for mask, other in enumerate(others, 1)]:
        current = current + arrived.astype(F32)
    current = current.astype(BF16)
    masks = [1 << bit for bit in range(length.bit_length() - 1)][parts.bit_length() - 1 :]
    for mask in masks:
        current = (current.astype(F32) + across(current, mask, length).astype(F32)).astype(BF16)
    pieces = [current] + [across(current, mask, length) for mask in range(1, parts)]

    other = swap(ends_send).astype(F32)
    ends = jnp.where(
        section == 0,
        jnp.concatenate([ends_mine, other]),
        jnp.concatenate([other, ends_mine]),
    )[None]
    news = []
    for at in range(6):
        shape = weights[3 * at].shape
        news += [jax.ShapeDtypeStruct(shape, F32)] * 3
        news.append(jax.ShapeDtypeStruct((1, shape[0], width) if at == 5 else shape, BF16))
    copy_count = 4 * (5 + -(-bins // (-(-bins // (STEPS * TILE)) * TILE)))
    updated = pl.pallas_call(
        functools.partial(update_kernel, lay, parts),
        in_specs=[in_smem] + [pl.BlockSpec(memory_space=pltpu.VMEM)] * (parts + 18),
        out_specs=[pl.BlockSpec(memory_space=pl.ANY)] * 24,
        out_shape=news,
        scratch_shapes=[pltpu.VMEM(new.shape, new.dtype) for new in news]
        + [pltpu.VMEM(packed_shape, BF16), pltpu.SemaphoreType.DMA((copy_count,))],
        compiler_params=pltpu.CompilerParams(vmem_limit_bytes=SMALL),
        name="update",
    )(place, *pieces, *weights)
    table_out, in_out, gain_out, up_out, down_out, head_out = (updated[4 * at : 4 * at + 4] for at in range(6))
    head_out = [jnp.transpose(array, (1, 2, 0)) for array in head_out[:3]] + [jnp.swapaxes(head_out[3], 1, 2)]
    return (ends, *table_out, *in_out, *gain_out, *up_out, *down_out, *head_out)


def solution(mesh):
    by_section = P("section", None, None)
    in_specs = (P("dp", None), P(None, None, "dp"), P(None, None, "dp"), P(None, "dp")) + (by_section,) * 18
    out_specs = (P("section", "dp", None),) + (by_section,) * 24
    return jax.shard_map(
        functools.partial(on_device, 512, 64, mesh.shape["dp"]),
        mesh=mesh,
        in_specs=in_specs,
        out_specs=out_specs,
        check_vma=False,
    )
```
